32 devices in a mesh: pair: 4 (over y, core), aux: 8 (over z, x).
Axes of the slice: x: 2, y: 2, z: 4, core: 2. Of those that a mesh axis runs over, the one named last changes fastest.
Arguments:
- three_index: float32 [8, 768, 8192], P('pair', None, 'aux'), may hold values from -0.6 to 0.6
- occupied_energy: float32 [8], P('pair'), may hold values from -2 to -0.5
- virtual_energy: float32 [768], replicated, may hold values from 0.2 to 3
- plan: int32 [2, 8], P(None, 'pair'), may hold values from 0 to 1, as said below
Outputs:
- gradient_blocks: float32 [8, 768, 8192], P('pair', None, 'aux')
- virtual_density: float32 [768, 768], P('aux', 'pair')
The draws below stay inside these ranges and needn't reach their ends.
Inputs may be any that keep to these rules, and one draw needn't show every extreme that they name: For block p and round r with q = p XOR 2**r: the row plan[r, p * 2 : (p + 1) * 2] is a permutation of the slots, and plan[r, q * 2 + plan[r, p * 2 + k]] = k, so every orbital is paired with exactly one orbital of block q in each round.
All inputs are finite; a program needn't handle non-finite values.
Results may differ from the reference program's by a relative error of at most 0.0001.
Values sent between devices are 32-bit elements; how exact they have to be, the bound alone decides.
No kernel may reach another device: no remote copies, remote signals or barrier semaphores. Data moves between devices by JAX's collectives and lax.ppermute only.
A program may use at most 128 MiB of HBM per device.

```python
import jax
import jax.numpy as jnp
from jax import lax

V = 768
NAUX = 8192
OB = 2
ROUNDS = 2
NOCC = 8


def draw_plan(key, part):
    blocks = NOCC // OB
    tables = []
    for turn_index in range(ROUNDS):
        keys = jax.random.split(jax.random.fold_in(key, 11 + turn_index), blocks)
        orders = jax.vmap(lambda single: jax.random.permutation(single, OB))(keys).astype(jnp.int32)
        indices = jnp.arange(blocks)
        upper_side = indices // 2 ** turn_index % 2
        lower_block = indices - upper_side * 2 ** turn_index
        base = orders[lower_block]
        inverse = jnp.argsort(base, axis=1).astype(jnp.int32)
        table = jnp.where(upper_side[:, None] == 1, inverse, base)
        tables.append(table.reshape(-1))
    return jnp.stack(tables).astype(jnp.int32)


def levels(key, shape, cuts, low, largest):
    level, own = 1.0, jax.random.fold_in(key, 6)
    for position, parts in cuts:
        steps = jnp.exp(jax.random.uniform(jax.random.fold_in(own, position), (parts,), jnp.float32, low / len(cuts), largest / len(cuts)))
        level = level * jnp.repeat(steps, shape[position] // parts).reshape([-1 if axis == position else 1 for axis in range(len(shape))])
    return level


def normal_values(rng, shape, spread, limit, pieces=(), held_as=jnp.bfloat16):
    result = spread * jax.random.normal(rng, shape, jnp.float32)
    if pieces:
        result = result * levels(rng, shape, pieces, -0.22, 0.18)
    return jnp.clip(result, -limit, limit).astype(held_as)


def setup_inputs(seed: int = 0) -> dict:
    seeds = jax.random.split(jax.random.key(seed), 5)
    return {
        "three_index": normal_values(seeds[0], (NOCC, V, NAUX), 0.1, 0.6, ((0, 4), (2, 8)), jnp.float32),
        "occupied_energy": jnp.clip(-2.0 + 1.5 * jax.random.uniform(seeds[1], (NOCC,), jnp.float32) ** levels(seeds[1], (NOCC,), ((0, 4),), -0.2, 0.2), -2.0, -0.5),
        "virtual_energy": jnp.clip(jax.random.uniform(seeds[2], (V,), jnp.float32, 0.2, 3.0), 0.2, 3.0),
        "plan": draw_plan(jax.random.fold_in(seeds[4], 71), 0),
    }


def reference(three_index, occupied_energy, virtual_energy, plan):
    highest = lax.Precision.HIGHEST
    blocks = NOCC // OB
    gradient = jnp.zeros(three_index.shape, jnp.float32)
    density = jnp.zeros((V, V), jnp.float32)
    for turn_index in range(ROUNDS):
        for block_index in range(blocks):
            if (block_index >> turn_index) & 1 == 0:
                partner_block = block_index ^ (1 << turn_index)
                for slot_index in range(OB):
                    own_orbital = block_index * OB + slot_index
                    peer_orbital = (partner_block * OB + plan[turn_index, own_orbital]).astype(jnp.int32)
                    left = three_index[own_orbital]
                    right = lax.dynamic_index_in_dim(three_index, peer_orbital, 0, keepdims=False)
                    peer_energy = lax.dynamic_index_in_dim(occupied_energy, peer_orbital, 0, keepdims=False)
                    integral = jnp.dot(left, right.T, precision=highest, preferred_element_type=jnp.float32)
                    denominator = occupied_energy[own_orbital] + peer_energy - virtual_energy[:, None] - virtual_energy[None, :]
                    amplitude = integral / denominator
                    tilde = 2.0 * amplitude - amplitude.T
                    gradient = gradient.at[own_orbital].add(jnp.dot(tilde, right, precision=highest, preferred_element_type=jnp.float32))
                    gradient = gradient.at[peer_orbital].add(jnp.dot(tilde.T, left, precision=highest, preferred_element_type=jnp.float32))
                    density = density + jnp.dot(amplitude, tilde.T, precision=highest, preferred_element_type=jnp.float32)
                    density = density + jnp.dot(amplitude.T, tilde, precision=highest, preferred_element_type=jnp.float32)
    return gradient, density
```

```python
import jax
import jax.numpy as jnp
from jax import lax
from jax.sharding import PartitionSpec as P


def swapped(block, axis, bit):
    count = lax.axis_size(axis)
    route = []
    for low in range(count):
        high = low | 1 << bit
        if high != low and high < count:
            route += [(low, high), (high, low)]
    return lax.ppermute(block, axis, route)


def side_of(axis, bit):
    return lax.axis_index(axis) // 2**bit % 2


def fold(block, bit, dim):
    side = side_of("aux", bit)
    half = block.shape[dim] // 2
    keep = lax.dynamic_slice_in_dim(block, side * half, half, dim)
    give = lax.dynamic_slice_in_dim(block, (1 - side) * half, half, dim)
    return keep + swapped(give, "aux", bit)


def unfold(block, bit, dim):
    side = side_of("aux", bit)
    other = swapped(block, "aux", bit)
    return jnp.where(
        side == 1,
        jnp.concatenate([other, block], axis=dim),
        jnp.concatenate([block, other], axis=dim),
    )


def owned(block, bits, dim):
    for bit in range(bits):
        half = block.shape[dim] // 2
        block = lax.dynamic_slice_in_dim(block, side_of("aux", bit) * half, half, dim)
    return block


def dot(expr, left, right):
    return jnp.einsum(
        expr, left, right, precision=lax.Precision.HIGH, preferred_element_type=jnp.float32
    )


def body(three_index, occupied_energy, virtual_energy, plan):
    per_block = three_index.shape[0]
    half_count = per_block // 2
    width = three_index.shape[1]
    aux_count = lax.axis_size("aux")
    bits = aux_count.bit_length() - 1
    row_count = width // aux_count
    row_start = lax.axis_index("aux") * row_count
    slots = jnp.arange(per_block, dtype=jnp.int32)
    rounds = plan.shape[0]
    sends = []
    for turn in range(rounds):
        table = plan[turn]
        upper_side = side_of("pair", turn) == 1
        inverse = jnp.sum(jnp.where(table[None, :] == slots[:, None], slots[None, :], 0), axis=1)
        own_slots = jnp.where(upper_side, inverse[half_count:], slots[:half_count])
        send_slots = jnp.where(upper_side, inverse[:half_count], slots[half_count:])
        own = jnp.take(three_index, own_slots, axis=0)
        give = jnp.take(three_index, send_slots, axis=0)
        own_energy = jnp.take(occupied_energy, own_slots)
        give_energy = jnp.take(occupied_energy, send_slots)
        sends.append((own_slots, send_slots, own, give, own_energy, give_energy))
    peers = [None] * rounds
    for turn in reversed(range(rounds)):
        own_slots, send_slots, own, give, own_energy, give_energy = sends[turn]
        first, energy = swapped((give, give_energy), "pair", turn)
        second = swapped(own, "pair", turn)
        peers[turn] = (first, own_energy + energy, second)
    gradient = jnp.zeros(three_index.shape, jnp.float32)
    density = jnp.zeros((row_count, width), jnp.float32)
    owned_energy = owned(virtual_energy, bits, 0)
    for turn in range(rounds):
        own_slots, send_slots, own, _, _, _ = sends[turn]
        first, pair_energy, second = peers[turn]
        part = dot("hap,hbp->hab", own, first)
        for bit in range(bits):
            part = fold(part, bit, 1)
        gap = pair_energy[:, None, None] - owned_energy[None, :, None] - virtual_energy[None, None, :]
        amp = part / gap
        amp_peer = swapped(amp, "pair", turn)
        for bit in reversed(range(bits)):
            amp = unfold(amp, bit, 1)
            amp_peer = unfold(amp_peer, bit, 1)
        tilde = 2.0 * amp - jnp.swapaxes(amp, 1, 2)
        tilde_peer = 2.0 * jnp.swapaxes(amp_peer, 1, 2) - amp_peer
        gradient = gradient.at[own_slots].add(dot("hab,hbp->hap", tilde, first))
        gradient = gradient.at[send_slots].add(dot("hab,hbp->hap", tilde_peer, second))
        rows = lax.dynamic_slice_in_dim(amp, row_start, row_count, 1)
        columns = lax.dynamic_slice_in_dim(amp, row_start, row_count, 2)
        density = density + dot("hac,hbc->ab", rows, tilde) + dot("hca,hcb->ab", columns, tilde)
    density = lax.psum_scatter(density, "pair", scatter_dimension=1, tiled=True)
    return (gradient, density)


def solution(mesh):
    in_specs = (P("pair", None, "aux"), P("pair"), P(), P(None, "pair"))
    out_specs = (P("pair", None, "aux"), P("aux", "pair"))
    return jax.shard_map(body, mesh=mesh, in_specs=in_specs, out_specs=out_specs, check_vma=False)
```

```python
import functools

import jax
import jax.numpy as jnp
from jax import lax
from jax.experimental import pallas as pl
from jax.experimental.pallas import tpu as pltpu
from jax.sharding import PartitionSpec as P


def swapped(block, axis, bit):
    count = lax.axis_size(axis)
    route = []
    for low in range(count):
        high = low | 1 << bit
        if high != low and high < count:
            route += [(low, high), (high, low)]
    return lax.ppermute(block, axis, route)


def after(value, *earlier):
    return lax.optimization_barrier((value, *earlier))[0]


def dot(expr, left, right):
    return jnp.einsum(
        expr, left, right, precision=lax.Precision.HIGH, preferred_element_type=jnp.float32
    )


def copy_kernel(plan_ref, side_ref, source_ref, target_ref):
    del plan_ref, side_ref
    target_ref[...] = source_ref[...]


def picked(three_index, plan, position, turn, own):
    per_block, width, depth = three_index.shape
    half_count = per_block // 2
    pieces = 4 if width % 32 == 0 else 1

    def source(h, piece, plan_ref, side_ref):
        upper = side_ref[0] // 2**turn % 2 == 1
        plain = h if own else half_count + h
        wanted = half_count + h if own else h
        inverse = 0
        for k in range(per_block):
            inverse += jnp.where(plan_ref[turn, k] == wanted, k, 0)
        return (jnp.where(upper, inverse, plain), piece, 0)

    return pl.pallas_call(
        copy_kernel,
        out_shape=jax.ShapeDtypeStruct((half_count, width, depth), jnp.float32),
        grid_spec=pltpu.PrefetchScalarGridSpec(
            num_scalar_prefetch=2,
            grid=(half_count, pieces),
            in_specs=[pl.BlockSpec((1, width // pieces, depth), source)],
            out_specs=pl.BlockSpec((1, width // pieces, depth), lambda h, piece, *_: (h, piece, 0)),
        ),
        compiler_params=pltpu.CompilerParams(vmem_limit_bytes=16 * 2**20),
        cost_estimate=pl.CostEstimate(
            flops=0, bytes_accessed=8 * half_count * width * depth, transcendentals=0
        ),
    )(plan, position, three_index)


def body(three_index, occupied_energy, virtual_energy, plan):
    per_block = three_index.shape[0]
    half_count = per_block // 2
    width = three_index.shape[1]
    aux_count = lax.axis_size("aux")
    row_count = width // aux_count
    row_start = lax.axis_index("aux") * row_count
    slots = jnp.arange(per_block, dtype=jnp.int32)
    rounds = plan.shape[0]
    position = lax.axis_index("pair").astype(jnp.int32)
    positions = position[None]
    gives = [None] * rounds
    firsts = [None] * rounds
    seconds = [None] * rounds
    for turn in range(1, rounds):
        gives[turn] = picked(three_index, plan, positions, turn, False)
        firsts[turn] = swapped(gives[turn], "pair", turn)
    other, = (swapped(three_index, "pair", 0),)
    owns = []
    energies = []
    where = []
    for turn in range(rounds):
        table = plan[turn]
        upper = position // 2**turn % 2 == 1
        inverse = jnp.sum(jnp.where(table[None, :] == slots[:, None], slots[None, :], 0), axis=1)
        own_slots = jnp.where(upper, inverse[half_count:], slots[:half_count])
        give_slots = jnp.where(upper, inverse[:half_count], slots[half_count:])
        where.append((own_slots, give_slots))
        peer_energy = swapped(occupied_energy[give_slots], "pair", turn)
        energies.append(occupied_energy[own_slots] + peer_energy)
        if turn == 0:
            owns.append(three_index[own_slots])
            firsts[0] = other[jnp.where(upper, slots[half_count:], table[:half_count])]
            seconds[0] = other[jnp.where(upper, slots[:half_count], table[half_count:])]
        else:
            owns.append(picked(three_index, plan, positions, turn, True))
            seconds[turn] = swapped(owns[turn], "pair", turn)
    rows_energy = lax.dynamic_slice_in_dim(virtual_energy, row_start, row_count, 0)
    gradient = jnp.zeros(three_index.shape, jnp.float32)
    density = jnp.zeros((row_count, width), jnp.float32)
    parts = []
    for turn in range(rounds):
        first = firsts[turn] if turn == 0 else after(firsts[turn], part)
        part = dot("hap,hbp->hab", owns[turn], first)
        parts.append(lax.psum_scatter(part, "aux", scatter_dimension=1, tiled=True))
    for turn in range(rounds):
        gap = energies[turn][:, None, None] - rows_energy[None, :, None] - virtual_energy[None, None, :]
        shard = parts[turn] / gap
        both = jnp.stack([shard, swapped(shard, "pair", turn)])
        amp, amp_peer = lax.all_gather(both, "aux", axis=2, tiled=True)
        tilde = 2.0 * amp - jnp.swapaxes(amp, 1, 2)
        tilde_peer = 2.0 * jnp.swapaxes(amp_peer, 1, 2) - amp_peer
        own_slots, give_slots = where[turn]
        gradient = gradient.at[own_slots].add(dot("hab,hbp->hap", tilde, firsts[turn]))
        gradient = gradient.at[give_slots].add(dot("hab,hbp->hap", tilde_peer, seconds[turn]))
        rows = lax.dynamic_slice_in_dim(amp, row_start, row_count, 1)
        columns = lax.dynamic_slice_in_dim(amp, row_start, row_count, 2)
        density = density + dot("hac,hbc->ab", rows, tilde) + dot("hca,hcb->ab", columns, tilde)
    density = lax.psum_scatter(density, "pair", scatter_dimension=1, tiled=True)
    return (gradient, density)


def solution(mesh):
    in_specs = (P("pair", None, "aux"), P("pair"), P(), P(None, "pair"))
    out_specs = (P("pair", None, "aux"), P("aux", "pair"))
    return jax.shard_map(body, mesh=mesh, in_specs=in_specs, out_specs=out_specs, check_vma=False)
```

```python
import functools

import jax
import jax.numpy as jnp
from jax import lax
from jax.experimental import pallas as pl
from jax.experimental.pallas import tpu as pltpu
from jax.sharding import PartitionSpec as P

VMEM = pl.BlockSpec(memory_space=pltpu.VMEM)
SMEM = pl.BlockSpec(memory_space=pltpu.SMEM)


def params(mebibytes):
    return pltpu.CompilerParams(vmem_limit_bytes=mebibytes * 2**20)


def cost(flops, read):
    return pl.CostEstimate(flops=int(flops), bytes_accessed=int(read), transcendentals=0)


def swapped(block, axis, bit):
    count = lax.axis_size(axis)
    route = []
    for low in range(count):
        high = low | 1 << bit
        if high != low and high < count:
            route += [(low, high), (high, low)]
    return lax.ppermute(block, axis, route)


def orders(bits):
    return (list(range(bits)), list(range(1, bits)) + [0])


def across(block, step):
    pairs, auxes = lax.axis_size("pair"), lax.axis_size("aux")
    order = orders(auxes.bit_length() - 1)
    route = []
    for p in range(pairs):
        for m in range(auxes):
            route.append((p * auxes + m, p * auxes + (m ^ 1 << order[p % 2][step])))
    return lax.ppermute(block, ("pair", "aux"), route)


def after(value, *earlier):
    return lax.optimization_barrier((value, *earlier))[0]


def dot(expr, left, right):
    return jnp.einsum(
        expr, left, right, precision=lax.Precision.HIGH, preferred_element_type=jnp.float32
    )


def halves(value):
    high = value.astype(jnp.bfloat16)
    return high, (value - high.astype(jnp.float32)).astype(jnp.bfloat16)


def multiply(left, right, dims):
    (lh, ll), (rh, rl) = left, right
    one = functools.partial(
        lax.dot_general, dimension_numbers=(dims, ((), ())), preferred_element_type=jnp.float32
    )
    return one(lh, rh) + (one(lh, rl) + one(ll, rh))


def slot_of(plan_ref, side_ref, per_block, turn, h, own):
    half_count = per_block // 2
    upper = side_ref[0] // 2**turn % 2 == 1
    plain = h if own else half_count + h
    wanted = half_count + h if own else h
    inverse = 0
    for k in range(per_block):
        inverse += jnp.where(plan_ref[turn, k] == wanted, k, 0)
    return jnp.where(upper, inverse, plain)


def copy_kernel(plan_ref, side_ref, source_ref, target_ref):
    del plan_ref, side_ref
    target_ref[...] = source_ref[...]


def picked(three_index, plan, state, turn, own, start, count):
    per_block, width, depth = three_index.shape
    half_count = per_block // 2
    rows = count // 2 if count % 16 == 0 and start % (count // 2) == 0 else count

    def source(h, piece, plan_ref, side_ref):
        return (slot_of(plan_ref, side_ref, per_block, turn, h, own), start // rows + piece, 0)

    return pl.pallas_call(
        copy_kernel,
        out_shape=jax.ShapeDtypeStruct((half_count, count, depth), jnp.float32),
        grid_spec=pltpu.PrefetchScalarGridSpec(
            num_scalar_prefetch=2,
            grid=(half_count, count // rows),
            in_specs=[pl.BlockSpec((1, rows, depth), source)],
            out_specs=pl.BlockSpec((1, rows, depth), lambda h, piece, *_: (h, piece, 0)),
        ),
        compiler_params=params(24),
        cost_estimate=cost(0, 8 * half_count * count * depth),
    )(plan, state, three_index)


def integral_kernel(turn, blocks, plan_ref, state_ref, own_ref, peer_ref, keep_ref, give_ref, high, low):
    del plan_ref
    band = pl.program_id(1)

    @pl.when(band == 0)
    def _():
        high[...], low[...] = halves(peer_ref[0])

    own = halves(own_ref[0])
    value = multiply(own, (high[...], low[...]), ((1,), (1,)))
    rows = keep_ref.shape[1] * 2 // blocks
    core = state_ref[0] % 2
    inside = own_ref.shape[1] // rows
    for part in range(inside):
        index = band * inside + part
        side, place = index // (blocks // 2), index % (blocks // 2)
        piece = value[part * rows : (part + 1) * rows]

        @pl.when(side == core)
        def _():
            keep_ref[0, pl.ds(pl.multiple_of((place ^ state_ref[1]) * rows, rows), rows), :] = piece

        @pl.when(side != core)
        def _():
            give_ref[0, pl.ds(pl.multiple_of((place ^ state_ref[2]) * rows, rows), rows), :] = piece


def integral(three_index, peer, plan, state, turn, blocks):
    per_block, width, depth = three_index.shape
    half_count, count, _ = peer.shape
    bands = 4 if blocks % 4 == 0 else 1
    out = jax.ShapeDtypeStruct((half_count, width // 2, count), jnp.float32)
    whole = pl.BlockSpec((1, width // 2, count), lambda h, band, *_: (h, 0, 0))
    return pl.pallas_call(
        functools.partial(integral_kernel, turn, blocks),
        out_shape=(out, out),
        grid_spec=pltpu.PrefetchScalarGridSpec(
            num_scalar_prefetch=2,
            grid=(half_count, bands),
            in_specs=[
                pl.BlockSpec(
                    (1, width // bands, depth),
                    lambda h, band, p, s: (slot_of(p, s, per_block, turn, h, True), band, 0),
                ),
                pl.BlockSpec((1, count, depth), lambda h, band, *_: (h, 0, 0)),
            ],
            out_specs=(whole, whole),
            scratch_shapes=[pltpu.VMEM((count, depth), jnp.bfloat16)] * 2,
        ),
        compiler_params=params(40),
        cost_estimate=cost(
            6 * half_count * width * count * depth,
            4 * half_count * (width * depth + count * depth + width * count),
        ),
    )(plan, state, three_index, peer)


def amplitude_kernel(turn, per_block, rows_at, info_ref, state_ref, column_ref, row_ref, left_ref, right_ref, out_ref):
    half_count = per_block // 2
    rows = out_ref.shape[2]
    start = pl.multiple_of(rows_at(state_ref) * rows, rows)
    down = column_ref[pl.ds(start, rows), :]
    for who in range(2):
        p = state_ref[0] ^ who
        q = p ^ 2**turn
        upper = p // 2**turn % 2 == 1
        for h in range(half_count):
            low = info_ref[p, h]
            high = info_ref[q, half_count + h]
            for k in range(per_block):
                slot = info_ref[p, per_block * (turn + 1) + k]
                high += jnp.where(slot == half_count + h, info_ref[p, k], 0.0)
            wanted = info_ref[p, per_block * (turn + 1) + h]
            for k in range(per_block):
                low += jnp.where(wanted == k, info_ref[q, k], 0.0)
            energy = jnp.where(upper, high, low)
            gap = energy - down - row_ref[...]
            out_ref[who, h] = (left_ref[who, h] + right_ref[who, h]) / gap


def amplitude(info, state, column, row, left, right, turn, per_block):
    def rows_at(state_ref):
        return state_ref[0] % 2 * lax.div(column.shape[0], 2 * left.shape[2]) + state_ref[1]

    return pl.pallas_call(
        functools.partial(amplitude_kernel, turn, per_block, rows_at),
        out_shape=jax.ShapeDtypeStruct(left.shape, jnp.float32),
        in_specs=[SMEM, SMEM, VMEM, VMEM, VMEM, VMEM],
        out_specs=VMEM,
        compiler_params=params(16),
        cost_estimate=cost(8 * left.size, 12 * left.size),
    )(info, state, column, row, left, right)


def tilde_kernel(blocks, count, flips, state_ref, *refs):
    mine, came, (amp_ref, tilde_ref) = refs[:count], refs[count : 2 * count], refs[2 * count :]
    width = amp_ref.shape[2]
    rows = width // blocks
    core = state_ref[0] % 2
    for h in range(amp_ref.shape[0]):
        offset = 0
        for part in range(count):
            size = mine[part].shape[2]
            for place in range(blocks // 2):
                spot = pl.ds(pl.multiple_of((core * (blocks // 2) + (place ^ state_ref[1])) * rows, rows), rows)
                amp_ref[h, spot, offset : offset + size] = mine[part][h, place * rows : (place + 1) * rows, :]
                spot = pl.ds(pl.multiple_of(((1 - core) * (blocks // 2) + (place ^ state_ref[2])) * rows, rows), rows)
                amp_ref[h, spot, offset : offset + size] = came[part][h, place * rows : (place + 1) * rows, :]
            offset += size
        band = 128 if width % 128 == 0 else width
        for part in range(width // band):
            spot = slice(part * band, (part + 1) * band)
            straight, turned = amp_ref[h, spot, :], amp_ref[h, :, spot].T
            tilde_ref[h, spot, :] = 2.0 * turned - straight if flips else 2.0 * straight - turned


def tilde_of(state, mine, came, blocks, flips):
    half_count, half, _ = mine[0].shape
    out = jax.ShapeDtypeStruct((half_count, 2 * half, 2 * half), jnp.float32)
    return pl.pallas_call(
        functools.partial(tilde_kernel, blocks, len(mine), flips),
        out_shape=(out, out),
        in_specs=[SMEM] + [VMEM] * (2 * len(mine)),
        out_specs=(VMEM, VMEM),
        compiler_params=params(32),
        cost_estimate=cost(8 * half * half, 48 * half * half),
    )(state, *mine, *came)


def body(three_index, occupied_energy, virtual_energy, plan):
    per_block, width, depth = three_index.shape
    half_count = per_block // 2
    aux_count = lax.axis_size("aux")
    bits = aux_count.bit_length() - 1
    blocks = 2 * aux_count
    row_count = width // aux_count
    aux = lax.axis_index("aux").astype(jnp.int32)
    row_start = aux * row_count
    slots = jnp.arange(per_block, dtype=jnp.int32)
    rounds = plan.shape[0]
    position = lax.axis_index("pair").astype(jnp.int32)

    def mask(order):
        return sum((aux >> bit & 1) << bits - 1 - step for step, bit in enumerate(order))

    first_mask, second_mask = (mask(order) for order in orders(bits))
    core = position % 2
    state = jnp.stack(
        [
            position,
            jnp.where(core == 0, first_mask, second_mask),
            jnp.where(core == 0, second_mask, first_mask),
        ]
    ).astype(jnp.int32)

    cuts = 2
    step = width // cuts
    firsts = [None] * rounds
    seconds = [None] * rounds
    for turn in range(1, rounds):
        firsts[turn] = [
            swapped(picked(three_index, plan, state, turn, False, cut * step, step), "pair", turn)
            for cut in range(cuts)
        ]
    other = swapped(three_index, "pair", 0)
    info = lax.all_gather(
        jnp.concatenate([occupied_energy, plan.astype(jnp.float32).reshape(-1)]), "pair", axis=0
    )
    where = []
    for turn in range(rounds):
        table = plan[turn]
        upper = position // 2**turn % 2 == 1
        inverse = jnp.sum(jnp.where(table[None, :] == slots[:, None], slots[None, :], 0), axis=1)
        own_slots = jnp.where(upper, inverse[half_count:], slots[:half_count])
        give_slots = jnp.where(upper, inverse[:half_count], slots[half_count:])
        where.append((own_slots, give_slots))
        if turn == 0:
            firsts[0] = [other[jnp.where(upper, slots[half_count:], table[:half_count])]]
            seconds[0] = other[jnp.where(upper, slots[:half_count], table[half_count:])]
        else:
            own = picked(three_index, plan, state, turn, True, 0, width)
            seconds[turn] = swapped(own, "pair", turn)

    column = virtual_energy[:, None]
    gradient = jnp.zeros(three_index.shape, jnp.float32)
    density = jnp.zeros((row_count, width), jnp.float32)
    begun = []
    for turn in range(rounds):
        offset = 0
        for first in firsts[turn]:
            if begun:
                first = after(first, begun[-1][4])
            keep, give = integral(three_index, first, plan, state, turn, blocks)
            size = first.shape[1]
            begun.append((turn, offset, size, keep, give))
            offset += size
    gathered = [([], []) for _ in range(rounds)]
    for turn, offset, size, keep, give in begun:
        value = jnp.stack([keep, swapped(give, "pair", 0)])
        for stage in range(bits):
            half = value.shape[2] // 2
            came = across(value[:, :, half:], stage)
            if stage < bits - 1:
                value = value[:, :, :half] + came
            else:
                value = amplitude(
                    info, state, column, virtual_energy[None, offset : offset + size],
                    value[:, :, :half], came, turn, per_block,
                )
        if turn > 0:
            value = jnp.concatenate([value, swapped(value, "pair", turn)], axis=1)
        for stage in reversed(range(bits)):
            value = jnp.concatenate([value, across(value, stage)], axis=2)
        mine, came = gathered[turn]
        if turn == 0:
            both = swapped(value, "pair", 0)
            mine.append((value[0], value[1]))
            came.append((both[1], both[0]))
        else:
            both = swapped(value[1], "pair", 0)
            mine.append((value[0, :half_count], value[0, half_count:]))
            came.append((both[:half_count], both[half_count:]))
    for turn in range(rounds):
        mine, came = gathered[turn]
        amp, tilde = tilde_of(state, [m[0] for m in mine], [c[0] for c in came], blocks, False)
        _, tilde_peer = tilde_of(state, [m[1] for m in mine], [c[1] for c in came], blocks, True)
        own_slots, give_slots = where[turn]
        first = jnp.concatenate(firsts[turn], axis=1)
        gradient = gradient.at[own_slots].add(dot("hab,hbp->hap", tilde, first))
        gradient = gradient.at[give_slots].add(dot("hab,hbp->hap", tilde_peer, seconds[turn]))
        rows = lax.dynamic_slice_in_dim(amp, row_start, row_count, 1)
        columns = lax.dynamic_slice_in_dim(amp, row_start, row_count, 2)
        density = density + dot("hac,hbc->ab", rows, tilde) + dot("hca,hcb->ab", columns, tilde)
    density = lax.psum_scatter(density, "pair", scatter_dimension=1, tiled=True)
    return (gradient, density)


def solution(mesh):
    in_specs = (P("pair", None, "aux"), P("pair"), P(), P(None, "pair"))
    out_specs = (P("pair", None, "aux"), P("aux", "pair"))
    return jax.shard_map(body, mesh=mesh, in_specs=in_specs, out_specs=out_specs, check_vma=False)
```

```python
import functools

import jax
import jax.numpy as jnp
from jax import lax
from jax.experimental import pallas as pl
from jax.experimental.pallas import tpu as pltpu
from jax.sharding import PartitionSpec as P

VMEM = pl.BlockSpec(memory_space=pltpu.VMEM)
SMEM = pl.BlockSpec(memory_space=pltpu.SMEM)
ANY = pl.BlockSpec(memory_space=pl.ANY)


def params(mebibytes):
    return pltpu.CompilerParams(vmem_limit_bytes=mebibytes * 2**20)


def cost(flops, read):
    return pl.CostEstimate(flops=int(flops), bytes_accessed=int(read), transcendentals=0)


def swapped(block, axis, bit):
    count = lax.axis_size(axis)
    route = []
    for low in range(count):
        high = low | 1 << bit
        if high != low and high < count:
            route += [(low, high), (high, low)]
    return lax.ppermute(block, axis, route)


def orders(bits):
    return (list(range(bits)), list(range(1, bits)) + [0])


def across(block, step):
    pairs, auxes = lax.axis_size("pair"), lax.axis_size("aux")
    order = orders(auxes.bit_length() - 1)
    route = []
    for p in range(pairs):
        for m in range(auxes):
            route.append((p * auxes + m, p * auxes + (m ^ 1 << order[p % 2][step])))
    return lax.ppermute(block, ("pair", "aux"), route)


def halves(value):
    high = value.astype(jnp.bfloat16)
    return high, (value - high.astype(jnp.float32)).astype(jnp.bfloat16)


def multiply(left, right, dims):
    (lh, ll), (rh, rl) = left, right
    one = functools.partial(
        lax.dot_general, dimension_numbers=(dims, ((), ())), preferred_element_type=jnp.float32
    )
    if dims[0] == (1,):
        count = lh.shape[0]
        both = one(jnp.concatenate([lh, ll], axis=0), rh)
        return both[:count] + (both[count:] + one(lh, rl))
    return one(lh, rh) + (one(lh, rl) + one(ll, rh))


def upper_in(position, turn):
    return position // 2**turn % 2 == 1


def slot_of(plan_ref, state_ref, per_block, turn, h, own):
    half_count = per_block // 2
    plain = jnp.where(own, h, half_count + h)
    wanted = jnp.where(own, half_count + h, h)
    inverse = 0
    for k in range(per_block):
        inverse += jnp.where(plan_ref[turn, k] == wanted, k, 0)
    return jnp.where(upper_in(state_ref[0], turn), inverse, plain)


def peer_slot_of(plan_ref, state_ref, per_block, turn, h, own):
    half_count = per_block // 2
    plain = jnp.where(own, h, half_count + h)
    wanted = jnp.where(own, half_count + h, h)
    paired = 0
    for k in range(per_block):
        paired += jnp.where(plain == k, plan_ref[turn, k], 0)
    return jnp.where(upper_in(state_ref[0], turn), wanted, paired)


def copy_kernel(plan_ref, state_ref, source_ref, token_ref, target_ref):
    del plan_ref, state_ref, token_ref
    target_ref[...] = source_ref[...]


def picked(three_index, plan, state, token, turn, own, start, count):
    per_block, width, depth = three_index.shape
    half_count = per_block // 2
    rows = count // 2 if count % 16 == 0 and start % (count // 2) == 0 else count

    def source(h, piece, plan_ref, state_ref):
        return (slot_of(plan_ref, state_ref, per_block, turn, h, own), start // rows + piece, 0)

    return pl.pallas_call(
        copy_kernel,
        out_shape=jax.ShapeDtypeStruct((half_count, count, depth), jnp.float32),
        grid_spec=pltpu.PrefetchScalarGridSpec(
            num_scalar_prefetch=2,
            grid=(half_count, count // rows),
            in_specs=[pl.BlockSpec((1, rows, depth), source), ANY],
            out_specs=pl.BlockSpec((1, rows, depth), lambda h, piece, *_: (h, piece, 0)),
        ),
        compiler_params=params(24),
        cost_estimate=cost(0, 8 * half_count * count * depth),
    )(plan, state, three_index, token)


def integral_kernel(turn, blocks, plan_ref, state_ref, own_ref, peer_ref, token_ref, keep_ref, give_ref, high, low):
    del plan_ref, token_ref
    band = pl.program_id(1)

    @pl.when(band == 0)
    def _():
        high[...], low[...] = halves(peer_ref[0])

    own = halves(own_ref[0])
    value = multiply(own, (high[...], low[...]), ((1,), (1,)))
    rows = keep_ref.shape[1] * 2 // blocks
    core = state_ref[0] % 2
    inside = own_ref.shape[1] // rows
    for part in range(inside):
        index = band * inside + part
        side, place = index // (blocks // 2), index % (blocks // 2)
        piece = value[part * rows : (part + 1) * rows]

        @pl.when(side == core)
        def _():
            keep_ref[0, pl.ds(pl.multiple_of((place ^ state_ref[1]) * rows, rows), rows), :] = piece

        @pl.when(side != core)
        def _():
            give_ref[0, pl.ds(pl.multiple_of((place ^ state_ref[2]) * rows, rows), rows), :] = piece


def integral(three_index, peer, plan, state, token, turn, blocks):
    per_block, width, depth = three_index.shape
    half_count, count = per_block // 2, peer.shape[1]
    bands = 2
    out = jax.ShapeDtypeStruct((half_count, width // 2, count), jnp.float32)
    whole = pl.BlockSpec((1, width // 2, count), lambda h, band, *_: (h, 0, 0))
    chosen = peer.shape[0] == per_block

    def peer_at(h, band, p, s):
        return (peer_slot_of(p, s, per_block, turn, h, True) if chosen else h, 0, 0)

    return pl.pallas_call(
        functools.partial(integral_kernel, turn, blocks),
        out_shape=(out, out),
        grid_spec=pltpu.PrefetchScalarGridSpec(
            num_scalar_prefetch=2,
            grid=(half_count, bands),
            in_specs=[
                pl.BlockSpec(
                    (1, width // bands, depth),
                    lambda h, band, p, s: (slot_of(p, s, per_block, turn, h, True), band, 0),
                ),
                pl.BlockSpec((1, count, depth), peer_at),
                ANY,
            ],
            out_specs=(whole, whole),
            scratch_shapes=[pltpu.VMEM((count, depth), jnp.bfloat16)] * 2,
        ),
        compiler_params=params(44),
        cost_estimate=cost(
            6 * half_count * width * count * depth,
            4 * half_count * (width * depth + count * depth + width * count),
        ),
    )(plan, state, three_index, peer, token)


def part_kernel(keep_ref, came_ref, token_ref, low_ref, high_ref):
    del token_ref
    half = low_ref.shape[2]
    low_ref[0], low_ref[1] = keep_ref[:, :half], came_ref[:, :half]
    high_ref[0], high_ref[1] = keep_ref[:, half:], came_ref[:, half:]


def add_kernel(keep_ref, came_ref, token_ref, low_ref, high_ref):
    del token_ref
    half = low_ref.shape[2]
    low_ref[...] = keep_ref[:, :, :half] + came_ref[:, :, :half]
    high_ref[...] = keep_ref[:, :, half:] + came_ref[:, :, half:]


def parted(keep, came, token):
    joined = len(keep.shape) == 3
    shape = ((2,) if joined else ()) + keep.shape
    out = jax.ShapeDtypeStruct(shape[:2] + (shape[2] // 2,) + shape[3:], jnp.float32)
    return pl.pallas_call(
        part_kernel if joined else add_kernel,
        out_shape=(out, out),
        in_specs=[VMEM, VMEM, ANY],
        out_specs=(VMEM, VMEM),
        compiler_params=params(16),
        cost_estimate=cost(keep.size, 12 * keep.size),
    )(keep, came, token)


def join_kernel(axis, one_ref, two_ref, token_ref, out_ref):
    del token_ref
    half = one_ref.shape[axis]
    if axis == 1:
        out_ref[:, :half], out_ref[:, half:] = one_ref[...], two_ref[...]
    else:
        out_ref[:, :, :half], out_ref[:, :, half:] = one_ref[...], two_ref[...]


def joined(one, two, token, axis):
    shape = list(one.shape)
    shape[axis] *= 2
    return pl.pallas_call(
        functools.partial(join_kernel, axis),
        out_shape=jax.ShapeDtypeStruct(tuple(shape), jnp.float32),
        in_specs=[VMEM, VMEM, ANY],
        out_specs=VMEM,
        compiler_params=params(24),
        cost_estimate=cost(0, 16 * one.size),
    )(one, two, token)


def amplitude_kernel(turn, per_block, ours_ref, theirs_ref, state_ref, column_ref, row_ref, left_ref, right_ref, token_ref, out_ref):
    del token_ref
    half_count = per_block // 2
    rows = out_ref.shape[2]
    place = state_ref[0] % 2 * lax.div(column_ref.shape[0], 2 * rows) + state_ref[1]
    down = column_ref[pl.ds(pl.multiple_of(place * rows, rows), rows), :]
    for who in range(2):
        upper = upper_in(state_ref[0] ^ who, turn)
        for h in range(half_count):
            low = ours_ref[who, h]
            high = theirs_ref[who, half_count + h]
            wanted = ours_ref[who, per_block * (turn + 1) + h]
            for k in range(per_block):
                slot = ours_ref[who, per_block * (turn + 1) + k]
                high += jnp.where(slot == half_count + h, ours_ref[who, k], 0.0)
                low += jnp.where(wanted == k, theirs_ref[who, k], 0.0)
            gap = jnp.where(upper, high, low) - down - row_ref[...]
            out_ref[who, h] = (left_ref[who, h] + right_ref[who, h]) / gap


def amplitude(ours, theirs, state, column, row, left, right, token, turn, per_block):
    return pl.pallas_call(
        functools.partial(amplitude_kernel, turn, per_block),
        out_shape=jax.ShapeDtypeStruct(left.shape, jnp.float32),
        in_specs=[SMEM, SMEM, SMEM, VMEM, VMEM, VMEM, VMEM, ANY],
        out_specs=VMEM,
        compiler_params=params(16),
        cost_estimate=cost(8 * left.size, 12 * left.size),
    )(ours, theirs, state, column, row, left, right, token)


def tilde_kernel(blocks, count, state_ref, token_ref, *refs):
    del token_ref
    sources, (high_ref, low_ref, density_ref, amp, tilde) = refs[: 4 * count], refs[4 * count :]
    width = amp.shape[0]
    rows = width // blocks
    core = state_ref[0] % 2
    share = density_ref.shape[0]
    band = 128 if width % 128 == 0 else width
    for h in range(high_ref.shape[1]):
        for who in range(2):
            offset = 0
            for part in range(count):
                mine, came = sources[who * 2 * count + part], sources[who * 2 * count + count + part]
                size = mine.shape[2]
                for place in range(blocks // 2):
                    here = slice(place * rows, (place + 1) * rows)
                    spot = (core * (blocks // 2) + (place ^ state_ref[1])) * rows
                    amp[pl.ds(pl.multiple_of(spot, rows), rows), offset : offset + size] = mine[h, here, :]
                    spot = ((1 - core) * (blocks // 2) + (place ^ state_ref[2])) * rows
                    amp[pl.ds(pl.multiple_of(spot, rows), rows), offset : offset + size] = came[h, here, :]
                offset += size
            for part in range(width // band):
                spot = slice(part * band, (part + 1) * band)
                straight, turned = amp[spot, :], amp[:, spot].T
                value = 2.0 * straight - turned if who == 0 else 2.0 * turned - straight
                if who == 0:
                    tilde[spot, :] = value
                high_ref[who, h, spot, :], low_ref[who, h, spot, :] = halves(value)
            if who == 0:
                start = pl.ds(pl.multiple_of(state_ref[3] * share, share), share)
                straight = amp[start, :]
                turned = 2.0 * straight - tilde[start, :]
                both = (high_ref[0, h], low_ref[0, h])
                value = multiply(halves(straight), both, ((1,), (1,)))
                value += multiply(halves(turned), both, ((1,), (0,)))
                if h == 0:
                    density_ref[...] = value
                else:
                    density_ref[...] += value


def tildes(state, token, own, peer, blocks, share):
    sources = [x for x, _ in own] + [y for _, y in own] + [x for x, _ in peer] + [y for _, y in peer]
    half_count, half, _ = sources[0].shape
    width = 2 * half
    out = jax.ShapeDtypeStruct((2, half_count, width, width), jnp.bfloat16)
    return pl.pallas_call(
        functools.partial(tilde_kernel, blocks, len(own)),
        out_shape=(out, out, jax.ShapeDtypeStruct((share, width), jnp.float32)),
        in_specs=[SMEM, ANY] + [VMEM] * len(sources),
        out_specs=(VMEM, VMEM, VMEM),
        scratch_shapes=[pltpu.VMEM((width, width), jnp.float32)] * 2,
        compiler_params=params(48),
        cost_estimate=cost(24 * width * width * share, 24 * width * width),
    )(state, token, *sources)


def gradient_kernel(count, based, plan_ref, state_ref, high_ref, low_ref, token_ref, *refs):
    del plan_ref, state_ref, token_ref
    out_ref = refs[-1]
    tall = high_ref.shape[2]
    value = refs[count][0] if based else None
    offset = 0
    for source in refs[:count]:
        size = source.shape[1]
        spot = slice(offset, offset + size)
        term = multiply((high_ref[0, 0, :, spot], low_ref[0, 0, :, spot]), halves(source[0]), ((1,), (0,)))
        value = term if value is None else value + term
        offset += size
    out_ref[0] = value


def gradient_terms(plan, state, token, high, low, sources, base, turn, per_block, terms):
    width, depth = high.shape[2], sources[0].shape[2]
    half_count = per_block // 2
    tile = depth // 4 if depth % 512 == 0 else depth
    chosen = sources[0].shape[0] == per_block

    def block_at(term, h, piece, p, s):
        return (slot_of(p, s, per_block, turn, h, terms[0] + term == 0), 0, piece)

    def source_at(term, h, piece, p, s):
        if not chosen:
            return (h, 0, piece)
        return (peer_slot_of(p, s, per_block, turn, h, terms[0] + term == 0), 0, piece)

    square = pl.BlockSpec((1, 1, width, width), lambda term, h, piece, *_: (terms[0] + term, h, 0, 0))
    out_spec = pl.BlockSpec((1, width, tile), block_at)
    return pl.pallas_call(
        functools.partial(gradient_kernel, len(sources), base is not None),
        out_shape=jax.ShapeDtypeStruct((per_block, width, depth), jnp.float32),
        grid_spec=pltpu.PrefetchScalarGridSpec(
            num_scalar_prefetch=2,
            grid=(len(terms), half_count, depth // tile),
            in_specs=[square, square, ANY]
            + [pl.BlockSpec((1, x.shape[1], tile), source_at) for x in sources]
            + ([out_spec] if base is not None else []),
            out_specs=out_spec,
        ),
        input_output_aliases={} if base is None else {5 + len(sources): 0},
        compiler_params=params(40),
        cost_estimate=cost(
            6 * len(terms) * half_count * width * width * depth,
            4 * len(terms) * half_count * (width * depth * 3 + width * width),
        ),
    )(plan, state, high, low, token, *sources, *(() if base is None else (base,)))


def chain(env, turn, offset, first):
    bits, per_block = env["bits"], env["per_block"]
    half_count = per_block // 2
    token = yield None
    keep, give = integral(env["three_index"], first, env["plan"], env["state"], token, turn, env["blocks"])
    came = swapped(give, "pair", 0)
    token = yield give
    for stage in range(bits):
        keep, give = parted(keep, came, token)
        came = across(give, stage)
        token = yield give
    row = env["virtual"][None, offset : offset + first.shape[1]]
    value = amplitude(
        env["info"], env["peer_info"][turn], env["state"], env["column"], row, keep, came, token, turn, per_block
    )
    if turn > 0:
        came = swapped(value, "pair", turn)
        token = yield value
        value = joined(value, came, token, 1)
    for stage in reversed(range(bits)):
        came = across(value, stage)
        token = yield value
        value = joined(value, came, token, 2)
    if turn == 0:
        came = swapped(value, "pair", 0)
        env["gathered"][turn].append(((value[0], came[1]), (value[1], came[0])))
    else:
        came = swapped(value[1], "pair", 0)
        env["gathered"][turn].append(
            ((value[0, :half_count], came[:half_count]), (value[0, half_count:], came[half_count:]))
        )
    yield value


def body(three_index, occupied_energy, virtual_energy, plan):
    per_block, width, depth = three_index.shape
    half_count = per_block // 2
    aux_count = lax.axis_size("aux")
    bits = aux_count.bit_length() - 1
    blocks = 2 * aux_count
    row_count = width // aux_count
    aux = lax.axis_index("aux").astype(jnp.int32)
    rounds = plan.shape[0]
    position = lax.axis_index("pair").astype(jnp.int32)

    def mask(order):
        return sum((aux >> bit & 1) << bits - 1 - step for step, bit in enumerate(order))

    first_mask, second_mask = (mask(order) for order in orders(bits))
    core = position % 2
    state = jnp.stack(
        [
            position,
            jnp.where(core == 0, first_mask, second_mask),
            jnp.where(core == 0, second_mask, first_mask),
            aux,
        ]
    ).astype(jnp.int32)

    cuts = 2
    step = width // cuts
    firsts = [None] * rounds
    token = virtual_energy
    for turn in range(1, rounds):
        firsts[turn] = []
        for cut in range(cuts):
            token = picked(three_index, plan, state, token, turn, False, cut * step, step)
            firsts[turn].append(swapped(token, "pair", turn))
    other = swapped(three_index, "pair", 0)
    firsts[0] = [other]
    mine = jnp.concatenate([occupied_energy, plan.astype(jnp.float32).reshape(-1)])
    core_info = swapped(mine, "pair", 0)
    info = jnp.stack([mine, core_info])
    env = {
        "bits": bits,
        "per_block": per_block,
        "blocks": blocks,
        "plan": plan,
        "state": state,
        "three_index": three_index,
        "virtual": virtual_energy,
        "column": virtual_energy[:, None],
        "info": info,
        "peer_info": [jnp.stack([core_info, mine])]
        + [swapped(info, "pair", turn) for turn in range(1, rounds)],
        "gathered": [[] for _ in range(rounds)],
    }

    tasks = []
    for turn in range(rounds):
        for cut, first in enumerate(firsts[turn]):
            worker = chain(env, turn, cut * step if turn else 0, first)
            next(worker)
            share = first.shape[1] / width
            clock = 18.0 if turn == 0 else 40.0 + 34.0 * cut + 70.0 * (turn - 1)
            times = [clock, clock + 3 + 9 * share + 3]
            wide = 12.8 * share
            for stage in range(bits):
                times.append(times[-1] + 4 + (wide if stage < 2 else wide / 2))
            if turn > 0:
                wide *= 2
                times.append(times[-1] + 6)
            for stage in range(bits):
                times.append(times[-1] + 4 + (wide if stage > 0 else wide / 2))
            tasks += [(time, turn, cut, worker) for time in times]
            if cut == len(firsts[turn]) - 1:
                tasks.append((times[-1] + 6, turn, cut, None))
    for turn in range(1, rounds):
        tasks.append((62.0 + 70.0 * (turn - 1), turn, -1, None))
    tasks.sort(key=lambda task: task[:3])
    seconds = [other] + [None] * (rounds - 1)
    gradient = None
    densities = []
    for _, turn, cut, worker in tasks:
        if worker is not None:
            token = worker.send(token)
        elif cut < 0:
            token = picked(three_index, plan, state, token, turn, True, 0, width)
            seconds[turn] = swapped(token, "pair", turn)
        else:
            own, peer = zip(*env["gathered"][turn])
            high, low, density = tildes(state, token, own, peer, blocks, row_count)
            densities.append(density)
            if turn == 0:
                gradient = gradient_terms(
                    plan, state, density, high, low, [other], None, turn, per_block, (0, 1)
                )
            else:
                gradient = gradient_terms(
                    plan, state, density, high, low, firsts[turn], gradient, turn, per_block, (0,)
                )
                gradient = gradient_terms(
                    plan, state, density, high, low, [seconds[turn]], gradient, turn, per_block, (1,)
                )
            token = density
    density = sum(densities)
    for bit in reversed(range(lax.axis_size("pair").bit_length() - 1)):
        half = density.shape[1] // 2
        side = position >> bit & 1
        give = lax.dynamic_slice_in_dim(density, (1 - side) * half, half, 1)
        density = lax.dynamic_slice_in_dim(density, side * half, half, 1) + swapped(give, "pair", bit)
    return (gradient, density)


def solution(mesh):
    in_specs = (P("pair", None, "aux"), P("pair"), P(), P(None, "pair"))
    out_specs = (P("pair", None, "aux"), P("aux", "pair"))
    return jax.shard_map(body, mesh=mesh, in_specs=in_specs, out_specs=out_specs, check_vma=False)
```

```python
import functools

import jax
import jax.numpy as jnp
from jax import lax
from jax.experimental import pallas as pl
from jax.experimental.pallas import tpu as pltpu
from jax.sharding import PartitionSpec as P

VMEM = pl.BlockSpec(memory_space=pltpu.VMEM)
SMEM = pl.BlockSpec(memory_space=pltpu.SMEM)
ANY = pl.BlockSpec(memory_space=pl.ANY)


def params(mebibytes):
    return pltpu.CompilerParams(vmem_limit_bytes=mebibytes * 2**20)


def cost():
    return pl.CostEstimate(flops=1, bytes_accessed=1, transcendentals=0)


def swapped(block, axis, bit):
    count = lax.axis_size(axis)
    route = []
    for low in range(count):
        high = low | 1 << bit
        if high != low and high < count:
            route += [(low, high), (high, low)]
    return lax.ppermute(block, axis, route)


def orders(bits):
    return (list(range(bits)), [1, 0] + list(range(2, bits)))


def across(block, step):
    pairs, auxes = lax.axis_size("pair"), lax.axis_size("aux")
    order = orders(auxes.bit_length() - 1)
    route = []
    for p in range(pairs):
        for m in range(auxes):
            route.append((p * auxes + m, p * auxes + (m ^ 1 << order[p % 2][step])))
    return lax.ppermute(block, ("pair", "aux"), route)


def halves(value):
    high = value.astype(jnp.bfloat16)
    return high, (value - high.astype(jnp.float32)).astype(jnp.bfloat16)


def multiply(left, right, dims):
    (lh, ll), (rh, rl) = left, right
    one = functools.partial(
        lax.dot_general, dimension_numbers=(dims, ((), ())), preferred_element_type=jnp.float32
    )
    if dims[0] == (1,):
        count = lh.shape[0]
        both = one(jnp.concatenate([lh, ll], axis=0), rh)
        return both[:count] + (both[count:] + one(lh, rl))
    return one(lh, rh) + (one(lh, rl) + one(ll, rh))


def upper_in(position, turn):
    return position // 2**turn % 2 == 1


def slot_of(plan_ref, state_ref, per_block, turn, h, own):
    half_count = per_block // 2
    plain = jnp.where(own, h, half_count + h)
    wanted = jnp.where(own, half_count + h, h)
    inverse = 0
    for k in range(per_block):
        inverse += jnp.where(plan_ref[turn, k] == wanted, k, 0)
    return jnp.where(upper_in(state_ref[0], turn), inverse, plain)


def peer_slot_of(plan_ref, state_ref, per_block, turn, h, own):
    half_count = per_block // 2
    plain = jnp.where(own, h, half_count + h)
    wanted = jnp.where(own, half_count + h, h)
    paired = 0
    for k in range(per_block):
        paired += jnp.where(plain == k, plan_ref[turn, k], 0)
    return jnp.where(upper_in(state_ref[0], turn), wanted, paired)


def copy_kernel(plan_ref, state_ref, source_ref, token_ref, target_ref):
    del plan_ref, state_ref, token_ref
    target_ref[...] = source_ref[...]


def picked(three_index, plan, state, token, turn, own, part, parts):
    per_block, width, depth = three_index.shape
    half_count = per_block // 2
    count = width if own else width // parts
    depth = depth // parts if own else depth
    rows = count // 2

    def source(h, piece, plan_ref, state_ref):
        slot = slot_of(plan_ref, state_ref, per_block, turn, h, own)
        return (slot, piece, part) if own else (slot, part * 2 + piece, 0)

    return pl.pallas_call(
        copy_kernel,
        out_shape=jax.ShapeDtypeStruct((half_count, count, depth), jnp.float32),
        grid_spec=pltpu.PrefetchScalarGridSpec(
            num_scalar_prefetch=2,
            grid=(half_count, count // rows),
            in_specs=[pl.BlockSpec((1, rows, depth), source), ANY],
            out_specs=pl.BlockSpec((1, rows, depth), lambda h, piece, *_: (h, piece, 0)),
        ),
        compiler_params=params(24),
        cost_estimate=cost(),
    )(plan, state, three_index, token)


def integral_kernel(turn, blocks, plan_ref, state_ref, own_ref, peer_ref, token_ref, keep_ref, give_ref, high, low):
    del plan_ref, token_ref
    band = pl.program_id(1)

    @pl.when(band == 0)
    def _():
        high[...], low[...] = halves(peer_ref[0])

    own = halves(own_ref[0])
    value = multiply(own, (high[...], low[...]), ((1,), (1,)))
    rows = keep_ref.shape[1] * 2 // blocks
    core = state_ref[0] % 2
    inside = own_ref.shape[1] // rows
    for part in range(inside):
        index = band * inside + part
        side, place = index // (blocks // 2), index % (blocks // 2)
        piece = value[part * rows : (part + 1) * rows]

        @pl.when(side == core)
        def _():
            keep_ref[0, pl.ds(pl.multiple_of((place ^ state_ref[1]) * rows, rows), rows), :] = piece

        @pl.when(side != core)
        def _():
            give_ref[0, pl.ds(pl.multiple_of((place ^ state_ref[2]) * rows, rows), rows), :] = piece


def integral(three_index, peer, plan, state, token, turn, blocks):
    per_block, width, depth = three_index.shape
    half_count, count = per_block // 2, peer.shape[1]
    bands = 2
    out = jax.ShapeDtypeStruct((half_count, width // 2, count), jnp.float32)
    whole = pl.BlockSpec((1, width // 2, count), lambda h, band, *_: (h, 0, 0))
    chosen = peer.shape[0] == per_block

    def peer_at(h, band, p, s):
        return (peer_slot_of(p, s, per_block, turn, h, True) if chosen else h, 0, 0)

    return pl.pallas_call(
        functools.partial(integral_kernel, turn, blocks),
        out_shape=(out, out),
        grid_spec=pltpu.PrefetchScalarGridSpec(
            num_scalar_prefetch=2,
            grid=(half_count, bands),
            in_specs=[
                pl.BlockSpec(
                    (1, width // bands, depth),
                    lambda h, band, p, s: (slot_of(p, s, per_block, turn, h, True), band, 0),
                ),
                pl.BlockSpec((1, count, depth), peer_at),
                ANY,
            ],
            out_specs=(whole, whole),
            scratch_shapes=[pltpu.VMEM((count, depth), jnp.bfloat16)] * 2,
        ),
        compiler_params=params(44),
        cost_estimate=cost(),
    )(plan, state, three_index, peer, token)


def part_kernel(keep_ref, came_ref, token_ref, low_ref, high_ref):
    del token_ref
    half = low_ref.shape[2]
    low_ref[0], low_ref[1] = keep_ref[:, :half], came_ref[:, :half]
    high_ref[0], high_ref[1] = keep_ref[:, half:], came_ref[:, half:]


def add_kernel(keep_ref, came_ref, token_ref, low_ref, high_ref):
    del token_ref
    half = low_ref.shape[2]
    low_ref[...] = keep_ref[:, :, :half] + came_ref[:, :, :half]
    high_ref[...] = keep_ref[:, :, half:] + came_ref[:, :, half:]


def parted(keep, came, token):
    joined = len(keep.shape) == 3
    shape = ((2,) if joined else ()) + keep.shape
    out = jax.ShapeDtypeStruct(shape[:2] + (shape[2] // 2,) + shape[3:], jnp.float32)
    return pl.pallas_call(
        part_kernel if joined else add_kernel,
        out_shape=(out, out),
        in_specs=[VMEM, VMEM, ANY],
        out_specs=(VMEM, VMEM),
        compiler_params=params(16),
        cost_estimate=cost(),
    )(keep, came, token)


def last_kernel(one_ref, two_ref, token_ref, keep_ref, give_ref):
    del token_ref
    half = one_ref.shape[2]
    keep_ref[:, :half], keep_ref[:, half:] = one_ref[0], two_ref[0]
    give_ref[:, :half], give_ref[:, half:] = one_ref[1], two_ref[1]


def last_joined(one, two, token):
    out = jax.ShapeDtypeStruct((one.shape[1], 2 * one.shape[2], one.shape[3]), jnp.float32)
    return pl.pallas_call(
        last_kernel,
        out_shape=(out, out),
        in_specs=[VMEM, VMEM, ANY],
        out_specs=(VMEM, VMEM),
        compiler_params=params(24),
        cost_estimate=cost(),
    )(one, two, token)


def join_kernel(axis, one_ref, two_ref, token_ref, out_ref):
    del token_ref
    half = one_ref.shape[axis]
    if axis == 1:
        out_ref[:, :half], out_ref[:, half:] = one_ref[...], two_ref[...]
    else:
        out_ref[:, :, :half], out_ref[:, :, half:] = one_ref[...], two_ref[...]


def joined(one, two, token, axis):
    shape = list(one.shape)
    shape[axis] *= 2
    return pl.pallas_call(
        functools.partial(join_kernel, axis),
        out_shape=jax.ShapeDtypeStruct(tuple(shape), jnp.float32),
        in_specs=[VMEM, VMEM, ANY],
        out_specs=VMEM,
        compiler_params=params(24),
        cost_estimate=cost(),
    )(one, two, token)


def amplitude_kernel(turn, per_block, ours_ref, theirs_ref, state_ref, column_ref, row_ref, left_ref, right_ref, token_ref, out_ref):
    del token_ref
    half_count = per_block // 2
    rows = out_ref.shape[2]
    place = state_ref[0] % 2 * lax.div(column_ref.shape[0], 2 * rows) + state_ref[1]
    down = column_ref[pl.ds(pl.multiple_of(place * rows, rows), rows), :]
    for who in range(2):
        upper = upper_in(state_ref[0] ^ who, turn)
        for h in range(half_count):
            low = ours_ref[who, h]
            high = theirs_ref[who, half_count + h]
            wanted = ours_ref[who, per_block * (turn + 1) + h]
            for k in range(per_block):
                slot = ours_ref[who, per_block * (turn + 1) + k]
                high += jnp.where(slot == half_count + h, ours_ref[who, k], 0.0)
                low += jnp.where(wanted == k, theirs_ref[who, k], 0.0)
            gap = jnp.where(upper, high, low) - down - row_ref[...]
            out_ref[who, h] = (left_ref[who, h] + right_ref[who, h]) / gap


def amplitude(ours, theirs, state, column, row, left, right, token, turn, per_block):
    return pl.pallas_call(
        functools.partial(amplitude_kernel, turn, per_block),
        out_shape=jax.ShapeDtypeStruct(left.shape, jnp.float32),
        in_specs=[SMEM, SMEM, SMEM, VMEM, VMEM, VMEM, VMEM, ANY],
        out_specs=VMEM,
        compiler_params=params(16),
        cost_estimate=cost(),
    )(ours, theirs, state, column, row, left, right, token)


def tilde_kernel(blocks, places, state_ref, token_ref, *refs):
    del token_ref
    count = len(places)
    sources, (high_ref, low_ref, density_ref, amp, tilde) = refs[: 2 * count], refs[2 * count :]
    width = amp.shape[0]
    rows = width // blocks
    core = state_ref[0] % 2
    share = density_ref.shape[0]
    band = 128 if width % 128 == 0 else width
    for h in range(high_ref.shape[1]):
        for who in range(2):
            offset = 0
            for part in range(count):
                mine, came = sources[2 * part], sources[2 * part + 1]
                first, second = (start + h for start in places[part][who])
                size = mine.shape[2]
                for place in range(blocks // 2):
                    here = slice(place * rows, (place + 1) * rows)
                    spot = (core * (blocks // 2) + (place ^ state_ref[1])) * rows
                    amp[pl.ds(pl.multiple_of(spot, rows), rows), offset : offset + size] = mine[first, here, :]
                    spot = ((1 - core) * (blocks // 2) + (place ^ state_ref[2])) * rows
                    amp[pl.ds(pl.multiple_of(spot, rows), rows), offset : offset + size] = came[second, here, :]
                offset += size
            for part in range(width // band):
                spot = slice(part * band, (part + 1) * band)
                straight, turned = amp[spot, :], amp[:, spot].T
                value = 2.0 * straight - turned if who == 0 else 2.0 * turned - straight
                if who == 0:
                    tilde[spot, :] = value
                high_ref[who, h, spot, :], low_ref[who, h, spot, :] = halves(value)
            if who == 0:
                start = pl.ds(pl.multiple_of(state_ref[3] * share, share), share)
                straight = amp[start, :]
                turned = 2.0 * straight - tilde[start, :]
                both = (high_ref[0, h], low_ref[0, h])
                value = multiply(halves(straight), both, ((1,), (1,)))
                value += multiply(halves(turned), both, ((1,), (0,)))
                if h == 0:
                    density_ref[...] = value
                else:
                    density_ref[...] += value


def tildes(state, token, gathered, blocks, share, half_count):
    sources = [array for mine, came, _, _ in gathered for array in (mine, came)]
    places = [spots for _, _, *spots in gathered]
    width = 2 * sources[0].shape[1]
    out = jax.ShapeDtypeStruct((2, half_count, width, width), jnp.bfloat16)
    return pl.pallas_call(
        functools.partial(tilde_kernel, blocks, places),
        out_shape=(out, out, jax.ShapeDtypeStruct((share, width), jnp.float32)),
        in_specs=[SMEM, ANY] + [VMEM] * len(sources),
        out_specs=(VMEM, VMEM, VMEM),
        scratch_shapes=[pltpu.VMEM((width, width), jnp.float32)] * 2,
        compiler_params=params(48),
        cost_estimate=cost(),
    )(state, token, *sources)


def gradient_kernel(count, based, columns, plan_ref, state_ref, high_ref, low_ref, token_ref, *refs):
    del plan_ref, state_ref, token_ref
    out_ref = refs[-1]

    def term(spot, source):
        tilde = (high_ref[0, 0, :, spot], low_ref[0, 0, :, spot])
        return multiply(tilde, halves(source[0]), ((1,), (0,)))

    if columns:
        for piece, source in enumerate(refs[:count]):

            @pl.when(pl.program_id(2) == piece)
            def _():
                out_ref[0] = refs[count][0] + term(slice(None), source)

        return
    value = refs[count][0] if based else None
    offset = 0
    for source in refs[:count]:
        added = term(slice(offset, offset + source.shape[1]), source)
        value = added if value is None else value + added
        offset += source.shape[1]
    out_ref[0] = value


def gradient_terms(plan, state, token, high, low, sources, base, turn, own, three_index):
    per_block, width, depth = three_index.shape
    half_count = per_block // 2
    columns = sources[0].shape[2] < depth
    tile = sources[0].shape[2] if columns else depth // 4 if depth % 512 == 0 else depth
    chosen = sources[0].shape[0] == per_block
    at = 0 if own else 1

    def block_at(h, _, piece, p, s):
        return (slot_of(p, s, per_block, turn, h, own), 0, piece)

    def source_at(h, _, piece, p, s):
        slot = peer_slot_of(p, s, per_block, turn, h, own) if chosen else h
        return (slot, 0, 0 if columns else piece)

    square = pl.BlockSpec((1, 1, width, width), lambda h, *_: (at, h, 0, 0))
    out_spec = pl.BlockSpec((1, width, tile), block_at)
    return pl.pallas_call(
        functools.partial(gradient_kernel, len(sources), turn > 0, columns),
        out_shape=jax.ShapeDtypeStruct((per_block, width, depth), jnp.float32),
        grid_spec=pltpu.PrefetchScalarGridSpec(
            num_scalar_prefetch=2,
            grid=(half_count, 1, depth // tile),
            in_specs=[square, square, ANY]
            + [pl.BlockSpec((1, x.shape[1], tile), source_at) for x in sources]
            + ([] if base is None else [out_spec] if turn > 0 else [ANY]),
            out_specs=out_spec,
        ),
        input_output_aliases={} if base is None else {5 + len(sources): 0},
        compiler_params=params(44),
        cost_estimate=cost(),
    )(plan, state, high, low, token, *sources, *(() if base is None else (base,)))


def chain(env, turn, offset, first):
    bits, per_block = env["bits"], env["per_block"]
    half_count = per_block // 2
    token = yield None
    keep, give = integral(env["three_index"], first, env["plan"], env["state"], token, turn, env["blocks"])
    came = swapped(give, "pair", 0)
    token = yield give
    for stage in range(bits):
        keep, give = parted(keep, came, token)
        came = across(give, stage)
        token = yield give
    row = env["virtual"][None, offset : offset + first.shape[1]]
    value = amplitude(
        env["info"], env["peer_info"][turn], env["state"], env["column"], row, keep, came, token, turn, per_block
    )
    if turn > 0:
        came = swapped(value, "pair", turn)
        token = yield value
        value = joined(value, came, token, 1)
    for stage in reversed(range(bits)):
        came = across(value, stage)
        token = yield value
        if stage > 0 or turn == 0:
            value = joined(value, came, token, 2)
        else:
            value, give = last_joined(value, came, token)
    if turn == 0:
        value = value.reshape((2 * half_count,) + value.shape[2:])
        came = swapped(value, "pair", 0)
        env["gathered"][turn].append((value, came, (0, half_count), (half_count, 0)))
    else:
        came = swapped(give, "pair", 0)
        env["gathered"][turn].append((value, came, (0, 0), (half_count, half_count)))
    yield value


def body(three_index, occupied_energy, virtual_energy, plan):
    per_block, width, depth = three_index.shape
    half_count = per_block // 2
    aux_count = lax.axis_size("aux")
    bits = aux_count.bit_length() - 1
    blocks = 2 * aux_count
    row_count = width // aux_count
    aux = lax.axis_index("aux").astype(jnp.int32)
    rounds = plan.shape[0]
    position = lax.axis_index("pair").astype(jnp.int32)

    def mask(order):
        return sum((aux >> bit & 1) << bits - 1 - step for step, bit in enumerate(order))

    first_mask, second_mask = (mask(order) for order in orders(bits))
    core = position % 2
    state = jnp.stack(
        [
            position,
            jnp.where(core == 0, first_mask, second_mask),
            jnp.where(core == 0, second_mask, first_mask),
            aux,
        ]
    ).astype(jnp.int32)

    mine = jnp.concatenate([occupied_energy, plan.astype(jnp.float32).reshape(-1)])
    core_info = swapped(mine, "pair", 0)
    info = jnp.stack([mine, core_info])
    peer_info = [jnp.stack([core_info, mine])]
    peer_info += [swapped(info, "pair", turn) for turn in range(1, rounds)]
    cuts, pieces = 2, 4
    step = width // cuts
    firsts = [None] * rounds
    token = virtual_energy
    for turn in range(1, rounds):
        firsts[turn] = []
        for cut in range(cuts):
            token = picked(three_index, plan, state, token, turn, False, cut, cuts)
            firsts[turn].append(swapped(token, "pair", turn))
    other = swapped(three_index, "pair", 0)
    firsts[0] = [other]
    env = {
        "bits": bits,
        "per_block": per_block,
        "blocks": blocks,
        "plan": plan,
        "state": state,
        "three_index": three_index,
        "virtual": virtual_energy,
        "column": virtual_energy[:, None],
        "info": info,
        "peer_info": peer_info,
        "gathered": [[] for _ in range(rounds)],
    }
    seconds = [[other]] + [[] for _ in range(1, rounds)]
    gradient = None
    tilde = [None] * rounds
    densities = []

    def send_piece(turn, piece):
        def run(token):
            token = picked(three_index, plan, state, token, turn, True, piece, pieces)
            seconds[turn].append(swapped(token, "pair", turn))
            return token

        return run

    def make_tilde(turn):
        def run(token):
            high, low, density = tildes(state, token, env["gathered"][turn], blocks, row_count, half_count)
            tilde[turn] = (high, low)
            densities.append(density)
            return density

        return run

    def add_terms(turn, own):
        def run(token):
            nonlocal gradient
            sources = firsts[turn] if own else seconds[turn]
            gradient = gradient_terms(
                plan, state, token, *tilde[turn], sources, gradient, turn, own, three_index
            )
            return gradient

        return run

    tasks = []
    late = []
    for turn in range(rounds):
        for cut, first in enumerate(firsts[turn]):
            worker = chain(env, turn, cut * step if turn else 0, first)
            next(worker)
            share = first.shape[1] / width
            clock = 12.0 if turn == 0 else 41.0 + 35.0 * cut + 137.0 * (turn - 1)
            times = [clock, clock + 4 + 8 * share]
            wide = 12.8 * share
            for stage in range(bits):
                times.append(times[-1] + 4 + (wide / 2 if stage == 1 else wide))
            if turn > 0:
                wide *= 2
                times.append(times[-1] + 8)
            for stage in range(bits):
                times.append(times[-1] + 4 + (wide / 2 if stage == 1 else wide))
            tasks += [(time, worker.send) for time in times]
            late.append(times)
    for turn in range(1, rounds):
        tasks += [(66.0 + 17.0 * piece + 137.0 * (turn - 1), send_piece(turn, piece)) for piece in range(pieces)]
    for turn in range(rounds):
        steps = [make_tilde(turn), add_terms(turn, True), add_terms(turn, False)]
        if turn == 0 and rounds > 1:
            tasks += [(time + 1, step_) for time, step_ in zip(late[cuts][-3:], steps)]
        else:
            tasks += [(late[-1][-1] + 6 + index, step_) for index, step_ in enumerate(steps)]
    tasks.sort(key=lambda task: task[0])
    for _, task in tasks:
        token = task(token)
    density = sum(densities)
    for bit in reversed(range(lax.axis_size("pair").bit_length() - 1)):
        half = density.shape[1] // 2
        side = position >> bit & 1
        give = lax.dynamic_slice_in_dim(density, (1 - side) * half, half, 1)
        density = lax.dynamic_slice_in_dim(density, side * half, half, 1) + swapped(give, "pair", bit)
    return (gradient, density)


def solution(mesh):
    in_specs = (P("pair", None, "aux"), P("pair"), P(), P(None, "pair"))
    out_specs = (P("pair", None, "aux"), P("aux", "pair"))
    return jax.shard_map(body, mesh=mesh, in_specs=in_specs, out_specs=out_specs, check_vma=False)
```

```python
import functools

import jax
import jax.numpy as jnp
from jax import lax
from jax.experimental import pallas as pl
from jax.experimental.pallas import tpu as pltpu
from jax.sharding import PartitionSpec as P

VMEM = pl.BlockSpec(memory_space=pltpu.VMEM)
SMEM = pl.BlockSpec(memory_space=pltpu.SMEM)
ANY = pl.BlockSpec(memory_space=pl.ANY)


def params(mebibytes):
    return pltpu.CompilerParams(vmem_limit_bytes=mebibytes * 2**20)


def cost():
    return pl.CostEstimate(flops=1, bytes_accessed=1, transcendentals=0)


def swapped(block, axis, bit):
    count = lax.axis_size(axis)
    route = []
    for low in range(count):
        high = low | 1 << bit
        if high != low and high < count:
            route += [(low, high), (high, low)]
    return lax.ppermute(block, axis, route)


def orders(bits):
    return (list(range(bits)), [1, 0] + list(range(2, bits)))


def across(block, step):
    pairs, auxes = lax.axis_size("pair"), lax.axis_size("aux")
    order = orders(auxes.bit_length() - 1)
    route = []
    for p in range(pairs):
        for m in range(auxes):
            route.append((p * auxes + m, p * auxes + (m ^ 1 << order[p % 2][step])))
    return lax.ppermute(block, ("pair", "aux"), route)


def halves(value):
    high = value.astype(jnp.bfloat16)
    return high, (value - high.astype(jnp.float32)).astype(jnp.bfloat16)


def multiply(left, right, dims):
    (lh, ll), (rh, rl) = left, right
    one = functools.partial(
        lax.dot_general, dimension_numbers=(dims, ((), ())), preferred_element_type=jnp.float32
    )
    if dims[0] == (1,):
        count = lh.shape[0]
        both = one(jnp.concatenate([lh, ll], axis=0), rh)
        return both[:count] + (both[count:] + one(lh, rl))
    return one(lh, rh) + (one(lh, rl) + one(ll, rh))


def upper_in(position, turn):
    return position // 2**turn % 2 == 1


def slot_of(plan_ref, state_ref, per_block, turn, h, own):
    half_count = per_block // 2
    plain = jnp.where(own, h, half_count + h)
    wanted = jnp.where(own, half_count + h, h)
    inverse = 0
    for k in range(per_block):
        inverse += jnp.where(plan_ref[turn, k] == wanted, k, 0)
    return jnp.where(upper_in(state_ref[0], turn), inverse, plain)


def peer_slot_of(plan_ref, state_ref, per_block, turn, h, own):
    half_count = per_block // 2
    plain = jnp.where(own, h, half_count + h)
    wanted = jnp.where(own, half_count + h, h)
    paired = 0
    for k in range(per_block):
        paired += jnp.where(plain == k, plan_ref[turn, k], 0)
    return jnp.where(upper_in(state_ref[0], turn), wanted, paired)


def copy_kernel(plan_ref, state_ref, source_ref, token_ref, target_ref):
    del plan_ref, state_ref, token_ref
    target_ref[...] = source_ref[...]


def picked(three_index, plan, state, token, turn, own, part, parts):
    per_block, width, depth = three_index.shape
    half_count = per_block // 2
    count = width if own else width // parts
    depth = depth // parts if own else depth
    rows = count // 2

    def source(h, piece, plan_ref, state_ref):
        slot = slot_of(plan_ref, state_ref, per_block, turn, h, own)
        return (slot, piece, part) if own else (slot, part * 2 + piece, 0)

    return pl.pallas_call(
        copy_kernel,
        out_shape=jax.ShapeDtypeStruct((half_count, count, depth), jnp.float32),
        grid_spec=pltpu.PrefetchScalarGridSpec(
            num_scalar_prefetch=2,
            grid=(half_count, count // rows),
            in_specs=[pl.BlockSpec((1, rows, depth), source), ANY],
            out_specs=pl.BlockSpec((1, rows, depth), lambda h, piece, *_: (h, piece, 0)),
        ),
        compiler_params=params(24),
        cost_estimate=cost(),
    )(plan, state, three_index, token)


def gate_kernel(*refs):
    refs[-1][...] = jnp.zeros_like(refs[-1])


def gated(*tokens):
    return pl.pallas_call(
        gate_kernel,
        out_shape=jax.ShapeDtypeStruct((8, 128), jnp.float32),
        in_specs=[ANY] * len(tokens),
        out_specs=VMEM,
        compiler_params=params(16),
        cost_estimate=cost(),
    )(*tokens)


def integral_kernel(turn, blocks, plan_ref, state_ref, own_ref, token_ref, *refs):
    del plan_ref, token_ref
    keep_ref, give_ref, high, low = refs[-4:]
    band = pl.program_id(1)

    @pl.when(band == 0)
    def _():
        offset = 0
        for peer_ref in refs[:-4]:
            spot = slice(offset, offset + peer_ref.shape[1])
            high[spot, :], low[spot, :] = halves(peer_ref[0])
            offset += peer_ref.shape[1]

    own = halves(own_ref[0])
    value = multiply(own, (high[...], low[...]), ((1,), (1,)))
    rows = keep_ref.shape[1] * 2 // blocks
    core = state_ref[0] % 2
    inside = own_ref.shape[1] // rows
    for part in range(inside):
        index = band * inside + part
        side, place = index // (blocks // 2), index % (blocks // 2)
        piece = value[part * rows : (part + 1) * rows]

        @pl.when(side == core)
        def _():
            keep_ref[0, pl.ds(pl.multiple_of((place ^ state_ref[1]) * rows, rows), rows), :] = piece

        @pl.when(side != core)
        def _():
            give_ref[0, pl.ds(pl.multiple_of((place ^ state_ref[2]) * rows, rows), rows), :] = piece


def integral(three_index, peers, plan, state, token, turn, blocks):
    per_block, width, depth = three_index.shape
    half_count, count = per_block // 2, sum(peer.shape[1] for peer in peers)
    bands = 2
    out = jax.ShapeDtypeStruct((half_count, width // 2, count), jnp.float32)
    whole = pl.BlockSpec((1, width // 2, count), lambda h, band, *_: (h, 0, 0))
    chosen = peers[0].shape[0] == per_block

    def peer_at(h, band, p, s):
        return (peer_slot_of(p, s, per_block, turn, h, True) if chosen else h, 0, 0)

    return pl.pallas_call(
        functools.partial(integral_kernel, turn, blocks),
        out_shape=(out, out),
        grid_spec=pltpu.PrefetchScalarGridSpec(
            num_scalar_prefetch=2,
            grid=(half_count, bands),
            in_specs=[
                pl.BlockSpec(
                    (1, width // bands, depth),
                    lambda h, band, p, s: (slot_of(p, s, per_block, turn, h, True), band, 0),
                ),
                ANY,
            ]
            + [pl.BlockSpec((1, peer.shape[1], depth), peer_at) for peer in peers],
            out_specs=(whole, whole),
            scratch_shapes=[pltpu.VMEM((count, depth), jnp.bfloat16)] * 2,
        ),
        compiler_params=params(44),
        cost_estimate=cost(),
    )(plan, state, three_index, token, *peers)


def part_kernel(keep_ref, came_ref, token_ref, low_ref, high_ref):
    del token_ref
    half = low_ref.shape[2]
    low_ref[0], low_ref[1] = keep_ref[:, :half], came_ref[:, :half]
    high_ref[0], high_ref[1] = keep_ref[:, half:], came_ref[:, half:]


def add_kernel(keep_ref, came_ref, token_ref, low_ref, high_ref):
    del token_ref
    half = low_ref.shape[2]
    low_ref[...] = keep_ref[:, :, :half] + came_ref[:, :, :half]
    high_ref[...] = keep_ref[:, :, half:] + came_ref[:, :, half:]


def parted(keep, came, token):
    joined = len(keep.shape) == 3
    shape = ((2,) if joined else ()) + keep.shape
    out = jax.ShapeDtypeStruct(shape[:2] + (shape[2] // 2,) + shape[3:], jnp.float32)
    return pl.pallas_call(
        part_kernel if joined else add_kernel,
        out_shape=(out, out),
        in_specs=[VMEM, VMEM, ANY],
        out_specs=(VMEM, VMEM),
        compiler_params=params(16),
        cost_estimate=cost(),
    )(keep, came, token)


def last_kernel(one_ref, two_ref, token_ref, keep_ref, give_ref):
    del token_ref
    half = one_ref.shape[2]
    keep_ref[:, :half], keep_ref[:, half:] = one_ref[0], two_ref[0]
    give_ref[:, :half], give_ref[:, half:] = one_ref[1], two_ref[1]


def last_joined(one, two, token):
    out = jax.ShapeDtypeStruct((one.shape[1], 2 * one.shape[2], one.shape[3]), jnp.float32)
    return pl.pallas_call(
        last_kernel,
        out_shape=(out, out),
        in_specs=[VMEM, VMEM, ANY],
        out_specs=(VMEM, VMEM),
        compiler_params=params(24),
        cost_estimate=cost(),
    )(one, two, token)


def join_kernel(axis, one_ref, two_ref, token_ref, out_ref):
    del token_ref
    half = one_ref.shape[axis]
    if axis == 1:
        out_ref[:, :half], out_ref[:, half:] = one_ref[...], two_ref[...]
    else:
        out_ref[:, :, :half], out_ref[:, :, half:] = one_ref[...], two_ref[...]


def joined(one, two, token, axis):
    shape = list(one.shape)
    shape[axis] *= 2
    return pl.pallas_call(
        functools.partial(join_kernel, axis),
        out_shape=jax.ShapeDtypeStruct(tuple(shape), jnp.float32),
        in_specs=[VMEM, VMEM, ANY],
        out_specs=VMEM,
        compiler_params=params(24),
        cost_estimate=cost(),
    )(one, two, token)


def amplitude_kernel(turn, per_block, ours_ref, theirs_ref, state_ref, column_ref, row_ref, left_ref, right_ref, token_ref, out_ref):
    del token_ref
    half_count = per_block // 2
    rows = out_ref.shape[2]
    place = state_ref[0] % 2 * lax.div(column_ref.shape[0], 2 * rows) + state_ref[1]
    down = column_ref[pl.ds(pl.multiple_of(place * rows, rows), rows), :]
    for who in range(2):
        upper = upper_in(state_ref[0] ^ who, turn)
        for h in range(half_count):
            low = ours_ref[who, h]
            high = theirs_ref[who, half_count + h]
            wanted = ours_ref[who, per_block * (turn + 1) + h]
            for k in range(per_block):
                slot = ours_ref[who, per_block * (turn + 1) + k]
                high += jnp.where(slot == half_count + h, ours_ref[who, k], 0.0)
                low += jnp.where(wanted == k, theirs_ref[who, k], 0.0)
            gap = jnp.where(upper, high, low) - down - row_ref[...]
            out_ref[who, h] = (left_ref[who, h] + right_ref[who, h]) / gap


def amplitude(ours, theirs, state, column, row, left, right, token, turn, per_block):
    return pl.pallas_call(
        functools.partial(amplitude_kernel, turn, per_block),
        out_shape=jax.ShapeDtypeStruct(left.shape, jnp.float32),
        in_specs=[SMEM, SMEM, SMEM, VMEM, VMEM, VMEM, VMEM, ANY],
        out_specs=VMEM,
        compiler_params=params(16),
        cost_estimate=cost(),
    )(ours, theirs, state, column, row, left, right, token)


def tilde_kernel(blocks, places, state_ref, token_ref, *refs):
    del token_ref
    count = len(places)
    sources, (high_ref, low_ref, density_ref, amp, tilde) = refs[: 2 * count], refs[2 * count :]
    width = amp.shape[0]
    rows = width // blocks
    core = state_ref[0] % 2
    share = density_ref.shape[0]
    band = 128 if width % 128 == 0 else width
    for h in range(high_ref.shape[1]):
        for who in range(2):
            offset = 0
            for part in range(count):
                mine, came = sources[2 * part], sources[2 * part + 1]
                first, second = (start + h for start in places[part][who])
                size = mine.shape[2]
                for place in range(blocks // 2):
                    here = slice(place * rows, (place + 1) * rows)
                    spot = (core * (blocks // 2) + (place ^ state_ref[1])) * rows
                    amp[pl.ds(pl.multiple_of(spot, rows), rows), offset : offset + size] = mine[first, here, :]
                    spot = ((1 - core) * (blocks // 2) + (place ^ state_ref[2])) * rows
                    amp[pl.ds(pl.multiple_of(spot, rows), rows), offset : offset + size] = came[second, here, :]
                offset += size
            for part in range(width // band):
                spot = slice(part * band, (part + 1) * band)
                straight, turned = amp[spot, :], amp[:, spot].T
                value = 2.0 * straight - turned if who == 0 else 2.0 * turned - straight
                if who == 0:
                    tilde[spot, :] = value
                high_ref[who, h, spot, :], low_ref[who, h, spot, :] = halves(value)
            if who == 0:
                start = pl.ds(pl.multiple_of(state_ref[3] * share, share), share)
                straight = amp[start, :]
                turned = 2.0 * straight - tilde[start, :]
                both = (high_ref[0, h], low_ref[0, h])
                value = multiply(halves(straight), both, ((1,), (1,)))
                value += multiply(halves(turned), both, ((1,), (0,)))
                if h == 0:
                    density_ref[...] = value
                else:
                    density_ref[...] += value


def tildes(state, token, gathered, blocks, share, half_count):
    sources = [array for mine, came, _, _ in gathered for array in (mine, came)]
    places = [spots for _, _, *spots in gathered]
    width = 2 * sources[0].shape[1]
    out = jax.ShapeDtypeStruct((2, half_count, width, width), jnp.bfloat16)
    return pl.pallas_call(
        functools.partial(tilde_kernel, blocks, places),
        out_shape=(out, out, jax.ShapeDtypeStruct((share, width), jnp.float32)),
        in_specs=[SMEM, ANY] + [VMEM] * len(sources),
        out_specs=(VMEM, VMEM, VMEM),
        scratch_shapes=[pltpu.VMEM((width, width), jnp.float32)] * 2,
        compiler_params=params(48),
        cost_estimate=cost(),
    )(state, token, *sources)


def gradient_kernel(count, based, columns, plan_ref, state_ref, high_ref, low_ref, token_ref, *refs):
    del plan_ref, state_ref, token_ref
    out_ref, done_ref = refs[-2:]
    done_ref[...] = jnp.zeros_like(done_ref)

    def term(spot, source):
        tilde = (high_ref[0, 0, :, spot], low_ref[0, 0, :, spot])
        return multiply(tilde, halves(source[0]), ((1,), (0,)))

    if columns:
        for piece, source in enumerate(refs[:count]):

            @pl.when(pl.program_id(2) == piece)
            def _():
                out_ref[0] = refs[count][0] + term(slice(None), source)

        return
    value = refs[count][0] if based else None
    offset = 0
    for source in refs[:count]:
        added = term(slice(offset, offset + source.shape[1]), source)
        value = added if value is None else value + added
        offset += source.shape[1]
    out_ref[0] = value


def gradient_terms(plan, state, token, high, low, sources, base, turn, own, three_index):
    per_block, width, depth = three_index.shape
    half_count = per_block // 2
    columns = sources[0].shape[2] < depth
    tile = sources[0].shape[2] if columns else depth // 4 if depth % 512 == 0 else depth
    chosen = sources[0].shape[0] == per_block
    at = 0 if own else 1

    def block_at(h, _, piece, p, s):
        return (slot_of(p, s, per_block, turn, h, own), 0, piece)

    def source_at(h, _, piece, p, s):
        slot = peer_slot_of(p, s, per_block, turn, h, own) if chosen else h
        return (slot, 0, 0 if columns else piece)

    square = pl.BlockSpec((1, 1, width, width), lambda h, *_: (at, h, 0, 0))
    out_spec = pl.BlockSpec((1, width, tile), block_at)
    return pl.pallas_call(
        functools.partial(gradient_kernel, len(sources), turn > 0, columns),
        out_shape=(
            jax.ShapeDtypeStruct((per_block, width, depth), jnp.float32),
            jax.ShapeDtypeStruct((8, 128), jnp.float32),
        ),
        grid_spec=pltpu.PrefetchScalarGridSpec(
            num_scalar_prefetch=2,
            grid=(half_count, 1, depth // tile),
            in_specs=[square, square, ANY]
            + [pl.BlockSpec((1, x.shape[1], tile), source_at) for x in sources]
            + ([] if base is None else [out_spec] if turn > 0 else [ANY]),
            out_specs=(out_spec, pl.BlockSpec((8, 128), lambda *_: (0, 0))),
        ),
        input_output_aliases={} if base is None else {5 + len(sources): 0},
        compiler_params=params(44),
        cost_estimate=cost(),
    )(plan, state, high, low, token, *sources, *(() if base is None else (base,)))


def chain(env, turn, offset, peers):
    bits, per_block = env["bits"], env["per_block"]
    half_count = per_block // 2
    token = yield None
    keep, give = integral(env["three_index"], peers, env["plan"], env["state"], token, turn, env["blocks"])
    came = swapped(give, "pair", 0)
    token = yield give
    for stage in range(bits):
        keep, give = parted(keep, came, token)
        came = across(give, stage)
        token = yield give
    row = env["virtual"][None, offset : offset + keep.shape[3]]
    value = amplitude(
        env["info"], env["peer_info"][turn], env["state"], env["column"], row, keep, came, token, turn, per_block
    )
    if turn > 0:
        came = swapped(value, "pair", turn)
        token = yield value
        value = joined(value, came, token, 1)
    for stage in reversed(range(bits)):
        came = across(value, stage)
        token = yield value
        if stage > 0 or turn == 0:
            value = joined(value, came, token, 2)
        else:
            value, give = last_joined(value, came, token)
    if turn == 0:
        value = value.reshape((2 * half_count,) + value.shape[2:])
        came = swapped(value, "pair", 0)
        env["gathered"][turn].append((value, came, (0, half_count), (half_count, 0)))
    else:
        came = swapped(give, "pair", 0)
        env["gathered"][turn].append((value, came, (0, 0), (half_count, half_count)))
    yield value


def body(three_index, occupied_energy, virtual_energy, plan):
    per_block, width, depth = three_index.shape
    half_count = per_block // 2
    aux_count = lax.axis_size("aux")
    bits = aux_count.bit_length() - 1
    blocks = 2 * aux_count
    row_count = width // aux_count
    aux = lax.axis_index("aux").astype(jnp.int32)
    rounds = plan.shape[0]
    position = lax.axis_index("pair").astype(jnp.int32)

    def mask(order):
        return sum((aux >> bit & 1) << bits - 1 - step for step, bit in enumerate(order))

    first_mask, second_mask = (mask(order) for order in orders(bits))
    core = position % 2
    state = jnp.stack(
        [
            position,
            jnp.where(core == 0, first_mask, second_mask),
            jnp.where(core == 0, second_mask, first_mask),
            aux,
        ]
    ).astype(jnp.int32)

    mine = jnp.concatenate([occupied_energy, plan.astype(jnp.float32).reshape(-1)])
    core_info = swapped(mine, "pair", 0)
    info = jnp.stack([mine, core_info])
    peer_info = [jnp.stack([core_info, mine])]
    peer_info += [swapped(info, "pair", turn) for turn in range(1, rounds)]
    cuts, rows, pieces = 2, 2, 4
    step = width // cuts
    firsts = [None] * rounds
    token = virtual_energy
    for turn in range(1, rounds):
        firsts[turn] = []
        for piece in range(cuts * rows):
            token = picked(three_index, plan, state, token, turn, False, piece, cuts * rows)
            firsts[turn].append(swapped(token, "pair", turn))
    other = swapped(three_index, "pair", 0)
    firsts[0] = [other]
    env = {
        "bits": bits,
        "per_block": per_block,
        "blocks": blocks,
        "plan": plan,
        "state": state,
        "three_index": three_index,
        "virtual": virtual_energy,
        "column": virtual_energy[:, None],
        "info": info,
        "peer_info": peer_info,
        "gathered": [[] for _ in range(rounds)],
    }
    seconds = [[other]] + [[] for _ in range(1, rounds)]
    gradient = None
    tilde = [None] * rounds
    densities = []

    def gate(*arrived):
        return lambda token: gated(token, *arrived)

    def gate_piece(turn, piece):
        return lambda token: gated(token, seconds[turn][piece])

    def send_piece(turn, piece):
        def run(token):
            token = picked(three_index, plan, state, token, turn, True, piece, pieces)
            seconds[turn].append(swapped(token, "pair", turn))
            return token

        return run

    def make_tilde(turn):
        def run(token):
            high, low, density = tildes(state, token, env["gathered"][turn], blocks, row_count, half_count)
            tilde[turn] = (high, low)
            densities.append(density)
            return density

        return run

    def add_terms(turn, own):
        def run(token):
            nonlocal gradient
            sources = firsts[turn] if own else seconds[turn]
            gradient, token = gradient_terms(
                plan, state, token, *tilde[turn], sources, gradient, turn, own, three_index
            )
            return token

        return run

    tasks = [(20.0, gate(*peer_info))]
    late = []
    for turn in range(rounds):
        arrivals = [42.0 + 36.0 * cut + 137.0 * (turn - 1) for cut in range(cuts)] if turn else [11.0]
        groups = [firsts[turn][cut * rows : (cut + 1) * rows] for cut in range(cuts)] if turn else [[other]]
        for cut, (clock, peers) in enumerate(zip(arrivals, groups)):
            worker = chain(env, turn, cut * step, peers)
            next(worker)
            share = 1 / len(groups)
            times = [clock, clock + 4 + 8 * share]
            wide = 12.8 * share
            for stage in range(bits):
                times.append(times[-1] + 4 + (wide / 2 if stage == 1 else wide))
            if turn > 0:
                wide *= 2
                times.append(times[-1] + 8)
            for stage in range(bits):
                times.append(times[-1] + 4 + (wide / 2 if stage == 1 else wide))
            tasks += [(time, worker.send) for time in times]
            late.append(times)
            if turn > 0:
                tasks.append((clock - 20.0, gate(peers[0])))
    for turn in range(1, rounds):
        for piece in range(pieces):
            time = 94.0 + 17.0 * piece + 137.0 * (turn - 1) + (4.0 if piece == pieces - 1 else 0.0)
            tasks += [(time - 20.0, send_piece(turn, piece)), (time, gate_piece(turn, piece))]
    for turn in range(rounds):
        steps = [make_tilde(turn), add_terms(turn, True), add_terms(turn, False)]
        if turn == 0 and rounds > 1:
            tasks += [(time + 1, step_) for time, step_ in zip(late[cuts][-3:], steps)]
        else:
            tasks += [(late[-1][-1] + 6 + index, step_) for index, step_ in enumerate(steps)]
    tasks.sort(key=lambda task: task[0])
    for _, task in tasks:
        token = task(token)
    density = sum(densities)
    for bit in reversed(range(lax.axis_size("pair").bit_length() - 1)):
        half = density.shape[1] // 2
        side = position >> bit & 1
        give = lax.dynamic_slice_in_dim(density, (1 - side) * half, half, 1)
        density = lax.dynamic_slice_in_dim(density, side * half, half, 1) + swapped(give, "pair", bit)
    return (gradient, density)


def solution(mesh):
    in_specs = (P("pair", None, "aux"), P("pair"), P(), P(None, "pair"))
    out_specs = (P("pair", None, "aux"), P("aux", "pair"))
    return jax.shard_map(body, mesh=mesh, in_specs=in_specs, out_specs=out_specs, check_vma=False)
```

```python
import functools

import jax
import jax.numpy as jnp
from jax import lax
from jax.experimental import pallas as pl
from jax.experimental.pallas import tpu as pltpu
from jax.sharding import PartitionSpec as P

VMEM = pl.BlockSpec(memory_space=pltpu.VMEM)
SMEM = pl.BlockSpec(memory_space=pltpu.SMEM)
ANY = pl.BlockSpec(memory_space=pl.ANY)


def params(mebibytes):
    return pltpu.CompilerParams(vmem_limit_bytes=mebibytes * 2**20)


def cost():
    return pl.CostEstimate(flops=1, bytes_accessed=1, transcendentals=0)


def swapped(block, axis, bit):
    count = lax.axis_size(axis)
    route = []
    for low in range(count):
        high = low | 1 << bit
        if high != low and high < count:
            route += [(low, high), (high, low)]
    return lax.ppermute(block, axis, route)


def orders(bits):
    return (list(range(bits)), [1, 0] + list(range(2, bits)))


def across(block, step):
    pairs, auxes = lax.axis_size("pair"), lax.axis_size("aux")
    order = orders(auxes.bit_length() - 1)
    route = []
    for p in range(pairs):
        for m in range(auxes):
            route.append((p * auxes + m, p * auxes + (m ^ 1 << order[p % 2][step])))
    return lax.ppermute(block, ("pair", "aux"), route)


def halves(value):
    high = value.astype(jnp.bfloat16)
    return high, (value - high.astype(jnp.float32)).astype(jnp.bfloat16)


def multiply(left, right, dims):
    rh, rl = right
    one = functools.partial(
        lax.dot_general, dimension_numbers=(dims, ((), ())), preferred_element_type=jnp.float32
    )
    count = left.shape[0] // 2
    both = one(left, rh)
    return both[:count] + (both[count:] + one(left[:count], rl))


def stacked(value):
    return jnp.concatenate(halves(value), axis=0)


def upper_in(position, turn):
    return position // 2**turn % 2 == 1


def slot_of(plan_ref, state_ref, per_block, turn, h, own):
    half_count = per_block // 2
    plain = jnp.where(own, h, half_count + h)
    wanted = jnp.where(own, half_count + h, h)
    inverse = 0
    for k in range(per_block):
        inverse += jnp.where(plan_ref[turn, k] == wanted, k, 0)
    return jnp.where(upper_in(state_ref[0], turn), inverse, plain)


def peer_slot_of(plan_ref, state_ref, per_block, turn, h, own):
    half_count = per_block // 2
    plain = jnp.where(own, h, half_count + h)
    wanted = jnp.where(own, half_count + h, h)
    paired = 0
    for k in range(per_block):
        paired += jnp.where(plain == k, plan_ref[turn, k], 0)
    return jnp.where(upper_in(state_ref[0], turn), wanted, paired)


def copy_kernel(extra, plan_ref, state_ref, source_ref, *refs):
    del plan_ref, state_ref
    rows = source_ref.shape[1]
    refs[-1][:, :rows] = source_ref[...]
    if extra:
        refs[-1][:, rows:] = refs[0][...][None]


def picked(three_index, plan, state, token, turn, own, part, parts, extra=None):
    per_block, width, depth = three_index.shape
    half_count = per_block // 2
    rows = width if own else width // parts
    depth = depth // parts if own else depth
    count = rows + (0 if extra is None else extra.shape[0])

    def source(h, plan_ref, state_ref):
        slot = slot_of(plan_ref, state_ref, per_block, turn, h, own)
        return (slot, 0, part) if own else (slot, part, 0)

    return pl.pallas_call(
        functools.partial(copy_kernel, extra is not None),
        out_shape=jax.ShapeDtypeStruct((half_count, count, depth), jnp.float32),
        grid_spec=pltpu.PrefetchScalarGridSpec(
            num_scalar_prefetch=2,
            grid=(half_count,),
            in_specs=[pl.BlockSpec((1, rows, depth), source)]
            + ([] if extra is None else [VMEM])
            + [ANY],
            out_specs=pl.BlockSpec((1, count, depth), lambda h, *_: (h, 0, 0)),
        ),
        compiler_params=params(24),
        cost_estimate=cost(),
    )(plan, state, three_index, *(() if extra is None else (extra,)), token)


def gate_kernel(*refs):
    refs[-1][...] = jnp.zeros_like(refs[-1])


def gated(*tokens):
    return pl.pallas_call(
        gate_kernel,
        out_shape=jax.ShapeDtypeStruct((8, 128), jnp.float32),
        in_specs=[ANY] * len(tokens),
        out_specs=VMEM,
        compiler_params=params(16),
        cost_estimate=cost(),
    )(*tokens)


def integral_kernel(turn, blocks, plan_ref, state_ref, own_ref, token_ref, *refs):
    del plan_ref, token_ref
    keep_ref, give_ref, high, low = refs[-4:]
    band = pl.program_id(1)
    count = high.shape[0] // (len(refs) - 4)

    @pl.when(band == 0)
    def _():
        for index, peer_ref in enumerate(refs[:-4]):
            spot = slice(index * count, (index + 1) * count)
            high[spot, :], low[spot, :] = halves(peer_ref[0, :count])

    value = multiply(stacked(own_ref[0]), (high[...], low[...]), ((1,), (1,)))
    rows = keep_ref.shape[1] * 2 // blocks
    inside = own_ref.shape[1] // rows
    for part in range(inside):
        place = (band * inside + part) ^ state_ref[1]
        piece = value[part * rows : (part + 1) * rows]

        @pl.when(place < blocks // 2)
        def _():
            keep_ref[0, pl.ds(pl.multiple_of(place * rows, rows), rows), :] = piece

        @pl.when(place >= blocks // 2)
        def _():
            spot = (place - blocks // 2) * rows
            give_ref[0, pl.ds(pl.multiple_of(spot, rows), rows), :] = piece


def integral(three_index, peers, plan, state, token, turn, blocks, count):
    per_block, width, depth = three_index.shape
    half_count = per_block // 2
    bands = 2
    out = jax.ShapeDtypeStruct((half_count, width // 2, count), jnp.float32)
    whole = pl.BlockSpec((1, width // 2, count), lambda h, band, *_: (h, 0, 0))
    chosen = peers[0].shape[0] == per_block

    def peer_at(h, band, p, s):
        return (peer_slot_of(p, s, per_block, turn, h, True) if chosen else h, 0, 0)

    return pl.pallas_call(
        functools.partial(integral_kernel, turn, blocks),
        out_shape=(out, out),
        grid_spec=pltpu.PrefetchScalarGridSpec(
            num_scalar_prefetch=2,
            grid=(half_count, bands),
            in_specs=[
                pl.BlockSpec(
                    (1, width // bands, depth),
                    lambda h, band, p, s: (slot_of(p, s, per_block, turn, h, True), band, 0),
                ),
                ANY,
            ]
            + [pl.BlockSpec((1, peer.shape[1], depth), peer_at) for peer in peers],
            out_specs=(whole, whole),
            scratch_shapes=[pltpu.VMEM((count, depth), jnp.bfloat16)] * 2,
        ),
        compiler_params=params(44),
        cost_estimate=cost(),
    )(plan, state, three_index, token, *peers)


def add_kernel(keep_ref, came_ref, token_ref, low_ref, high_ref):
    del token_ref
    half = low_ref.shape[1]
    low_ref[...] = keep_ref[:, :half] + came_ref[:, :half]
    high_ref[...] = keep_ref[:, half:] + came_ref[:, half:]


def parted(keep, came, token):
    out = jax.ShapeDtypeStruct((keep.shape[0], keep.shape[1] // 2, keep.shape[2]), jnp.float32)
    return pl.pallas_call(
        add_kernel,
        out_shape=(out, out),
        in_specs=[VMEM, VMEM, ANY],
        out_specs=(VMEM, VMEM),
        compiler_params=params(16),
        cost_estimate=cost(),
    )(keep, came, token)


def join_kernel(axis, one_ref, two_ref, token_ref, out_ref):
    del token_ref
    half = one_ref.shape[axis]
    if axis == 0:
        out_ref[:half], out_ref[half:] = one_ref[...], two_ref[...]
    else:
        out_ref[:, :half], out_ref[:, half:] = one_ref[...], two_ref[...]


def joined(one, two, token, axis):
    shape = list(one.shape)
    shape[axis] *= 2
    return pl.pallas_call(
        functools.partial(join_kernel, axis),
        out_shape=jax.ShapeDtypeStruct(tuple(shape), jnp.float32),
        in_specs=[VMEM, VMEM, ANY],
        out_specs=VMEM,
        compiler_params=params(24),
        cost_estimate=cost(),
    )(one, two, token)


def amplitude_kernel(turn, per_block, ours_ref, theirs_ref, state_ref, column_ref, row_ref, left_ref, right_ref, token_ref, out_ref):
    del token_ref
    half_count = per_block // 2
    rows = out_ref.shape[1]
    down = column_ref[pl.ds(pl.multiple_of(state_ref[1] * rows, rows), rows), :]
    theirs = theirs_ref[...].reshape(theirs_ref.shape[-2:])
    upper = upper_in(state_ref[0], turn)
    for h in range(half_count):
        low = ours_ref[0, h] + jnp.zeros((1, 1), jnp.float32)
        high = theirs[0:1, half_count + h : half_count + h + 1]
        wanted = ours_ref[0, per_block * (turn + 1) + h]
        for k in range(per_block):
            slot = ours_ref[0, per_block * (turn + 1) + k]
            high = high + jnp.where(slot == half_count + h, ours_ref[0, k], 0.0)
            low = low + jnp.where(wanted == k, 1.0, 0.0) * theirs[0:1, k : k + 1]
        gap = jnp.where(upper, high, low) - down - row_ref[...]
        out_ref[h] = (left_ref[h] + right_ref[h]) / gap


def amplitude(ours, theirs, theirs_spec, state, column, row, left, right, token, turn, per_block):
    return pl.pallas_call(
        functools.partial(amplitude_kernel, turn, per_block),
        out_shape=jax.ShapeDtypeStruct(left.shape, jnp.float32),
        grid=(1,),
        in_specs=[SMEM, theirs_spec, SMEM, VMEM, VMEM, VMEM, VMEM, ANY],
        out_specs=VMEM,
        compiler_params=params(16),
        cost_estimate=cost(),
    )(ours, theirs, state, column, row, left, right, token)


def tilde_kernel(blocks, places, state_ref, token_ref, *refs):
    del token_ref
    count = len(places)
    sources, (tall_ref, density_ref, amp, tilde) = refs[: 2 * count], refs[2 * count :]
    width = amp.shape[0]
    rows = width // blocks
    share = density_ref.shape[0]
    band = 128 if width % 128 == 0 else width
    for h in range(tall_ref.shape[1]):
        for who in range(2):
            offset = 0
            for part in range(count):
                first, order = places[part][who]
                source = sources[2 * part + who]
                size = source.shape[2]
                for place in range(blocks):
                    spot = pl.ds(pl.multiple_of((place ^ state_ref[order]) * rows, rows), rows)
                    amp[spot, offset : offset + size] = source[first + h, place * rows : (place + 1) * rows, :]
                offset += size
            for part in range(width // band):
                spot = slice(part * band, (part + 1) * band)
                straight, turned = amp[spot, :], amp[:, spot].T
                value = 2.0 * straight - turned if who == 0 else 2.0 * turned - straight
                if who == 0:
                    tilde[spot, :] = value
                below = slice(width + part * band, width + (part + 1) * band)
                tall_ref[who, h, spot, :], tall_ref[who, h, below, :] = halves(value)
            if who == 0:
                start = pl.ds(pl.multiple_of(state_ref[3] * share, share), share)
                straight = amp[start, :]
                turned = 2.0 * straight - tilde[start, :]
                both = (tall_ref[0, h, :width], tall_ref[0, h, width:])
                value = multiply(stacked(straight), both, ((1,), (1,)))
                value += multiply(stacked(turned), both, ((1,), (0,)))
                if h == 0:
                    density_ref[...] = value
                else:
                    density_ref[...] += value


def tildes(state, token, gathered, blocks, share, half_count):
    sources = [array for own, peer, _ in gathered for array in (own, peer)]
    places = [spots for _, _, spots in gathered]
    width = sources[0].shape[1]
    return pl.pallas_call(
        functools.partial(tilde_kernel, blocks, places),
        out_shape=(
            jax.ShapeDtypeStruct((2, half_count, 2 * width, width), jnp.bfloat16),
            jax.ShapeDtypeStruct((share, width), jnp.float32),
        ),
        in_specs=[SMEM, ANY] + [VMEM] * len(sources),
        out_specs=(VMEM, VMEM),
        scratch_shapes=[pltpu.VMEM((width, width), jnp.float32)] * 2,
        compiler_params=params(48),
        cost_estimate=cost(),
    )(state, token, *sources)


def gradient_kernel(count, based, columns, plan_ref, state_ref, tall_ref, token_ref, *refs):
    del plan_ref, state_ref, token_ref
    out_ref, done_ref = refs[-2:]
    done_ref[...] = jnp.zeros_like(done_ref)

    def term(offset, source):
        size = min(source.shape[1], tall_ref.shape[3] // (1 if columns else count))
        tilde = tall_ref[0, 0, :, offset : offset + size]
        return multiply(tilde, halves(source[0, :size]), ((1,), (0,)))

    if columns:
        for piece, source in enumerate(refs[:count]):

            @pl.when(pl.program_id(2) == piece)
            def _():
                out_ref[0] = refs[count][0] + term(0, source)

        return
    value = refs[count][0] if based else None
    for index, source in enumerate(refs[:count]):
        added = term(index * (tall_ref.shape[3] // count), source)
        value = added if value is None else value + added
    out_ref[0] = value


def gradient_terms(plan, state, token, tall, sources, base, turn, own, three_index):
    per_block, width, depth = three_index.shape
    half_count = per_block // 2
    columns = sources[0].shape[2] < depth
    tile = sources[0].shape[2] if columns else depth // 4 if depth % 512 == 0 else depth
    chosen = sources[0].shape[0] == per_block
    at = 0 if own else 1

    def block_at(h, _, piece, p, s):
        return (slot_of(p, s, per_block, turn, h, own), 0, piece)

    def source_at(h, _, piece, p, s):
        slot = peer_slot_of(p, s, per_block, turn, h, own) if chosen else h
        return (slot, 0, 0 if columns else piece)

    tilde_spec = pl.BlockSpec((1, 1, 2 * width, width), lambda h, *_: (at, h, 0, 0))
    out_spec = pl.BlockSpec((1, width, tile), block_at)
    return pl.pallas_call(
        functools.partial(gradient_kernel, len(sources), turn > 0, columns),
        out_shape=(
            jax.ShapeDtypeStruct((per_block, width, depth), jnp.float32),
            jax.ShapeDtypeStruct((8, 128), jnp.float32),
        ),
        grid_spec=pltpu.PrefetchScalarGridSpec(
            num_scalar_prefetch=2,
            grid=(half_count, 1, depth // tile),
            in_specs=[tilde_spec, ANY]
            + [pl.BlockSpec((1, x.shape[1], tile), source_at) for x in sources]
            + ([] if base is None else [out_spec] if turn > 0 else [ANY]),
            out_specs=(out_spec, pl.BlockSpec((8, 128), lambda *_: (0, 0))),
        ),
        input_output_aliases={} if base is None else {4 + len(sources): 0},
        compiler_params=params(44),
        cost_estimate=cost(),
    )(plan, state, tall, token, *sources, *(() if base is None else (base,)))


def chain(env, turn, offset, size, peers):
    bits, per_block, state = env["bits"], env["per_block"], env["state"]
    half_count = per_block // 2
    count = size // len(peers)
    token = yield None
    keep, give = integral(
        env["three_index"], peers, env["plan"], state, token, turn, env["blocks"], count
    )
    for stage in range(bits - 1):
        came = across(give, stage)
        token = yield give
        keep, give = parted(keep, came, token)
    came = across(give, bits - 1)
    token = yield give
    row = env["virtual"][None, offset : offset + size]
    theirs, spec = env["theirs"][turn]
    value = amplitude(
        env["ours"], theirs, spec, state, env["column"], row, keep, came, token, turn, per_block
    )
    if turn > 0:
        came = swapped(value, "pair", turn)
        token = yield value
        value = joined(value, came, token, 0)
    for stage in reversed(range(bits)):
        came = across(value, stage)
        token = yield value
        value = joined(value, came, token, 1)
    if turn == 0:
        came = swapped(value, "pair", 0)
        env["gathered"][turn].append((value, came, ((0, 1), (0, 2))))
    else:
        env["gathered"][turn].append((value, value, ((0, 1), (half_count, 1))))
    yield value


def body(three_index, occupied_energy, virtual_energy, plan):
    per_block, width, depth = three_index.shape
    half_count = per_block // 2
    aux_count = lax.axis_size("aux")
    bits = aux_count.bit_length() - 1
    blocks = aux_count
    row_count = width // aux_count
    aux = lax.axis_index("aux").astype(jnp.int32)
    rounds = plan.shape[0]
    position = lax.axis_index("pair").astype(jnp.int32)

    def mask(order):
        return sum((aux >> bit & 1) << bits - 1 - step for step, bit in enumerate(order))

    first_mask, second_mask = (mask(order) for order in orders(bits))
    core = position % 2
    state = jnp.stack(
        [
            position,
            jnp.where(core == 0, first_mask, second_mask),
            jnp.where(core == 0, second_mask, first_mask),
            aux,
        ]
    ).astype(jnp.int32)

    mine = jnp.concatenate([occupied_energy, plan.astype(jnp.float32).reshape(-1)])[None]
    extra = jnp.pad(mine, ((0, 7), (0, depth - mine.shape[1])))
    cuts, pieces = 2, 4
    step = width // cuts
    firsts = [None] * rounds
    theirs = [(swapped(mine, "pair", 0), VMEM)]
    token = virtual_energy
    for turn in range(1, rounds):
        firsts[turn] = []
        for cut in range(cuts):
            token = picked(
                three_index, plan, state, token, turn, False, cut, cuts, None if cut else extra
            )
            firsts[turn].append(swapped(token, "pair", turn))
        theirs.append((firsts[turn][0], pl.BlockSpec((1, 8, depth), lambda _: (0, step // 8, 0))))
    other = swapped(three_index, "pair", 0)
    firsts[0] = [other]
    env = {
        "bits": bits,
        "per_block": per_block,
        "blocks": blocks,
        "plan": plan,
        "state": state,
        "three_index": three_index,
        "virtual": virtual_energy,
        "column": virtual_energy[:, None],
        "ours": mine,
        "theirs": theirs,
        "gathered": [[] for _ in range(rounds)],
    }
    seconds = [[other]] + [[] for _ in range(1, rounds)]
    gradient = None
    tilde = [None] * rounds
    densities = []

    def gate_piece(turn, piece):
        return lambda token: gated(token, seconds[turn][piece])

    def send_piece(turn, piece):
        def run(token):
            token = picked(three_index, plan, state, token, turn, True, piece, pieces)
            seconds[turn].append(swapped(token, "pair", turn))
            return token

        return run

    def make_tilde(turn):
        def run(token):
            tilde[turn], density = tildes(
                state, token, env["gathered"][turn], blocks, row_count, half_count
            )
            densities.append(density)
            return density

        return run

    def add_terms(turn, own):
        def run(token):
            nonlocal gradient
            sources = firsts[turn] if own else seconds[turn]
            gradient, token = gradient_terms(
                plan, state, token, tilde[turn], sources, gradient, turn, own, three_index
            )
            return token

        return run

    tasks = []
    late = []
    for turn in range(rounds):
        groups = [[first] for first in firsts[turn]]
        for cut, peers in enumerate(groups):
            clock = 42.0 + 36.0 * cut + 137.0 * (turn - 1) if turn else 11.0
            share = 1 / len(groups)
            worker = chain(env, turn, cut * step, width // len(groups), peers)
            next(worker)
            wide = 12.8 * share
            times = [clock, clock + 3 + 8 * share + wide]
            for stage in range(1, bits):
                times.append(times[-1] + 3 + (wide / 2 if stage == 1 else wide))
            if turn > 0:
                wide *= 2
                times.append(times[-1] + 7)
            for stage in range(bits):
                times.append(times[-1] + 3 + (wide / 2 if stage == 1 else wide))
            tasks += [(time, worker.send) for time in times]
            late.append(times)
    for turn in range(1, rounds):
        begin = 74.0 + 137.0 * (turn - 1)
        for piece, (send, there) in enumerate(((0, 20), (17, 37), (34, 56), (51, 75))):
            tasks += [(begin + send, send_piece(turn, piece)), (begin + there, gate_piece(turn, piece))]
    for turn in range(rounds):
        steps = [make_tilde(turn), add_terms(turn, True), add_terms(turn, False)]
        if turn == 0 and rounds > 1:
            tasks += [(time + 1, step_) for time, step_ in zip(late[cuts][-4:-1], steps)]
        else:
            tasks += [(late[-1][-1] + 6 + index, step_) for index, step_ in enumerate(steps)]
    tasks.sort(key=lambda task: task[0])
    for _, task in tasks:
        token = task(token)
    density = sum(densities)
    for bit in reversed(range(lax.axis_size("pair").bit_length() - 1)):
        half = density.shape[1] // 2
        side = position >> bit & 1
        give = lax.dynamic_slice_in_dim(density, (1 - side) * half, half, 1)
        density = lax.dynamic_slice_in_dim(density, side * half, half, 1) + swapped(give, "pair", bit)
    return (gradient, density)


def solution(mesh):
    in_specs = (P("pair", None, "aux"), P("pair"), P(), P(None, "pair"))
    out_specs = (P("pair", None, "aux"), P("aux", "pair"))
    return jax.shard_map(body, mesh=mesh, in_specs=in_specs, out_specs=out_specs, check_vma=False)
```

```python
import functools

import jax
import jax.numpy as jnp
from jax import lax
from jax.experimental import pallas as pl
from jax.experimental.pallas import tpu as pltpu
from jax.sharding import PartitionSpec as P

VMEM = pl.BlockSpec(memory_space=pltpu.VMEM)
SMEM = pl.BlockSpec(memory_space=pltpu.SMEM)
ANY = pl.BlockSpec(memory_space=pl.ANY)


def params(mebibytes):
    return pltpu.CompilerParams(vmem_limit_bytes=mebibytes * 2**20)


def cost():
    return pl.CostEstimate(flops=1, bytes_accessed=1, transcendentals=0)


def swapped(block, axis, bit):
    count = lax.axis_size(axis)
    route = []
    for low in range(count):
        high = low | 1 << bit
        if high != low and high < count:
            route += [(low, high), (high, low)]
    return lax.ppermute(block, axis, route)


def orders(bits):
    return (list(range(bits)), [1, 0] + list(range(2, bits)))


def across(block, step):
    pairs, auxes = lax.axis_size("pair"), lax.axis_size("aux")
    order = orders(auxes.bit_length() - 1)
    route = []
    for p in range(pairs):
        for m in range(auxes):
            route.append((p * auxes + m, p * auxes + (m ^ 1 << order[p % 2][step])))
    return lax.ppermute(block, ("pair", "aux"), route)


def halves(value):
    high = value.astype(jnp.bfloat16)
    return high, (value - high.astype(jnp.float32)).astype(jnp.bfloat16)


def multiply(left, right, dims):
    rh, rl = right
    one = functools.partial(
        lax.dot_general, dimension_numbers=(dims, ((), ())), preferred_element_type=jnp.float32
    )
    count = left.shape[0] // 2
    both = one(left, rh)
    return both[:count] + (both[count:] + one(left[:count], rl))


def stacked(value):
    return jnp.concatenate(halves(value), axis=0)


def upper_in(position, turn):
    return position // 2**turn % 2 == 1


def slot_of(plan_ref, state_ref, per_block, turn, h, own):
    half_count = per_block // 2
    plain = jnp.where(own, h, half_count + h)
    wanted = jnp.where(own, half_count + h, h)
    inverse = 0
    for k in range(per_block):
        inverse += jnp.where(plan_ref[turn, k] == wanted, k, 0)
    return jnp.where(upper_in(state_ref[0], turn), inverse, plain)


def peer_slot_of(plan_ref, state_ref, per_block, turn, h, own):
    half_count = per_block // 2
    plain = jnp.where(own, h, half_count + h)
    wanted = jnp.where(own, half_count + h, h)
    paired = 0
    for k in range(per_block):
        paired += jnp.where(plain == k, plan_ref[turn, k], 0)
    return jnp.where(upper_in(state_ref[0], turn), wanted, paired)


def copy_kernel(extra, plan_ref, state_ref, source_ref, *refs):
    del plan_ref, state_ref
    rows = source_ref.shape[1]
    refs[-1][:, :rows] = source_ref[...]
    if extra:
        refs[-1][:, rows:] = refs[0][...][None]


def picked(three_index, plan, state, token, turn, own, part, parts, extra=None):
    per_block, width, depth = three_index.shape
    half_count = per_block // 2
    rows = width if own else width // parts
    depth = depth // parts if own else depth
    count = rows + (0 if extra is None else extra.shape[0])

    def source(h, plan_ref, state_ref):
        slot = slot_of(plan_ref, state_ref, per_block, turn, h, own)
        return (slot, 0, part) if own else (slot, part, 0)

    return pl.pallas_call(
        functools.partial(copy_kernel, extra is not None),
        out_shape=jax.ShapeDtypeStruct((half_count, count, depth), jnp.float32),
        grid_spec=pltpu.PrefetchScalarGridSpec(
            num_scalar_prefetch=2,
            grid=(half_count,),
            in_specs=[pl.BlockSpec((1, rows, depth), source)]
            + ([] if extra is None else [VMEM])
            + [ANY],
            out_specs=pl.BlockSpec((1, count, depth), lambda h, *_: (h, 0, 0)),
        ),
        compiler_params=params(24),
        cost_estimate=cost(),
    )(plan, state, three_index, *(() if extra is None else (extra,)), token)


def gate_kernel(*refs):
    refs[-1][...] = jnp.zeros_like(refs[-1])


def gated(*tokens):
    return pl.pallas_call(
        gate_kernel,
        out_shape=jax.ShapeDtypeStruct((8, 128), jnp.float32),
        in_specs=[ANY] * len(tokens),
        out_specs=VMEM,
        compiler_params=params(16),
        cost_estimate=cost(),
    )(*tokens)


def pass_kernel(value_ref, token_ref, out_ref):
    del token_ref
    out_ref[...] = value_ref[...]


def passed(value, token):
    return pl.pallas_call(
        pass_kernel,
        out_shape=jax.ShapeDtypeStruct(value.shape, value.dtype),
        in_specs=[VMEM, ANY],
        out_specs=VMEM,
        compiler_params=params(16),
        cost_estimate=cost(),
    )(value, token)


def integral_kernel(turn, blocks, plan_ref, state_ref, own_ref, token_ref, *refs):
    del plan_ref, token_ref
    keep_ref, give_ref, high, low = refs[-4:]
    band = pl.program_id(1)
    count = high.shape[0] // (len(refs) - 4)

    @pl.when(band == 0)
    def _():
        for index, peer_ref in enumerate(refs[:-4]):
            spot = slice(index * count, (index + 1) * count)
            high[spot, :], low[spot, :] = halves(peer_ref[0, :count])

    value = multiply(stacked(own_ref[0]), (high[...], low[...]), ((1,), (1,)))
    rows = keep_ref.shape[1] * 2 // blocks
    inside = own_ref.shape[1] // rows
    for part in range(inside):
        place = (band * inside + part) ^ state_ref[1]
        piece = value[part * rows : (part + 1) * rows]

        @pl.when(place < blocks // 2)
        def _():
            keep_ref[0, pl.ds(pl.multiple_of(place * rows, rows), rows), :] = piece

        @pl.when(place >= blocks // 2)
        def _():
            spot = (place - blocks // 2) * rows
            give_ref[0, pl.ds(pl.multiple_of(spot, rows), rows), :] = piece


def integral(three_index, peers, plan, state, token, turn, blocks, count):
    per_block, width, depth = three_index.shape
    half_count = per_block // 2
    bands = 2
    out = jax.ShapeDtypeStruct((half_count, width // 2, count), jnp.float32)
    whole = pl.BlockSpec((1, width // 2, count), lambda h, band, *_: (h, 0, 0))
    chosen = peers[0].shape[0] == per_block

    def peer_at(h, band, p, s):
        return (peer_slot_of(p, s, per_block, turn, h, True) if chosen else h, 0, 0)

    return pl.pallas_call(
        functools.partial(integral_kernel, turn, blocks),
        out_shape=(out, out),
        grid_spec=pltpu.PrefetchScalarGridSpec(
            num_scalar_prefetch=2,
            grid=(half_count, bands),
            in_specs=[
                pl.BlockSpec(
                    (1, width // bands, depth),
                    lambda h, band, p, s: (slot_of(p, s, per_block, turn, h, True), band, 0),
                ),
                ANY,
            ]
            + [pl.BlockSpec((1, peer.shape[1], depth), peer_at) for peer in peers],
            out_specs=(whole, whole),
            scratch_shapes=[pltpu.VMEM((count, depth), jnp.bfloat16)] * 2,
        ),
        compiler_params=params(44),
        cost_estimate=cost(),
    )(plan, state, three_index, token, *peers)


def add_kernel(keep_ref, came_ref, token_ref, low_ref, high_ref):
    del token_ref
    half = low_ref.shape[1]
    low_ref[...] = keep_ref[:, :half] + came_ref[:, :half]
    high_ref[...] = keep_ref[:, half:] + came_ref[:, half:]


def parted(keep, came, token):
    out = jax.ShapeDtypeStruct((keep.shape[0], keep.shape[1] // 2, keep.shape[2]), jnp.float32)
    return pl.pallas_call(
        add_kernel,
        out_shape=(out, out),
        in_specs=[VMEM, VMEM, ANY],
        out_specs=(VMEM, VMEM),
        compiler_params=params(16),
        cost_estimate=cost(),
    )(keep, came, token)


def join_kernel(axis, one_ref, two_ref, token_ref, out_ref):
    del token_ref
    half = one_ref.shape[axis]
    if axis == 0:
        out_ref[:half], out_ref[half:] = one_ref[...], two_ref[...]
    else:
        out_ref[:, :half], out_ref[:, half:] = one_ref[...], two_ref[...]


def joined(one, two, token, axis):
    shape = list(one.shape)
    shape[axis] *= 2
    return pl.pallas_call(
        functools.partial(join_kernel, axis),
        out_shape=jax.ShapeDtypeStruct(tuple(shape), jnp.float32),
        in_specs=[VMEM, VMEM, ANY],
        out_specs=VMEM,
        compiler_params=params(24),
        cost_estimate=cost(),
    )(one, two, token)


def amplitude_kernel(turn, per_block, ours_ref, theirs_ref, state_ref, column_ref, row_ref, left_ref, right_ref, token_ref, out_ref):
    del token_ref
    half_count = per_block // 2
    rows = out_ref.shape[1]
    down = column_ref[pl.ds(pl.multiple_of(state_ref[1] * rows, rows), rows), :]
    theirs = theirs_ref[...].reshape(theirs_ref.shape[-2:])
    upper = upper_in(state_ref[0], turn)
    for h in range(half_count):
        low = ours_ref[0, h] + jnp.zeros((1, 1), jnp.float32)
        high = theirs[0:1, half_count + h : half_count + h + 1]
        wanted = ours_ref[0, per_block * (turn + 1) + h]
        for k in range(per_block):
            slot = ours_ref[0, per_block * (turn + 1) + k]
            high = high + jnp.where(slot == half_count + h, ours_ref[0, k], 0.0)
            low = low + jnp.where(wanted == k, 1.0, 0.0) * theirs[0:1, k : k + 1]
        gap = jnp.where(upper, high, low) - down - row_ref[...]
        out_ref[h] = (left_ref[h] + right_ref[h]) / gap


def amplitude(ours, theirs, theirs_spec, state, column, row, left, right, token, turn, per_block):
    return pl.pallas_call(
        functools.partial(amplitude_kernel, turn, per_block),
        out_shape=jax.ShapeDtypeStruct(left.shape, jnp.float32),
        grid=(1,),
        in_specs=[SMEM, theirs_spec, SMEM, VMEM, VMEM, VMEM, VMEM, ANY],
        out_specs=VMEM,
        compiler_params=params(16),
        cost_estimate=cost(),
    )(ours, theirs, state, column, row, left, right, token)


def tilde_kernel(blocks, places, state_ref, token_ref, *refs):
    del token_ref
    count = len(places)
    sources, (tall_ref, density_ref, amp, tilde) = refs[: 2 * count], refs[2 * count :]
    width = amp.shape[0]
    rows = width // blocks
    share = density_ref.shape[0]
    band = 128 if width % 128 == 0 else width
    for h in range(tall_ref.shape[1]):
        for who in range(2):
            offset = 0
            for part in range(count):
                first, order = places[part][who]
                source = sources[2 * part + who]
                size = source.shape[2]
                for place in range(blocks):
                    spot = pl.ds(pl.multiple_of((place ^ state_ref[order]) * rows, rows), rows)
                    amp[spot, offset : offset + size] = source[first + h, place * rows : (place + 1) * rows, :]
                offset += size
            for part in range(width // band):
                spot = slice(part * band, (part + 1) * band)
                straight, turned = amp[spot, :], amp[:, spot].T
                value = 2.0 * straight - turned if who == 0 else 2.0 * turned - straight
                if who == 0:
                    tilde[spot, :] = value
                below = slice(width + part * band, width + (part + 1) * band)
                tall_ref[who, h, spot, :], tall_ref[who, h, below, :] = halves(value)
            if who == 0:
                start = pl.ds(pl.multiple_of(state_ref[3] * share, share), share)
                straight = amp[start, :]
                turned = 2.0 * straight - tilde[start, :]
                both = (tall_ref[0, h, :width], tall_ref[0, h, width:])
                value = multiply(stacked(straight), both, ((1,), (1,)))
                value += multiply(stacked(turned), both, ((1,), (0,)))
                if h == 0:
                    density_ref[...] = value
                else:
                    density_ref[...] += value


def tildes(state, token, gathered, blocks, share, half_count):
    sources = [array for own, peer, _ in gathered for array in (own, peer)]
    places = [spots for _, _, spots in gathered]
    width = sources[0].shape[1]
    return pl.pallas_call(
        functools.partial(tilde_kernel, blocks, places),
        out_shape=(
            jax.ShapeDtypeStruct((2, half_count, 2 * width, width), jnp.bfloat16),
            jax.ShapeDtypeStruct((share, width), jnp.float32),
        ),
        in_specs=[SMEM, ANY] + [VMEM] * len(sources),
        out_specs=(VMEM, VMEM),
        scratch_shapes=[pltpu.VMEM((width, width), jnp.float32)] * 2,
        compiler_params=params(48),
        cost_estimate=cost(),
    )(state, token, *sources)


def gradient_kernel(count, based, columns, plan_ref, state_ref, tall_ref, token_ref, *refs):
    del plan_ref, state_ref, token_ref
    out_ref, done_ref = refs[-2:]
    done_ref[...] = jnp.zeros_like(done_ref)

    def term(offset, source):
        size = min(source.shape[1], tall_ref.shape[3] // (1 if columns else count))
        tilde = tall_ref[0, 0, :, offset : offset + size]
        return multiply(tilde, halves(source[0, :size]), ((1,), (0,)))

    if columns:
        for piece, source in enumerate(refs[:count]):

            @pl.when(pl.program_id(2) == piece)
            def _():
                out_ref[0] = refs[count][0] + term(0, source)

        return
    value = refs[count][0] if based else None
    for index, source in enumerate(refs[:count]):
        added = term(index * (tall_ref.shape[3] // count), source)
        value = added if value is None else value + added
    out_ref[0] = value


def gradient_terms(plan, state, token, tall, sources, base, turn, own, three_index):
    per_block, width, depth = three_index.shape
    half_count = per_block // 2
    columns = sources[0].shape[2] < depth
    tile = sources[0].shape[2] if columns else depth // 4 if depth % 512 == 0 else depth
    chosen = sources[0].shape[0] == per_block
    at = 0 if own else 1

    def block_at(h, _, piece, p, s):
        return (slot_of(p, s, per_block, turn, h, own), 0, piece)

    def source_at(h, _, piece, p, s):
        slot = peer_slot_of(p, s, per_block, turn, h, own) if chosen else h
        return (slot, 0, 0 if columns else piece)

    tilde_spec = pl.BlockSpec((1, 1, 2 * width, width), lambda h, *_: (at, h, 0, 0))
    out_spec = pl.BlockSpec((1, width, tile), block_at)
    return pl.pallas_call(
        functools.partial(gradient_kernel, len(sources), turn > 0, columns),
        out_shape=(
            jax.ShapeDtypeStruct((per_block, width, depth), jnp.float32),
            jax.ShapeDtypeStruct((8, 128), jnp.float32),
        ),
        grid_spec=pltpu.PrefetchScalarGridSpec(
            num_scalar_prefetch=2,
            grid=(half_count, 1, depth // tile),
            in_specs=[tilde_spec, ANY]
            + [pl.BlockSpec((1, x.shape[1], tile), source_at) for x in sources]
            + ([] if base is None else [out_spec] if turn > 0 else [ANY]),
            out_specs=(out_spec, pl.BlockSpec((8, 128), lambda *_: (0, 0))),
        ),
        input_output_aliases={} if base is None else {4 + len(sources): 0},
        compiler_params=params(44),
        cost_estimate=cost(),
    )(plan, state, tall, token, *sources, *(() if base is None else (base,)))


def chain(env, turn, offset, size, peers):
    bits, per_block, state = env["bits"], env["per_block"], env["state"]
    half_count = per_block // 2
    count = size // len(peers)
    token = yield None
    keep, give = integral(
        env["three_index"], peers, env["plan"], state, token, turn, env["blocks"], count
    )
    for stage in range(bits - 1):
        came = across(give, stage)
        token = yield give
        keep, give = parted(keep, came, token)
    came = across(give, bits - 1)
    token = yield give
    row = env["virtual"][None, offset : offset + size]
    theirs, spec = env["theirs"][turn]
    value = amplitude(
        env["ours"], theirs, spec, state, env["column"], row, keep, came, token, turn, per_block
    )
    if turn > 0:
        came = swapped(value, "pair", turn)
        token = yield value
        value = joined(value, came, token, 0)
    for stage in reversed(range(bits)):
        came = across(value, stage)
        token = yield value
        value = joined(value, came, token, 1)
    if turn == 0:
        came = swapped(value, "pair", 0)
        env["gathered"][turn].append((value, came, ((0, 1), (0, 2))))
    else:
        env["gathered"][turn].append((value, value, ((0, 1), (half_count, 1))))
    yield value


def body(three_index, occupied_energy, virtual_energy, plan):
    per_block, width, depth = three_index.shape
    half_count = per_block // 2
    aux_count = lax.axis_size("aux")
    bits = aux_count.bit_length() - 1
    blocks = aux_count
    row_count = width // aux_count
    aux = lax.axis_index("aux").astype(jnp.int32)
    rounds = plan.shape[0]
    position = lax.axis_index("pair").astype(jnp.int32)

    def mask(order):
        return sum((aux >> bit & 1) << bits - 1 - step for step, bit in enumerate(order))

    first_mask, second_mask = (mask(order) for order in orders(bits))
    core = position % 2
    state = jnp.stack(
        [
            position,
            jnp.where(core == 0, first_mask, second_mask),
            jnp.where(core == 0, second_mask, first_mask),
            aux,
        ]
    ).astype(jnp.int32)

    mine = jnp.concatenate([occupied_energy, plan.astype(jnp.float32).reshape(-1)])[None]
    extra = jnp.pad(mine, ((0, 7), (0, depth - mine.shape[1])))
    cuts, pieces = 2, 4
    step = width // cuts
    firsts = [None] * rounds
    theirs = [(swapped(mine, "pair", 0), VMEM)]
    token = virtual_energy
    for turn in range(1, rounds):
        firsts[turn] = []
        for cut in range(cuts):
            token = picked(
                three_index, plan, state, token, turn, False, cut, cuts, None if cut else extra
            )
            firsts[turn].append(swapped(token, "pair", turn))
        theirs.append((firsts[turn][0], pl.BlockSpec((1, 8, depth), lambda _: (0, step // 8, 0))))
    other = swapped(three_index, "pair", 0)
    firsts[0] = [other]
    env = {
        "bits": bits,
        "per_block": per_block,
        "blocks": blocks,
        "plan": plan,
        "state": state,
        "three_index": three_index,
        "virtual": virtual_energy,
        "column": virtual_energy[:, None],
        "ours": mine,
        "theirs": theirs,
        "gathered": [[] for _ in range(rounds)],
    }
    seconds = [[other]] + [[] for _ in range(1, rounds)]
    gradient = None
    tilde = [None] * rounds
    densities = []

    def gate_piece(turn, piece):
        return lambda token: gated(token, seconds[turn][piece])

    def send_piece(turn, piece):
        def run(token):
            token = picked(three_index, plan, state, token, turn, True, piece, pieces)
            seconds[turn].append(swapped(token, "pair", turn))
            return token

        return run

    def make_tilde(turn):
        def run(token):
            tilde[turn], density = tildes(
                state, token, env["gathered"][turn], blocks, row_count, half_count
            )
            densities.append(density)
            return density

        return run

    def add_terms(turn, own):
        def run(token):
            nonlocal gradient
            sources = firsts[turn] if own else seconds[turn]
            gradient, token = gradient_terms(
                plan, state, token, tilde[turn], sources, gradient, turn, own, three_index
            )
            return token

        return run

    tasks = []
    late = []
    tuned = bits == 3 and rounds == 2 and cuts == 2
    for turn in range(rounds):
        groups = [[first] for first in firsts[turn]]
        for cut, peers in enumerate(groups):
            clock = 42.0 + 36.0 * cut + 137.0 * (turn - 1) if turn else 11.0
            share = 1 / len(groups)
            worker = chain(env, turn, cut * step, width // len(groups), peers)
            next(worker)
            wide = 12.8 * share
            times = [clock, clock + 3 + 8 * share + wide]
            for stage in range(1, bits):
                times.append(times[-1] + 3 + (wide / 2 if stage == 1 else wide))
            if turn > 0:
                wide *= 2
                times.append(times[-1] + 7)
            for stage in range(bits):
                times.append(times[-1] + 3 + (wide / 2 if stage == 1 else wide))
            if tuned and turn > 0 and cut == cuts - 1:
                times = [70.0, 80.0, 87.0, 95.0, 101.5, 104.0, 120.0, 130.0]
            tasks += [(time, worker.send) for time in times]
            late.append(times)
    for turn in range(1, rounds):
        begin = 0.0 if tuned else 74.0 + 137.0 * (turn - 1)
        plain = ((0.0, 20.0), (17.0, 37.0), (34.0, 56.0), (51.0, 75.0))
        ordered = ((79.0, 94.5), (86.0, 101.2), (102.0, 119.7), (102.1, 129.0))
        for piece, (send, there) in enumerate(ordered if tuned else plain):
            tasks += [(begin + send, send_piece(turn, piece)), (begin + there, gate_piece(turn, piece))]
    for turn in range(rounds):
        steps = [make_tilde(turn), add_terms(turn, True), add_terms(turn, False)]
        if turn == 0 and rounds > 1:
            times = [119.5, 121.0, 122.0] if tuned else [time + 1 for time in late[cuts][-4:-1]]
            tasks += list(zip(times, steps))
        else:
            tasks += [(late[-1][-1] + 6 + index, step_) for index, step_ in enumerate(steps)]
    tasks.sort(key=lambda task: task[0])
    for _, task in tasks[:-1]:
        token = task(token)
    density = sum(densities)
    for bit in reversed(range(lax.axis_size("pair").bit_length() - 1)):
        half = density.shape[1] // 2
        side = position >> bit & 1
        give = lax.dynamic_slice_in_dim(density, (1 - side) * half, half, 1)
        came = swapped(give, "pair", bit)
        if tasks:
            came = passed(came, token)
            token = tasks.pop()[1](token)
            tasks = []
        density = lax.dynamic_slice_in_dim(density, side * half, half, 1) + came
    return (gradient, density)


def solution(mesh):
    in_specs = (P("pair", None, "aux"), P("pair"), P(), P(None, "pair"))
    out_specs = (P("pair", None, "aux"), P("aux", "pair"))
    return jax.shard_map(body, mesh=mesh, in_specs=in_specs, out_specs=out_specs, check_vma=False)
```

```python
import functools

import jax
import jax.numpy as jnp
from jax import lax
from jax.experimental import pallas as pl
from jax.experimental.pallas import tpu as pltpu
from jax.sharding import PartitionSpec as P

VMEM = pl.BlockSpec(memory_space=pltpu.VMEM)
SMEM = pl.BlockSpec(memory_space=pltpu.SMEM)
ANY = pl.BlockSpec(memory_space=pl.ANY)


def params(mebibytes):
    return pltpu.CompilerParams(vmem_limit_bytes=mebibytes * 2**20)


def cost():
    return pl.CostEstimate(flops=1, bytes_accessed=1, transcendentals=0)


def swapped(block, axis, bit):
    count = lax.axis_size(axis)
    route = []
    for low in range(count):
        high = low | 1 << bit
        if high != low and high < count:
            route += [(low, high), (high, low)]
    return lax.ppermute(block, axis, route)


def orders(bits):
    return (list(range(bits)), [1, 0] + list(range(2, bits)))


def across(block, step):
    pairs, auxes = lax.axis_size("pair"), lax.axis_size("aux")
    order = orders(auxes.bit_length() - 1)
    route = []
    for p in range(pairs):
        for m in range(auxes):
            route.append((p * auxes + m, p * auxes + (m ^ 1 << order[p % 2][step])))
    return lax.ppermute(block, ("pair", "aux"), route)


def halves(value):
    high = value.astype(jnp.bfloat16)
    return high, (value - high.astype(jnp.float32)).astype(jnp.bfloat16)


def multiply(left, right, dims):
    rh, rl = right
    one = functools.partial(
        lax.dot_general, dimension_numbers=(dims, ((), ())), preferred_element_type=jnp.float32
    )
    count = left.shape[0] // 2
    both = one(left, rh)
    return both[:count] + (both[count:] + one(left[:count], rl))


def stacked(value):
    return jnp.concatenate(halves(value), axis=0)


def upper_in(position, turn):
    return position // 2**turn % 2 == 1


def slot_of(plan_ref, state_ref, per_block, turn, h, own):
    half_count = per_block // 2
    plain = jnp.where(own, h, half_count + h)
    wanted = jnp.where(own, half_count + h, h)
    inverse = 0
    for k in range(per_block):
        inverse += jnp.where(plan_ref[turn, k] == wanted, k, 0)
    return jnp.where(upper_in(state_ref[0], turn), inverse, plain)


def peer_slot_of(plan_ref, state_ref, per_block, turn, h, own):
    half_count = per_block // 2
    plain = jnp.where(own, h, half_count + h)
    wanted = jnp.where(own, half_count + h, h)
    paired = 0
    for k in range(per_block):
        paired += jnp.where(plain == k, plan_ref[turn, k], 0)
    return jnp.where(upper_in(state_ref[0], turn), wanted, paired)


def copy_kernel(extra, plan_ref, state_ref, source_ref, *refs):
    del plan_ref, state_ref
    rows = source_ref.shape[1]
    refs[-1][:, :rows] = source_ref[...]
    if extra:
        refs[-1][:, rows:] = refs[0][...][None]


def picked(three_index, plan, state, token, turn, own, part, parts, extra=None):
    per_block, width, depth = three_index.shape
    half_count = per_block // 2
    rows = width if own else width // parts
    depth = depth // parts if own else depth
    count = rows + (0 if extra is None else extra.shape[0])

    def source(h, plan_ref, state_ref):
        slot = slot_of(plan_ref, state_ref, per_block, turn, h, own)
        return (slot, 0, part) if own else (slot, part, 0)

    return pl.pallas_call(
        functools.partial(copy_kernel, extra is not None),
        out_shape=jax.ShapeDtypeStruct((half_count, count, depth), jnp.float32),
        grid_spec=pltpu.PrefetchScalarGridSpec(
            num_scalar_prefetch=2,
            grid=(half_count,),
            in_specs=[pl.BlockSpec((1, rows, depth), source)]
            + ([] if extra is None else [VMEM])
            + [ANY],
            out_specs=pl.BlockSpec((1, count, depth), lambda h, *_: (h, 0, 0)),
        ),
        compiler_params=params(24),
        cost_estimate=cost(),
    )(plan, state, three_index, *(() if extra is None else (extra,)), token)


def gate_kernel(*refs):
    refs[-1][...] = jnp.zeros_like(refs[-1])


def gated(*tokens):
    return pl.pallas_call(
        gate_kernel,
        out_shape=jax.ShapeDtypeStruct((8, 128), jnp.float32),
        in_specs=[ANY] * len(tokens),
        out_specs=VMEM,
        compiler_params=params(16),
        cost_estimate=cost(),
    )(*tokens)


def pass_kernel(value_ref, token_ref, out_ref):
    del token_ref
    out_ref[...] = value_ref[...]


def passed(value, token):
    return pl.pallas_call(
        pass_kernel,
        out_shape=jax.ShapeDtypeStruct(value.shape, value.dtype),
        in_specs=[VMEM, ANY],
        out_specs=VMEM,
        compiler_params=params(16),
        cost_estimate=cost(),
    )(value, token)


def integral_kernel(turn, blocks, plan_ref, state_ref, own_ref, token_ref, *refs):
    del plan_ref, token_ref
    keep_ref, give_ref, high, low = refs[-4:]
    band = pl.program_id(1)
    count = high.shape[0] // (len(refs) - 4)

    @pl.when(band == 0)
    def _():
        for index, peer_ref in enumerate(refs[:-4]):
            spot = slice(index * count, (index + 1) * count)
            high[spot, :], low[spot, :] = halves(peer_ref[0, :count])

    value = multiply(stacked(own_ref[0]), (high[...], low[...]), ((1,), (1,)))
    rows = keep_ref.shape[1] * 2 // blocks
    inside = own_ref.shape[1] // rows
    for part in range(inside):
        place = (band * inside + part) ^ state_ref[1]
        piece = value[part * rows : (part + 1) * rows]

        @pl.when(place < blocks // 2)
        def _():
            keep_ref[0, pl.ds(pl.multiple_of(place * rows, rows), rows), :] = piece

        @pl.when(place >= blocks // 2)
        def _():
            spot = (place - blocks // 2) * rows
            give_ref[0, pl.ds(pl.multiple_of(spot, rows), rows), :] = piece


def integral(three_index, peers, plan, state, token, turn, blocks, count):
    per_block, width, depth = three_index.shape
    half_count = per_block // 2
    bands = 2
    out = jax.ShapeDtypeStruct((half_count, width // 2, count), jnp.float32)
    whole = pl.BlockSpec((1, width // 2, count), lambda h, band, *_: (h, 0, 0))
    chosen = peers[0].shape[0] == per_block

    def peer_at(h, band, p, s):
        return (peer_slot_of(p, s, per_block, turn, h, True) if chosen else h, 0, 0)

    return pl.pallas_call(
        functools.partial(integral_kernel, turn, blocks),
        out_shape=(out, out),
        grid_spec=pltpu.PrefetchScalarGridSpec(
            num_scalar_prefetch=2,
            grid=(half_count, bands),
            in_specs=[
                pl.BlockSpec(
                    (1, width // bands, depth),
                    lambda h, band, p, s: (slot_of(p, s, per_block, turn, h, True), band, 0),
                ),
                ANY,
            ]
            + [pl.BlockSpec((1, peer.shape[1], depth), peer_at) for peer in peers],
            out_specs=(whole, whole),
            scratch_shapes=[pltpu.VMEM((count, depth), jnp.bfloat16)] * 2,
        ),
        compiler_params=params(44),
        cost_estimate=cost(),
    )(plan, state, three_index, token, *peers)


def add_kernel(keep_ref, came_ref, token_ref, low_ref, high_ref):
    del token_ref
    half = low_ref.shape[1]
    low_ref[...] = keep_ref[:, :half] + came_ref[:, :half]
    high_ref[...] = keep_ref[:, half:] + came_ref[:, half:]


def parted(keep, came, token):
    out = jax.ShapeDtypeStruct((keep.shape[0], keep.shape[1] // 2, keep.shape[2]), jnp.float32)
    return pl.pallas_call(
        add_kernel,
        out_shape=(out, out),
        in_specs=[VMEM, VMEM, ANY],
        out_specs=(VMEM, VMEM),
        compiler_params=params(16),
        cost_estimate=cost(),
    )(keep, came, token)


def join_kernel(axis, one_ref, two_ref, token_ref, out_ref):
    del token_ref
    half = one_ref.shape[axis]
    if axis == 0:
        out_ref[:half], out_ref[half:] = one_ref[...], two_ref[...]
    else:
        out_ref[:, :half], out_ref[:, half:] = one_ref[...], two_ref[...]


def joined(one, two, token, axis):
    shape = list(one.shape)
    shape[axis] *= 2
    return pl.pallas_call(
        functools.partial(join_kernel, axis),
        out_shape=jax.ShapeDtypeStruct(tuple(shape), jnp.float32),
        in_specs=[VMEM, VMEM, ANY],
        out_specs=VMEM,
        compiler_params=params(24),
        cost_estimate=cost(),
    )(one, two, token)


def amplitude_kernel(turn, per_block, ours_ref, theirs_ref, state_ref, column_ref, row_ref, left_ref, right_ref, token_ref, out_ref):
    del token_ref
    half_count = per_block // 2
    rows = out_ref.shape[1]
    down = column_ref[pl.ds(pl.multiple_of(state_ref[1] * rows, rows), rows), :]
    theirs = theirs_ref[...].reshape(theirs_ref.shape[-2:])
    upper = upper_in(state_ref[0], turn)
    for h in range(half_count):
        low = ours_ref[0, h] + jnp.zeros((1, 1), jnp.float32)
        high = theirs[0:1, half_count + h : half_count + h + 1]
        wanted = ours_ref[0, per_block * (turn + 1) + h]
        for k in range(per_block):
            slot = ours_ref[0, per_block * (turn + 1) + k]
            high = high + jnp.where(slot == half_count + h, ours_ref[0, k], 0.0)
            low = low + jnp.where(wanted == k, 1.0, 0.0) * theirs[0:1, k : k + 1]
        gap = jnp.where(upper, high, low) - down - row_ref[...]
        out_ref[h] = (left_ref[h] + right_ref[h]) / gap


def amplitude(ours, theirs, theirs_spec, state, column, row, left, right, token, turn, per_block):
    return pl.pallas_call(
        functools.partial(amplitude_kernel, turn, per_block),
        out_shape=jax.ShapeDtypeStruct(left.shape, jnp.float32),
        grid=(1,),
        in_specs=[SMEM, theirs_spec, SMEM, VMEM, VMEM, VMEM, VMEM, ANY],
        out_specs=VMEM,
        compiler_params=params(16),
        cost_estimate=cost(),
    )(ours, theirs, state, column, row, left, right, token)


def tilde_kernel(blocks, places, state_ref, token_ref, *refs):
    del token_ref
    count = len(places)
    sources, (tall_ref, density_ref, amp, tilde) = refs[: 2 * count], refs[2 * count :]
    width = amp.shape[0]
    rows = width // blocks
    share = density_ref.shape[0]
    band = 128 if width % 128 == 0 else width
    for h in range(tall_ref.shape[1]):
        for who in range(2):
            offset = 0
            for part in range(count):
                first, order = places[part][who]
                source = sources[2 * part + who]
                size = source.shape[2]
                for place in range(blocks):
                    spot = pl.ds(pl.multiple_of((place ^ state_ref[order]) * rows, rows), rows)
                    amp[spot, offset : offset + size] = source[first + h, place * rows : (place + 1) * rows, :]
                offset += size
            for part in range(width // band):
                spot = slice(part * band, (part + 1) * band)
                straight, turned = amp[spot, :], amp[:, spot].T
                value = 2.0 * straight - turned if who == 0 else 2.0 * turned - straight
                if who == 0:
                    tilde[spot, :] = value
                below = slice(width + part * band, width + (part + 1) * band)
                tall_ref[who, h, spot, :], tall_ref[who, h, below, :] = halves(value)
            if who == 0:
                start = pl.ds(pl.multiple_of(state_ref[3] * share, share), share)
                straight = amp[start, :]
                turned = 2.0 * straight - tilde[start, :]
                both = (tall_ref[0, h, :width], tall_ref[0, h, width:])
                value = multiply(stacked(straight), both, ((1,), (1,)))
                value += multiply(stacked(turned), both, ((1,), (0,)))
                if h == 0:
                    density_ref[...] = value
                else:
                    density_ref[...] += value


def tildes(state, token, gathered, blocks, share, half_count):
    sources = [array for own, peer, _ in gathered for array in (own, peer)]
    places = [spots for _, _, spots in gathered]
    width = sources[0].shape[1]
    return pl.pallas_call(
        functools.partial(tilde_kernel, blocks, places),
        out_shape=(
            jax.ShapeDtypeStruct((2, half_count, 2 * width, width), jnp.bfloat16),
            jax.ShapeDtypeStruct((share, width), jnp.float32),
        ),
        in_specs=[SMEM, ANY] + [VMEM] * len(sources),
        out_specs=(VMEM, VMEM),
        scratch_shapes=[pltpu.VMEM((width, width), jnp.float32)] * 2,
        compiler_params=params(48),
        cost_estimate=cost(),
    )(state, token, *sources)


def gradient_kernel(count, based, columns, plan_ref, state_ref, tall_ref, token_ref, *refs):
    del plan_ref, state_ref, token_ref
    out_ref, done_ref = refs[-2:]
    done_ref[...] = jnp.zeros_like(done_ref)

    def term(offset, source):
        size = min(source.shape[1], tall_ref.shape[3] // (1 if columns else count))
        tilde = tall_ref[0, 0, :, offset : offset + size]
        return multiply(tilde, halves(source[0, :size]), ((1,), (0,)))

    if columns:
        for piece, source in enumerate(refs[:count]):

            @pl.when(pl.program_id(2) == piece)
            def _():
                out_ref[0] = refs[count][0] + term(0, source)

        return
    value = refs[count][0] if based else None
    for index, source in enumerate(refs[:count]):
        added = term(index * (tall_ref.shape[3] // count), source)
        value = added if value is None else value + added
    out_ref[0] = value


def gradient_terms(plan, state, token, tall, sources, base, turn, own, three_index):
    per_block, width, depth = three_index.shape
    half_count = per_block // 2
    columns = sources[0].shape[2] < depth
    tile = sources[0].shape[2] if columns else depth // 4 if depth % 512 == 0 else depth
    chosen = sources[0].shape[0] == per_block
    at = 0 if own else 1

    def block_at(h, _, piece, p, s):
        return (slot_of(p, s, per_block, turn, h, own), 0, piece)

    def source_at(h, _, piece, p, s):
        slot = peer_slot_of(p, s, per_block, turn, h, own) if chosen else h
        return (slot, 0, 0 if columns else piece)

    tilde_spec = pl.BlockSpec((1, 1, 2 * width, width), lambda h, *_: (at, h, 0, 0))
    out_spec = pl.BlockSpec((1, width, tile), block_at)
    return pl.pallas_call(
        functools.partial(gradient_kernel, len(sources), turn > 0, columns),
        out_shape=(
            jax.ShapeDtypeStruct((per_block, width, depth), jnp.float32),
            jax.ShapeDtypeStruct((8, 128), jnp.float32),
        ),
        grid_spec=pltpu.PrefetchScalarGridSpec(
            num_scalar_prefetch=2,
            grid=(half_count, 1, depth // tile),
            in_specs=[tilde_spec, ANY]
            + [pl.BlockSpec((1, x.shape[1], tile), source_at) for x in sources]
            + ([] if base is None else [out_spec] if turn > 0 else [ANY]),
            out_specs=(out_spec, pl.BlockSpec((8, 128), lambda *_: (0, 0))),
        ),
        input_output_aliases={} if base is None else {4 + len(sources): 0},
        compiler_params=params(44),
        cost_estimate=cost(),
    )(plan, state, tall, token, *sources, *(() if base is None else (base,)))


def chain(env, turn, offset, size, peers):
    bits, per_block, state = env["bits"], env["per_block"], env["state"]
    half_count = per_block // 2
    count = size // len(peers)
    token = yield None
    keep, give = integral(
        env["three_index"], peers, env["plan"], state, token, turn, env["blocks"], count
    )
    for stage in range(bits - 1):
        came = across(give, stage)
        token = yield give
        keep, give = parted(keep, came, token)
    came = across(give, bits - 1)
    token = yield give
    row = env["virtual"][None, offset : offset + size]
    theirs, spec = env["theirs"][turn]
    value = amplitude(
        env["ours"], theirs, spec, state, env["column"], row, keep, came, token, turn, per_block
    )
    if turn > 0:
        came = swapped(value, "pair", turn)
        token = yield value
        value = joined(value, came, token, 0)
    for stage in reversed(range(bits)):
        came = across(value, stage)
        token = yield value
        value = joined(value, came, token, 1)
    if turn == 0:
        came = swapped(value, "pair", 0)
        env["gathered"][turn].append((value, came, ((0, 1), (0, 2))))
    else:
        env["gathered"][turn].append((value, value, ((0, 1), (half_count, 1))))
    yield value


def body(three_index, occupied_energy, virtual_energy, plan):
    per_block, width, depth = three_index.shape
    half_count = per_block // 2
    aux_count = lax.axis_size("aux")
    bits = aux_count.bit_length() - 1
    blocks = aux_count
    row_count = width // aux_count
    aux = lax.axis_index("aux").astype(jnp.int32)
    rounds = plan.shape[0]
    position = lax.axis_index("pair").astype(jnp.int32)

    def mask(order):
        return sum((aux >> bit & 1) << bits - 1 - step for step, bit in enumerate(order))

    first_mask, second_mask = (mask(order) for order in orders(bits))
    core = position % 2
    state = jnp.stack(
        [
            position,
            jnp.where(core == 0, first_mask, second_mask),
            jnp.where(core == 0, second_mask, first_mask),
            aux,
        ]
    ).astype(jnp.int32)

    mine = jnp.concatenate([occupied_energy, plan.astype(jnp.float32).reshape(-1)])[None]
    extra = jnp.pad(mine, ((0, 7), (0, depth - mine.shape[1])))
    cuts, pieces = 2, 4
    step = width // cuts
    firsts = [None] * rounds
    theirs = [(swapped(mine, "pair", 0), VMEM)]
    token = virtual_energy
    for turn in range(1, rounds):
        firsts[turn] = []
        for cut in range(cuts):
            token = picked(
                three_index, plan, state, token, turn, False, cut, cuts, None if cut else extra
            )
            firsts[turn].append(swapped(token, "pair", turn))
        theirs.append((firsts[turn][0], pl.BlockSpec((1, 8, depth), lambda _: (0, step // 8, 0))))
    other = swapped(three_index, "pair", 0)
    firsts[0] = [other]
    env = {
        "bits": bits,
        "per_block": per_block,
        "blocks": blocks,
        "plan": plan,
        "state": state,
        "three_index": three_index,
        "virtual": virtual_energy,
        "column": virtual_energy[:, None],
        "ours": mine,
        "theirs": theirs,
        "gathered": [[] for _ in range(rounds)],
    }
    seconds = [[other]] + [[] for _ in range(1, rounds)]
    gradient = None
    tilde = [None] * rounds
    densities = []

    def gate_piece(turn, piece):
        return lambda token: gated(token, seconds[turn][piece])

    def send_piece(turn, piece):
        def run(token):
            token = picked(three_index, plan, state, token, turn, True, piece, pieces)
            seconds[turn].append(swapped(token, "pair", turn))
            return token

        return run

    def make_tilde(turn):
        def run(token):
            tilde[turn], density = tildes(
                state, token, env["gathered"][turn], blocks, row_count, half_count
            )
            densities.append(density)
            return density

        return run

    def add_terms(turn, own):
        def run(token):
            nonlocal gradient
            sources = firsts[turn] if own else seconds[turn]
            gradient, token = gradient_terms(
                plan, state, token, tilde[turn], sources, gradient, turn, own, three_index
            )
            return token

        return run

    tasks = []
    late = []
    tuned = bits == 3 and rounds == 2 and cuts == 2
    for turn in range(rounds):
        groups = [[first] for first in firsts[turn]]
        for cut, peers in enumerate(groups):
            clock = 42.0 + 36.0 * cut + 137.0 * (turn - 1) if turn else 11.0
            share = 1 / len(groups)
            worker = chain(env, turn, cut * step, width // len(groups), peers)
            next(worker)
            wide = 12.8 * share
            times = [clock, clock + 3 + 8 * share + wide]
            for stage in range(1, bits):
                times.append(times[-1] + 3 + (wide / 2 if stage == 1 else wide))
            if turn > 0:
                wide *= 2
                times.append(times[-1] + 7)
            for stage in range(bits):
                times.append(times[-1] + 3 + (wide / 2 if stage == 1 else wide))
            if tuned and turn > 0 and cut == cuts - 1:
                times = [70.0, 80.0, 84.0, 95.0, 101.5, 104.0, 120.0, 130.0]
            elif tuned and turn == 0:
                times[-1] = 104.2
            elif tuned:
                times[-1] = 120.2
            tasks += [(time, worker.send) for time in times]
            late.append(times)
    for turn in range(1, rounds):
        begin = 0.0 if tuned else 74.0 + 137.0 * (turn - 1)
        plain = ((0.0, 20.0), (17.0, 37.0), (34.0, 56.0), (51.0, 75.0))
        ordered = ((79.0, 101.1), (102.0, 119.7), (104.5, 129.0), (120.5, 136.5))
        for piece, (send, there) in enumerate(ordered if tuned else plain):
            tasks += [(begin + send, send_piece(turn, piece)), (begin + there, gate_piece(turn, piece))]
    for turn in range(rounds):
        steps = [make_tilde(turn), add_terms(turn, True), add_terms(turn, False)]
        if turn == 0 and rounds > 1:
            times = [119.5, 121.0, 122.0] if tuned else [time + 1 for time in late[cuts][-4:-1]]
            tasks += list(zip(times, steps))
        else:
            tasks += [(late[-1][-1] + 6 + index, step_) for index, step_ in enumerate(steps)]
    tasks.sort(key=lambda task: task[0])
    for _, task in tasks[:-1]:
        token = task(token)
    density = sum(densities)
    for bit in reversed(range(lax.axis_size("pair").bit_length() - 1)):
        half = density.shape[1] // 2
        side = position >> bit & 1
        give = lax.dynamic_slice_in_dim(density, (1 - side) * half, half, 1)
        came = swapped(give, "pair", bit)
        if tasks:
            came = passed(came, token)
            token = tasks.pop()[1](token)
            tasks = []
        density = lax.dynamic_slice_in_dim(density, side * half, half, 1) + came
    return (gradient, density)


def solution(mesh):
    in_specs = (P("pair", None, "aux"), P("pair"), P(), P(None, "pair"))
    out_specs = (P("pair", None, "aux"), P("aux", "pair"))
    return jax.shard_map(body, mesh=mesh, in_specs=in_specs, out_specs=out_specs, check_vma=False)
```

```python
import functools

import jax
import jax.numpy as jnp
from jax import lax
from jax.experimental import pallas as pl
from jax.experimental.pallas import tpu as pltpu
from jax.sharding import PartitionSpec as P

VMEM = pl.BlockSpec(memory_space=pltpu.VMEM)
SMEM = pl.BlockSpec(memory_space=pltpu.SMEM)
ANY = pl.BlockSpec(memory_space=pl.ANY)


def params(mebibytes):
    return pltpu.CompilerParams(vmem_limit_bytes=mebibytes * 2**20)


def cost():
    return pl.CostEstimate(flops=1, bytes_accessed=1, transcendentals=0)


def swapped(block, axis, bit):
    count = lax.axis_size(axis)
    route = []
    for low in range(count):
        high = low | 1 << bit
        if high != low and high < count:
            route += [(low, high), (high, low)]
    return lax.ppermute(block, axis, route)


def orders(bits):
    return (list(range(bits)), [1, 0] + list(range(2, bits)))


def across(block, step):
    pairs, auxes = lax.axis_size("pair"), lax.axis_size("aux")
    order = orders(auxes.bit_length() - 1)
    route = []
    for p in range(pairs):
        for m in range(auxes):
            route.append((p * auxes + m, p * auxes + (m ^ 1 << order[p % 2][step])))
    return lax.ppermute(block, ("pair", "aux"), route)


def halves(value):
    high = value.astype(jnp.bfloat16)
    return high, (value - high.astype(jnp.float32)).astype(jnp.bfloat16)


def multiply(left, right, dims):
    rh, rl = right
    one = functools.partial(
        lax.dot_general, dimension_numbers=(dims, ((), ())), preferred_element_type=jnp.float32
    )
    count = left.shape[0] // 2
    both = one(left, rh)
    return both[:count] + (both[count:] + one(left[:count], rl))


def stacked(value):
    return jnp.concatenate(halves(value), axis=0)


def upper_in(position, turn):
    return position // 2**turn % 2 == 1


def slot_of(plan_ref, state_ref, per_block, turn, h, own):
    half_count = per_block // 2
    plain = jnp.where(own, h, half_count + h)
    wanted = jnp.where(own, half_count + h, h)
    inverse = 0
    for k in range(per_block):
        inverse += jnp.where(plan_ref[turn, k] == wanted, k, 0)
    return jnp.where(upper_in(state_ref[0], turn), inverse, plain)


def peer_slot_of(plan_ref, state_ref, per_block, turn, h, own):
    half_count = per_block // 2
    plain = jnp.where(own, h, half_count + h)
    wanted = jnp.where(own, half_count + h, h)
    paired = 0
    for k in range(per_block):
        paired += jnp.where(plain == k, plan_ref[turn, k], 0)
    return jnp.where(upper_in(state_ref[0], turn), wanted, paired)


def copy_kernel(extra, plan_ref, state_ref, source_ref, *refs):
    del plan_ref, state_ref
    rows = source_ref.shape[1]
    refs[-1][:, :rows] = source_ref[...]
    if extra:
        refs[-1][:, rows:] = refs[0][...][None]


def picked(three_index, plan, state, token, turn, own, part, parts, extra=None):
    per_block, width, depth = three_index.shape
    half_count = per_block // 2
    rows = width if own else width // parts
    depth = depth // parts if own else depth
    count = rows + (0 if extra is None else extra.shape[0])

    def source(h, plan_ref, state_ref):
        slot = slot_of(plan_ref, state_ref, per_block, turn, h, own)
        return (slot, 0, part) if own else (slot, part, 0)

    return pl.pallas_call(
        functools.partial(copy_kernel, extra is not None),
        out_shape=jax.ShapeDtypeStruct((half_count, count, depth), jnp.float32),
        grid_spec=pltpu.PrefetchScalarGridSpec(
            num_scalar_prefetch=2,
            grid=(half_count,),
            in_specs=[pl.BlockSpec((1, rows, depth), source)]
            + ([] if extra is None else [VMEM])
            + [ANY],
            out_specs=pl.BlockSpec((1, count, depth), lambda h, *_: (h, 0, 0)),
        ),
        compiler_params=params(24),
        cost_estimate=cost(),
    )(plan, state, three_index, *(() if extra is None else (extra,)), token)


def gate_kernel(*refs):
    refs[-1][...] = jnp.zeros_like(refs[-1])


def gated(*tokens):
    return pl.pallas_call(
        gate_kernel,
        out_shape=jax.ShapeDtypeStruct((8, 128), jnp.float32),
        in_specs=[ANY] * len(tokens),
        out_specs=VMEM,
        compiler_params=params(16),
        cost_estimate=cost(),
    )(*tokens)


def pass_kernel(value_ref, token_ref, out_ref):
    del token_ref
    out_ref[...] = value_ref[...]


def passed(value, token):
    return pl.pallas_call(
        pass_kernel,
        out_shape=jax.ShapeDtypeStruct(value.shape, value.dtype),
        in_specs=[VMEM, ANY],
        out_specs=VMEM,
        compiler_params=params(16),
        cost_estimate=cost(),
    )(value, token)


def integral_kernel(turn, blocks, plan_ref, state_ref, own_ref, token_ref, *refs):
    del plan_ref, token_ref
    keep_ref, give_ref, high, low = refs[-4:]
    band = pl.program_id(1)
    count = high.shape[0] // (len(refs) - 4)

    @pl.when(band == 0)
    def _():
        for index, peer_ref in enumerate(refs[:-4]):
            spot = slice(index * count, (index + 1) * count)
            high[spot, :], low[spot, :] = halves(peer_ref[0, :count])

    value = multiply(stacked(own_ref[0]), (high[...], low[...]), ((1,), (1,)))
    rows = keep_ref.shape[1] * 2 // blocks
    inside = own_ref.shape[1] // rows
    for part in range(inside):
        place = (band * inside + part) ^ state_ref[1]
        piece = value[part * rows : (part + 1) * rows]

        @pl.when(place < blocks // 2)
        def _():
            keep_ref[0, pl.ds(pl.multiple_of(place * rows, rows), rows), :] = piece

        @pl.when(place >= blocks // 2)
        def _():
            spot = (place - blocks // 2) * rows
            give_ref[0, pl.ds(pl.multiple_of(spot, rows), rows), :] = piece


def integral(three_index, peers, plan, state, token, turn, blocks, count):
    per_block, width, depth = three_index.shape
    half_count = per_block // 2
    bands = 2
    out = jax.ShapeDtypeStruct((half_count, width // 2, count), jnp.float32)
    whole = pl.BlockSpec((1, width // 2, count), lambda h, band, *_: (h, 0, 0))
    chosen = peers[0].shape[0] == per_block

    def peer_at(h, band, p, s):
        return (peer_slot_of(p, s, per_block, turn, h, True) if chosen else h, 0, 0)

    return pl.pallas_call(
        functools.partial(integral_kernel, turn, blocks),
        out_shape=(out, out),
        grid_spec=pltpu.PrefetchScalarGridSpec(
            num_scalar_prefetch=2,
            grid=(half_count, bands),
            in_specs=[
                pl.BlockSpec(
                    (1, width // bands, depth),
                    lambda h, band, p, s: (slot_of(p, s, per_block, turn, h, True), band, 0),
                ),
                ANY,
            ]
            + [pl.BlockSpec((1, peer.shape[1], depth), peer_at) for peer in peers],
            out_specs=(whole, whole),
            scratch_shapes=[pltpu.VMEM((count, depth), jnp.bfloat16)] * 2,
        ),
        compiler_params=params(44),
        cost_estimate=cost(),
    )(plan, state, three_index, token, *peers)


def add_kernel(keep_ref, came_ref, token_ref, low_ref, high_ref):
    del token_ref
    half = low_ref.shape[1]
    low_ref[...] = keep_ref[:, :half] + came_ref[:, :half]
    high_ref[...] = keep_ref[:, half:] + came_ref[:, half:]


def parted(keep, came, token):
    out = jax.ShapeDtypeStruct((keep.shape[0], keep.shape[1] // 2, keep.shape[2]), jnp.float32)
    return pl.pallas_call(
        add_kernel,
        out_shape=(out, out),
        in_specs=[VMEM, VMEM, ANY],
        out_specs=(VMEM, VMEM),
        compiler_params=params(16),
        cost_estimate=cost(),
    )(keep, came, token)


def join_kernel(axis, one_ref, two_ref, token_ref, out_ref):
    del token_ref
    half = one_ref.shape[axis]
    if axis == 0:
        out_ref[:half], out_ref[half:] = one_ref[...], two_ref[...]
    else:
        out_ref[:, :half], out_ref[:, half:] = one_ref[...], two_ref[...]


def joined(one, two, token, axis):
    shape = list(one.shape)
    shape[axis] *= 2
    return pl.pallas_call(
        functools.partial(join_kernel, axis),
        out_shape=jax.ShapeDtypeStruct(tuple(shape), jnp.float32),
        in_specs=[VMEM, VMEM, ANY],
        out_specs=VMEM,
        compiler_params=params(24),
        cost_estimate=cost(),
    )(one, two, token)


def amplitude_kernel(turn, per_block, ours_ref, theirs_ref, state_ref, column_ref, row_ref, left_ref, right_ref, token_ref, out_ref):
    del token_ref
    half_count = per_block // 2
    rows = out_ref.shape[1]
    down = column_ref[pl.ds(pl.multiple_of(state_ref[1] * rows, rows), rows), :]
    theirs = theirs_ref[...].reshape(theirs_ref.shape[-2:])
    upper = upper_in(state_ref[0], turn)
    for h in range(half_count):
        low = ours_ref[0, h] + jnp.zeros((1, 1), jnp.float32)
        high = theirs[0:1, half_count + h : half_count + h + 1]
        wanted = ours_ref[0, per_block * (turn + 1) + h]
        for k in range(per_block):
            slot = ours_ref[0, per_block * (turn + 1) + k]
            high = high + jnp.where(slot == half_count + h, ours_ref[0, k], 0.0)
            low = low + jnp.where(wanted == k, 1.0, 0.0) * theirs[0:1, k : k + 1]
        gap = jnp.where(upper, high, low) - down - row_ref[...]
        out_ref[h] = (left_ref[h] + right_ref[h]) / gap


def amplitude(ours, theirs, theirs_spec, state, column, row, left, right, token, turn, per_block):
    return pl.pallas_call(
        functools.partial(amplitude_kernel, turn, per_block),
        out_shape=jax.ShapeDtypeStruct(left.shape, jnp.float32),
        grid=(1,),
        in_specs=[SMEM, theirs_spec, SMEM, VMEM, VMEM, VMEM, VMEM, ANY],
        out_specs=VMEM,
        compiler_params=params(16),
        cost_estimate=cost(),
    )(ours, theirs, state, column, row, left, right, token)


def tilde_kernel(blocks, places, state_ref, token_ref, *refs):
    del token_ref
    count = len(places)
    sources, (tall_ref, density_ref, amp, tilde) = refs[: 2 * count], refs[2 * count :]
    width = amp.shape[0]
    rows = width // blocks
    share = density_ref.shape[0]
    band = 128 if width % 128 == 0 else width
    for h in range(tall_ref.shape[1]):
        for who in range(2):
            offset = 0
            for part in range(count):
                first, order = places[part][who]
                source = sources[2 * part + who]
                size = source.shape[2]
                for place in range(blocks):
                    spot = pl.ds(pl.multiple_of((place ^ state_ref[order]) * rows, rows), rows)
                    amp[spot, offset : offset + size] = source[first + h, place * rows : (place + 1) * rows, :]
                offset += size
            for part in range(width // band):
                spot = slice(part * band, (part + 1) * band)
                straight, turned = amp[spot, :], amp[:, spot].T
                value = 2.0 * straight - turned if who == 0 else 2.0 * turned - straight
                if who == 0:
                    tilde[spot, :] = value
                below = slice(width + part * band, width + (part + 1) * band)
                tall_ref[who, h, spot, :], tall_ref[who, h, below, :] = halves(value)
            if who == 0:
                start = pl.ds(pl.multiple_of(state_ref[3] * share, share), share)
                straight = amp[start, :]
                turned = 2.0 * straight - tilde[start, :]
                both = (tall_ref[0, h, :width], tall_ref[0, h, width:])
                value = multiply(stacked(straight), both, ((1,), (1,)))
                value += multiply(stacked(turned), both, ((1,), (0,)))
                if h == 0:
                    density_ref[...] = value
                else:
                    density_ref[...] += value


def tildes(state, token, gathered, blocks, share, half_count):
    sources = [array for own, peer, _ in gathered for array in (own, peer)]
    places = [spots for _, _, spots in gathered]
    width = sources[0].shape[1]
    return pl.pallas_call(
        functools.partial(tilde_kernel, blocks, places),
        out_shape=(
            jax.ShapeDtypeStruct((2, half_count, 2 * width, width), jnp.bfloat16),
            jax.ShapeDtypeStruct((share, width), jnp.float32),
        ),
        in_specs=[SMEM, ANY] + [VMEM] * len(sources),
        out_specs=(VMEM, VMEM),
        scratch_shapes=[pltpu.VMEM((width, width), jnp.float32)] * 2,
        compiler_params=params(48),
        cost_estimate=cost(),
    )(state, token, *sources)


def gradient_kernel(count, based, columns, plan_ref, state_ref, tall_ref, token_ref, *refs):
    del plan_ref, state_ref, token_ref
    out_ref, done_ref = refs[-2:]
    done_ref[...] = jnp.zeros_like(done_ref)

    def term(offset, source):
        size = min(source.shape[1], tall_ref.shape[3] // (1 if columns else count))
        tilde = tall_ref[0, 0, :, offset : offset + size]
        return multiply(tilde, halves(source[0, :size]), ((1,), (0,)))

    if columns:
        for piece, source in enumerate(refs[:count]):

            @pl.when(pl.program_id(2) == piece)
            def _():
                out_ref[0] = refs[count][0] + term(0, source)

        return
    value = refs[count][0] if based else None
    for index, source in enumerate(refs[:count]):
        added = term(index * (tall_ref.shape[3] // count), source)
        value = added if value is None else value + added
    out_ref[0] = value


def gradient_terms(plan, state, token, tall, sources, base, turn, own, three_index):
    per_block, width, depth = three_index.shape
    half_count = per_block // 2
    columns = sources[0].shape[2] < depth
    tile = sources[0].shape[2] if columns else depth // 4 if depth % 512 == 0 else depth
    chosen = sources[0].shape[0] == per_block
    at = 0 if own else 1

    def block_at(h, _, piece, p, s):
        return (slot_of(p, s, per_block, turn, h, own), 0, piece)

    def source_at(h, _, piece, p, s):
        slot = peer_slot_of(p, s, per_block, turn, h, own) if chosen else h
        return (slot, 0, 0 if columns else piece)

    tilde_spec = pl.BlockSpec((1, 1, 2 * width, width), lambda h, *_: (at, h, 0, 0))
    out_spec = pl.BlockSpec((1, width, tile), block_at)
    return pl.pallas_call(
        functools.partial(gradient_kernel, len(sources), turn > 0, columns),
        out_shape=(
            jax.ShapeDtypeStruct((per_block, width, depth), jnp.float32),
            jax.ShapeDtypeStruct((8, 128), jnp.float32),
        ),
        grid_spec=pltpu.PrefetchScalarGridSpec(
            num_scalar_prefetch=2,
            grid=(half_count, 1, depth // tile),
            in_specs=[tilde_spec, ANY]
            + [pl.BlockSpec((1, x.shape[1], tile), source_at) for x in sources]
            + ([] if base is None else [out_spec] if turn > 0 else [ANY]),
            out_specs=(out_spec, pl.BlockSpec((8, 128), lambda *_: (0, 0))),
        ),
        input_output_aliases={} if base is None else {4 + len(sources): 0},
        compiler_params=params(44),
        cost_estimate=cost(),
    )(plan, state, tall, token, *sources, *(() if base is None else (base,)))


def chain(env, turn, offset, size, peers):
    bits, per_block, state = env["bits"], env["per_block"], env["state"]
    half_count = per_block // 2
    count = size // len(peers)
    token = yield None
    keep, give = integral(
        env["three_index"], peers, env["plan"], state, token, turn, env["blocks"], count
    )
    for stage in range(bits - 1):
        came = across(give, stage)
        token = yield give
        keep, give = parted(keep, came, token)
    came = across(give, bits - 1)
    token = yield give
    row = env["virtual"][None, offset : offset + size]
    theirs, spec = env["theirs"][turn]
    value = amplitude(
        env["ours"], theirs, spec, state, env["column"], row, keep, came, token, turn, per_block
    )
    if turn > 0:
        came = swapped(value, "pair", turn)
        token = yield value
        value = joined(value, came, token, 0)
    for stage in reversed(range(bits)):
        came = across(value, stage)
        token = yield value
        value = joined(value, came, token, 1)
    if turn == 0:
        came = swapped(value, "pair", 0)
        env["gathered"][turn].append((value, came, ((0, 1), (0, 2))))
    else:
        env["gathered"][turn].append((value, value, ((0, 1), (half_count, 1))))
    yield value


def body(three_index, occupied_energy, virtual_energy, plan):
    per_block, width, depth = three_index.shape
    half_count = per_block // 2
    aux_count = lax.axis_size("aux")
    bits = aux_count.bit_length() - 1
    blocks = aux_count
    row_count = width // aux_count
    aux = lax.axis_index("aux").astype(jnp.int32)
    rounds = plan.shape[0]
    position = lax.axis_index("pair").astype(jnp.int32)

    def mask(order):
        return sum((aux >> bit & 1) << bits - 1 - step for step, bit in enumerate(order))

    first_mask, second_mask = (mask(order) for order in orders(bits))
    core = position % 2
    state = jnp.stack(
        [
            position,
            jnp.where(core == 0, first_mask, second_mask),
            jnp.where(core == 0, second_mask, first_mask),
            aux,
        ]
    ).astype(jnp.int32)

    mine = jnp.concatenate([occupied_energy, plan.astype(jnp.float32).reshape(-1)])[None]
    extra = jnp.pad(mine, ((0, 7), (0, depth - mine.shape[1])))
    cuts, pieces = 2, 4
    step = width // cuts
    firsts = [None] * rounds
    theirs = [(swapped(mine, "pair", 0), VMEM)]
    token = virtual_energy
    for turn in range(1, rounds):
        firsts[turn] = []
        for cut in range(cuts):
            token = picked(
                three_index, plan, state, token, turn, False, cut, cuts, None if cut else extra
            )
            firsts[turn].append(swapped(token, "pair", turn))
        theirs.append((firsts[turn][0], pl.BlockSpec((1, 8, depth), lambda _: (0, step // 8, 0))))
    other = swapped(three_index, "pair", 0)
    firsts[0] = [other]
    env = {
        "bits": bits,
        "per_block": per_block,
        "blocks": blocks,
        "plan": plan,
        "state": state,
        "three_index": three_index,
        "virtual": virtual_energy,
        "column": virtual_energy[:, None],
        "ours": mine,
        "theirs": theirs,
        "gathered": [[] for _ in range(rounds)],
    }
    seconds = [[other]] + [[] for _ in range(1, rounds)]
    gradient = None
    tilde = [None] * rounds
    densities = []

    def gate_piece(turn, piece):
        return lambda token: gated(token, seconds[turn][piece])

    def send_piece(turn, piece):
        def run(token):
            token = picked(three_index, plan, state, token, turn, True, piece, pieces)
            seconds[turn].append(swapped(token, "pair", turn))
            return token

        return run

    def make_tilde(turn):
        def run(token):
            tilde[turn], density = tildes(
                state, token, env["gathered"][turn], blocks, row_count, half_count
            )
            densities.append(density)
            return density

        return run

    def add_terms(turn, own):
        def run(token):
            nonlocal gradient
            sources = firsts[turn] if own else seconds[turn]
            gradient, token = gradient_terms(
                plan, state, token, tilde[turn], sources, gradient, turn, own, three_index
            )
            return token

        return run

    tasks = []
    late = []
    tuned = bits == 3 and rounds == 2 and cuts == 2
    for turn in range(rounds):
        groups = [[first] for first in firsts[turn]]
        for cut, peers in enumerate(groups):
            clock = 42.0 + 36.0 * cut + 137.0 * (turn - 1) if turn else 11.0
            share = 1 / len(groups)
            worker = chain(env, turn, cut * step, width // len(groups), peers)
            next(worker)
            wide = 12.8 * share
            times = [clock, clock + 3 + 8 * share + wide]
            for stage in range(1, bits):
                times.append(times[-1] + 3 + (wide / 2 if stage == 1 else wide))
            if turn > 0:
                wide *= 2
                times.append(times[-1] + 7)
            for stage in range(bits):
                times.append(times[-1] + 3 + (wide / 2 if stage == 1 else wide))
            if tuned and turn > 0 and cut == cuts - 1:
                times = [70.0, 70.5, 72.0, 79.0, 86.0, 100.0, 120.0, 130.0]
            elif tuned and turn == 0:
                times[-1] = 104.2
            elif tuned:
                times[-1] = 120.2
            tasks += [(time, worker.send) for time in times]
            late.append(times)
    for turn in range(1, rounds):
        begin = 0.0 if tuned else 74.0 + 137.0 * (turn - 1)
        plain = ((0.0, 20.0), (17.0, 37.0), (34.0, 56.0), (51.0, 75.0))
        ordered = ((69.9, 71.2), (87.0, 119.7), (104.5, 129.0), (120.5, 136.5))
        for piece, (send, there) in enumerate(ordered if tuned else plain):
            tasks += [(begin + send, send_piece(turn, piece)), (begin + there, gate_piece(turn, piece))]
    for turn in range(rounds):
        steps = [make_tilde(turn), add_terms(turn, True), add_terms(turn, False)]
        if turn == 0 and rounds > 1:
            times = [119.5, 121.0, 122.0] if tuned else [time + 1 for time in late[cuts][-4:-1]]
            tasks += list(zip(times, steps))
        else:
            tasks += [(late[-1][-1] + 6 + index, step_) for index, step_ in enumerate(steps)]
    tasks.sort(key=lambda task: task[0])
    for _, task in tasks[:-1]:
        token = task(token)
    density = sum(densities)
    for bit in reversed(range(lax.axis_size("pair").bit_length() - 1)):
        half = density.shape[1] // 2
        side = position >> bit & 1
        give = lax.dynamic_slice_in_dim(density, (1 - side) * half, half, 1)
        came = swapped(give, "pair", bit)
        if tasks:
            came = passed(came, token)
            token = tasks.pop()[1](token)
            tasks = []
        density = lax.dynamic_slice_in_dim(density, side * half, half, 1) + came
    return (gradient, density)


def solution(mesh):
    in_specs = (P("pair", None, "aux"), P("pair"), P(), P(None, "pair"))
    out_specs = (P("pair", None, "aux"), P("aux", "pair"))
    return jax.shard_map(body, mesh=mesh, in_specs=in_specs, out_specs=out_specs, check_vma=False)
```

```python
import functools

import jax
import jax.numpy as jnp
from jax import lax
from jax.experimental import pallas as pl
from jax.experimental.pallas import tpu as pltpu
from jax.sharding import PartitionSpec as P

VMEM = pl.BlockSpec(memory_space=pltpu.VMEM)
SMEM = pl.BlockSpec(memory_space=pltpu.SMEM)
ANY = pl.BlockSpec(memory_space=pl.ANY)


def params(mebibytes):
    return pltpu.CompilerParams(vmem_limit_bytes=mebibytes * 2**20)


def cost():
    return pl.CostEstimate(flops=1, bytes_accessed=1, transcendentals=0)


def swapped(block, axis, bit):
    count = lax.axis_size(axis)
    route = []
    for low in range(count):
        high = low | 1 << bit
        if high != low and high < count:
            route += [(low, high), (high, low)]
    return lax.ppermute(block, axis, route)


def orders(bits):
    return (list(range(bits)), [1, 0] + list(range(2, bits)))


def across(block, step):
    pairs, auxes = lax.axis_size("pair"), lax.axis_size("aux")
    order = orders(auxes.bit_length() - 1)
    route = []
    for p in range(pairs):
        for m in range(auxes):
            route.append((p * auxes + m, p * auxes + (m ^ 1 << order[p % 2][step])))
    return lax.ppermute(block, ("pair", "aux"), route)


def halves(value):
    high = value.astype(jnp.bfloat16)
    return high, (value - high.astype(jnp.float32)).astype(jnp.bfloat16)


def multiply(left, right, dims):
    rh, rl = right
    one = functools.partial(
        lax.dot_general, dimension_numbers=(dims, ((), ())), preferred_element_type=jnp.float32
    )
    count = left.shape[0] // 2
    both = one(left, rh)
    return both[:count] + (both[count:] + one(left[:count], rl))


def stacked(value):
    return jnp.concatenate(halves(value), axis=0)


def upper_in(position, turn):
    return position // 2**turn % 2 == 1


def slot_of(plan_ref, state_ref, per_block, turn, h, own):
    half_count = per_block // 2
    plain = jnp.where(own, h, half_count + h)
    wanted = jnp.where(own, half_count + h, h)
    inverse = 0
    for k in range(per_block):
        inverse += jnp.where(plan_ref[turn, k] == wanted, k, 0)
    return jnp.where(upper_in(state_ref[0], turn), inverse, plain)


def peer_slot_of(plan_ref, state_ref, per_block, turn, h, own):
    half_count = per_block // 2
    plain = jnp.where(own, h, half_count + h)
    wanted = jnp.where(own, half_count + h, h)
    paired = 0
    for k in range(per_block):
        paired += jnp.where(plain == k, plan_ref[turn, k], 0)
    return jnp.where(upper_in(state_ref[0], turn), wanted, paired)


def copy_kernel(extra, plan_ref, state_ref, source_ref, *refs):
    del plan_ref, state_ref
    rows = source_ref.shape[1]
    refs[-1][:, :rows] = source_ref[...]
    if extra:
        refs[-1][:, rows:] = refs[0][...][None]


def picked(three_index, plan, state, token, turn, own, part, parts, extra=None):
    per_block, width, depth = three_index.shape
    half_count = per_block // 2
    rows = width if own else width // parts
    depth = depth // parts if own else depth
    count = rows + (0 if extra is None else extra.shape[0])

    def source(h, plan_ref, state_ref):
        slot = slot_of(plan_ref, state_ref, per_block, turn, h, own)
        return (slot, 0, part) if own else (slot, part, 0)

    return pl.pallas_call(
        functools.partial(copy_kernel, extra is not None),
        out_shape=jax.ShapeDtypeStruct((half_count, count, depth), jnp.float32),
        grid_spec=pltpu.PrefetchScalarGridSpec(
            num_scalar_prefetch=2,
            grid=(half_count,),
            in_specs=[pl.BlockSpec((1, rows, depth), source)]
            + ([] if extra is None else [VMEM])
            + [ANY],
            out_specs=pl.BlockSpec((1, count, depth), lambda h, *_: (h, 0, 0)),
        ),
        compiler_params=params(24),
        cost_estimate=cost(),
    )(plan, state, three_index, *(() if extra is None else (extra,)), token)


def gate_kernel(*refs):
    refs[-1][...] = jnp.zeros_like(refs[-1])


def gated(*tokens):
    return pl.pallas_call(
        gate_kernel,
        out_shape=jax.ShapeDtypeStruct((8, 128), jnp.float32),
        in_specs=[ANY] * len(tokens),
        out_specs=VMEM,
        compiler_params=params(16),
        cost_estimate=cost(),
    )(*tokens)


def pass_kernel(value_ref, token_ref, out_ref):
    del token_ref
    out_ref[...] = value_ref[...]


def passed(value, token):
    return pl.pallas_call(
        pass_kernel,
        out_shape=jax.ShapeDtypeStruct(value.shape, value.dtype),
        in_specs=[VMEM, ANY],
        out_specs=VMEM,
        compiler_params=params(16),
        cost_estimate=cost(),
    )(value, token)


def integral_kernel(turn, blocks, plan_ref, state_ref, own_ref, token_ref, *refs):
    del plan_ref, token_ref
    keep_ref, give_ref, high, low = refs[-4:]
    band = pl.program_id(1)
    count = high.shape[0] // (len(refs) - 4)

    @pl.when(band == 0)
    def _():
        for index, peer_ref in enumerate(refs[:-4]):
            spot = slice(index * count, (index + 1) * count)
            high[spot, :], low[spot, :] = halves(peer_ref[0, :count])

    value = multiply(stacked(own_ref[0]), (high[...], low[...]), ((1,), (1,)))
    rows = keep_ref.shape[1] * 2 // blocks
    inside = own_ref.shape[1] // rows
    for part in range(inside):
        place = (band * inside + part) ^ state_ref[1]
        piece = value[part * rows : (part + 1) * rows]

        @pl.when(place < blocks // 2)
        def _():
            keep_ref[0, pl.ds(pl.multiple_of(place * rows, rows), rows), :] = piece

        @pl.when(place >= blocks // 2)
        def _():
            spot = (place - blocks // 2) * rows
            give_ref[0, pl.ds(pl.multiple_of(spot, rows), rows), :] = piece


def integral(three_index, peers, plan, state, token, turn, blocks, count):
    per_block, width, depth = three_index.shape
    half_count = per_block // 2
    bands = 2
    out = jax.ShapeDtypeStruct((half_count, width // 2, count), jnp.float32)
    whole = pl.BlockSpec((1, width // 2, count), lambda h, band, *_: (h, 0, 0))
    chosen = peers[0].shape[0] == per_block

    def peer_at(h, band, p, s):
        return (peer_slot_of(p, s, per_block, turn, h, True) if chosen else h, 0, 0)

    return pl.pallas_call(
        functools.partial(integral_kernel, turn, blocks),
        out_shape=(out, out),
        grid_spec=pltpu.PrefetchScalarGridSpec(
            num_scalar_prefetch=2,
            grid=(half_count, bands),
            in_specs=[
                pl.BlockSpec(
                    (1, width // bands, depth),
                    lambda h, band, p, s: (slot_of(p, s, per_block, turn, h, True), band, 0),
                ),
                ANY,
            ]
            + [pl.BlockSpec((1, peer.shape[1], depth), peer_at) for peer in peers],
            out_specs=(whole, whole),
            scratch_shapes=[pltpu.VMEM((count, depth), jnp.bfloat16)] * 2,
        ),
        compiler_params=params(44),
        cost_estimate=cost(),
    )(plan, state, three_index, token, *peers)


def add_kernel(keep_ref, came_ref, token_ref, low_ref, high_ref):
    del token_ref
    half = low_ref.shape[1]
    low_ref[...] = keep_ref[:, :half] + came_ref[:, :half]
    high_ref[...] = keep_ref[:, half:] + came_ref[:, half:]


def parted(keep, came, token):
    out = jax.ShapeDtypeStruct((keep.shape[0], keep.shape[1] // 2, keep.shape[2]), jnp.float32)
    return pl.pallas_call(
        add_kernel,
        out_shape=(out, out),
        in_specs=[VMEM, VMEM, ANY],
        out_specs=(VMEM, VMEM),
        compiler_params=params(16),
        cost_estimate=cost(),
    )(keep, came, token)


def join_kernel(axis, one_ref, two_ref, token_ref, out_ref):
    del token_ref
    half = one_ref.shape[axis]
    if axis == 0:
        out_ref[:half], out_ref[half:] = one_ref[...], two_ref[...]
    else:
        out_ref[:, :half], out_ref[:, half:] = one_ref[...], two_ref[...]


def joined(one, two, token, axis):
    shape = list(one.shape)
    shape[axis] *= 2
    return pl.pallas_call(
        functools.partial(join_kernel, axis),
        out_shape=jax.ShapeDtypeStruct(tuple(shape), jnp.float32),
        in_specs=[VMEM, VMEM, ANY],
        out_specs=VMEM,
        compiler_params=params(24),
        cost_estimate=cost(),
    )(one, two, token)


def amplitude_kernel(turn, per_block, ours_ref, theirs_ref, state_ref, column_ref, row_ref, left_ref, right_ref, token_ref, out_ref):
    del token_ref
    half_count = per_block // 2
    rows = out_ref.shape[1]
    down = column_ref[pl.ds(pl.multiple_of(state_ref[1] * rows, rows), rows), :]
    theirs = theirs_ref[...].reshape(theirs_ref.shape[-2:])
    upper = upper_in(state_ref[0], turn)
    for h in range(half_count):
        low = ours_ref[0, h] + jnp.zeros((1, 1), jnp.float32)
        high = theirs[0:1, half_count + h : half_count + h + 1]
        wanted = ours_ref[0, per_block * (turn + 1) + h]
        for k in range(per_block):
            slot = ours_ref[0, per_block * (turn + 1) + k]
            high = high + jnp.where(slot == half_count + h, ours_ref[0, k], 0.0)
            low = low + jnp.where(wanted == k, 1.0, 0.0) * theirs[0:1, k : k + 1]
        gap = jnp.where(upper, high, low) - down - row_ref[...]
        out_ref[h] = (left_ref[h] + right_ref[h]) / gap


def amplitude(ours, theirs, theirs_spec, state, column, row, left, right, token, turn, per_block):
    return pl.pallas_call(
        functools.partial(amplitude_kernel, turn, per_block),
        out_shape=jax.ShapeDtypeStruct(left.shape, jnp.float32),
        grid=(1,),
        in_specs=[SMEM, theirs_spec, SMEM, VMEM, VMEM, VMEM, VMEM, ANY],
        out_specs=VMEM,
        compiler_params=params(16),
        cost_estimate=cost(),
    )(ours, theirs, state, column, row, left, right, token)


def tilde_kernel(blocks, places, state_ref, token_ref, *refs):
    del token_ref
    count = len(places)
    sources, (tall_ref, density_ref, amp, tilde) = refs[: 2 * count], refs[2 * count :]
    width = amp.shape[0]
    rows = width // blocks
    share = density_ref.shape[0]
    band = 128 if width % 128 == 0 else width
    for h in range(tall_ref.shape[1]):
        for who in range(2):
            offset = 0
            for part in range(count):
                first, order = places[part][who]
                source = sources[2 * part + who]
                size = source.shape[2]
                for place in range(blocks):
                    spot = pl.ds(pl.multiple_of((place ^ state_ref[order]) * rows, rows), rows)
                    amp[spot, offset : offset + size] = source[first + h, place * rows : (place + 1) * rows, :]
                offset += size
            for part in range(width // band):
                spot = slice(part * band, (part + 1) * band)
                straight, turned = amp[spot, :], amp[:, spot].T
                value = 2.0 * straight - turned if who == 0 else 2.0 * turned - straight
                if who == 0:
                    tilde[spot, :] = value
                below = slice(width + part * band, width + (part + 1) * band)
                tall_ref[who, h, spot, :], tall_ref[who, h, below, :] = halves(value)
            if who == 0:
                start = pl.ds(pl.multiple_of(state_ref[3] * share, share), share)
                straight = amp[start, :]
                turned = 2.0 * straight - tilde[start, :]
                both = (tall_ref[0, h, :width], tall_ref[0, h, width:])
                value = multiply(stacked(straight), both, ((1,), (1,)))
                value += multiply(stacked(turned), both, ((1,), (0,)))
                if h == 0:
                    density_ref[...] = value
                else:
                    density_ref[...] += value


def tildes(state, token, gathered, blocks, share, half_count):
    sources = [array for own, peer, _ in gathered for array in (own, peer)]
    places = [spots for _, _, spots in gathered]
    width = sources[0].shape[1]
    return pl.pallas_call(
        functools.partial(tilde_kernel, blocks, places),
        out_shape=(
            jax.ShapeDtypeStruct((2, half_count, 2 * width, width), jnp.bfloat16),
            jax.ShapeDtypeStruct((share, width), jnp.float32),
        ),
        in_specs=[SMEM, ANY] + [VMEM] * len(sources),
        out_specs=(VMEM, VMEM),
        scratch_shapes=[pltpu.VMEM((width, width), jnp.float32)] * 2,
        compiler_params=params(48),
        cost_estimate=cost(),
    )(state, token, *sources)


def gradient_kernel(count, based, columns, plan_ref, state_ref, tall_ref, token_ref, *refs):
    del plan_ref, state_ref, token_ref
    out_ref, done_ref = refs[-2:]
    done_ref[...] = jnp.zeros_like(done_ref)

    def term(offset, source):
        size = min(source.shape[1], tall_ref.shape[3] // (1 if columns else count))
        tilde = tall_ref[0, 0, :, offset : offset + size]
        return multiply(tilde, halves(source[0, :size]), ((1,), (0,)))

    if columns:
        for piece, source in enumerate(refs[:count]):

            @pl.when(pl.program_id(2) == piece)
            def _():
                out_ref[0] = refs[count][0] + term(0, source)

        return
    value = refs[count][0] if based else None
    for index, source in enumerate(refs[:count]):
        added = term(index * (tall_ref.shape[3] // count), source)
        value = added if value is None else value + added
    out_ref[0] = value


def gradient_terms(plan, state, token, tall, sources, base, turn, own, three_index):
    per_block, width, depth = three_index.shape
    half_count = per_block // 2
    columns = sources[0].shape[2] < depth
    tile = sources[0].shape[2] if columns else depth // 4 if depth % 512 == 0 else depth
    chosen = sources[0].shape[0] == per_block
    at = 0 if own else 1

    def block_at(h, _, piece, p, s):
        return (slot_of(p, s, per_block, turn, h, own), 0, piece)

    def source_at(h, _, piece, p, s):
        slot = peer_slot_of(p, s, per_block, turn, h, own) if chosen else h
        return (slot, 0, 0 if columns else piece)

    tilde_spec = pl.BlockSpec((1, 1, 2 * width, width), lambda h, *_: (at, h, 0, 0))
    out_spec = pl.BlockSpec((1, width, tile), block_at)
    return pl.pallas_call(
        functools.partial(gradient_kernel, len(sources), turn > 0, columns),
        out_shape=(
            jax.ShapeDtypeStruct((per_block, width, depth), jnp.float32),
            jax.ShapeDtypeStruct((8, 128), jnp.float32),
        ),
        grid_spec=pltpu.PrefetchScalarGridSpec(
            num_scalar_prefetch=2,
            grid=(half_count, 1, depth // tile),
            in_specs=[tilde_spec, ANY]
            + [pl.BlockSpec((1, x.shape[1], tile), source_at) for x in sources]
            + ([] if base is None else [out_spec] if turn > 0 else [ANY]),
            out_specs=(out_spec, pl.BlockSpec((8, 128), lambda *_: (0, 0))),
        ),
        input_output_aliases={} if base is None else {4 + len(sources): 0},
        compiler_params=params(44),
        cost_estimate=cost(),
    )(plan, state, tall, token, *sources, *(() if base is None else (base,)))


def chain(env, turn, offset, size, peers):
    bits, per_block, state = env["bits"], env["per_block"], env["state"]
    half_count = per_block // 2
    count = size // len(peers)
    token = yield None
    keep, give = integral(
        env["three_index"], peers, env["plan"], state, token, turn, env["blocks"], count
    )
    for stage in range(bits - 1):
        came = across(give, stage)
        token = yield give
        keep, give = parted(keep, came, token)
    came = across(give, bits - 1)
    token = yield give
    row = env["virtual"][None, offset : offset + size]
    theirs, spec = env["theirs"][turn]
    value = amplitude(
        env["ours"], theirs, spec, state, env["column"], row, keep, came, token, turn, per_block
    )
    if turn > 0:
        came = swapped(value, "pair", turn)
        token = yield value
        value = joined(value, came, token, 0)
    for stage in reversed(range(bits)):
        came = across(value, stage)
        token = yield value
        value = joined(value, came, token, 1)
    if turn == 0:
        came = swapped(value, "pair", 0)
        env["gathered"][turn].append((value, came, ((0, 1), (0, 2))))
    else:
        env["gathered"][turn].append((value, value, ((0, 1), (half_count, 1))))
    yield value


def body(three_index, occupied_energy, virtual_energy, plan):
    per_block, width, depth = three_index.shape
    half_count = per_block // 2
    aux_count = lax.axis_size("aux")
    bits = aux_count.bit_length() - 1
    blocks = aux_count
    row_count = width // aux_count
    aux = lax.axis_index("aux").astype(jnp.int32)
    rounds = plan.shape[0]
    position = lax.axis_index("pair").astype(jnp.int32)

    def mask(order):
        return sum((aux >> bit & 1) << bits - 1 - step for step, bit in enumerate(order))

    first_mask, second_mask = (mask(order) for order in orders(bits))
    core = position % 2
    state = jnp.stack(
        [
            position,
            jnp.where(core == 0, first_mask, second_mask),
            jnp.where(core == 0, second_mask, first_mask),
            aux,
        ]
    ).astype(jnp.int32)

    mine = jnp.concatenate([occupied_energy, plan.astype(jnp.float32).reshape(-1)])[None]
    extra = jnp.pad(mine, ((0, 7), (0, depth - mine.shape[1])))
    cuts, pieces = 2, 4
    step = width // cuts
    firsts = [None] * rounds
    theirs = [(swapped(mine, "pair", 0), VMEM)]
    token = virtual_energy
    for turn in range(1, rounds):
        firsts[turn] = []
        for cut in range(cuts):
            token = picked(
                three_index, plan, state, token, turn, False, cut, cuts, None if cut else extra
            )
            firsts[turn].append(swapped(token, "pair", turn))
        theirs.append((firsts[turn][0], pl.BlockSpec((1, 8, depth), lambda _: (0, step // 8, 0))))
    other = swapped(three_index, "pair", 0)
    firsts[0] = [other]
    env = {
        "bits": bits,
        "per_block": per_block,
        "blocks": blocks,
        "plan": plan,
        "state": state,
        "three_index": three_index,
        "virtual": virtual_energy,
        "column": virtual_energy[:, None],
        "ours": mine,
        "theirs": theirs,
        "gathered": [[] for _ in range(rounds)],
    }
    seconds = [[other]] + [[] for _ in range(1, rounds)]
    gradient = None
    tilde = [None] * rounds
    densities = []

    def gate_piece(turn, piece):
        return lambda token: gated(token, seconds[turn][piece])

    def send_piece(turn, piece):
        def run(token):
            token = picked(three_index, plan, state, token, turn, True, piece, pieces)
            seconds[turn].append(swapped(token, "pair", turn))
            return token

        return run

    def make_tilde(turn):
        def run(token):
            tilde[turn], density = tildes(
                state, token, env["gathered"][turn], blocks, row_count, half_count
            )
            densities.append(density)
            return density

        return run

    def add_terms(turn, own):
        def run(token):
            nonlocal gradient
            sources = firsts[turn] if own else seconds[turn]
            gradient, token = gradient_terms(
                plan, state, token, tilde[turn], sources, gradient, turn, own, three_index
            )
            return token

        return run

    tasks = []
    late = []
    tuned = bits == 3 and rounds == 2 and cuts == 2
    for turn in range(rounds):
        groups = [[first] for first in firsts[turn]]
        for cut, peers in enumerate(groups):
            clock = 42.0 + 36.0 * cut + 137.0 * (turn - 1) if turn else 11.0
            share = 1 / len(groups)
            worker = chain(env, turn, cut * step, width // len(groups), peers)
            next(worker)
            wide = 12.8 * share
            times = [clock, clock + 3 + 8 * share + wide]
            for stage in range(1, bits):
                times.append(times[-1] + 3 + (wide / 2 if stage == 1 else wide))
            if turn > 0:
                wide *= 2
                times.append(times[-1] + 7)
            for stage in range(bits):
                times.append(times[-1] + 3 + (wide / 2 if stage == 1 else wide))
            if tuned and turn > 0 and cut == cuts - 1:
                times = [70.0, 80.0, 84.0, 95.0, 101.5, 104.0, 120.0, 130.0]
            elif tuned and turn == 0:
                times[-1] = 104.2
            elif tuned:
                times[-1] = 120.2
            tasks += [(time, worker.send) for time in times]
            late.append(times)
    for turn in range(1, rounds):
        begin = 0.0 if tuned else 74.0 + 137.0 * (turn - 1)
        plain = ((0.0, 20.0), (17.0, 37.0), (34.0, 56.0), (51.0, 75.0))
        ordered = ((79.0, 101.1), (102.0, 119.7), (104.5, 129.0), (120.5, 136.5))
        for piece, (send, there) in enumerate(ordered if tuned else plain):
            tasks += [(begin + send, send_piece(turn, piece)), (begin + there, gate_piece(turn, piece))]
    for turn in range(rounds):
        steps = [make_tilde(turn), add_terms(turn, True), add_terms(turn, False)]
        if turn == 0 and rounds > 1:
            times = [119.5, 119.6, 122.0] if tuned else [time + 1 for time in late[cuts][-4:-1]]
            tasks += list(zip(times, steps))
        else:
            tasks += [(late[-1][-1] + 6 + index, step_) for index, step_ in enumerate(steps)]
    tasks.sort(key=lambda task: task[0])
    for _, task in tasks[:-1]:
        token = task(token)
    density = sum(densities)
    for bit in reversed(range(lax.axis_size("pair").bit_length() - 1)):
        half = density.shape[1] // 2
        side = position >> bit & 1
        give = lax.dynamic_slice_in_dim(density, (1 - side) * half, half, 1)
        came = swapped(give, "pair", bit)
        if tasks:
            came = passed(came, token)
            token = tasks.pop()[1](token)
            tasks = []
        density = lax.dynamic_slice_in_dim(density, side * half, half, 1) + came
    return (gradient, density)


def solution(mesh):
    in_specs = (P("pair", None, "aux"), P("pair"), P(), P(None, "pair"))
    out_specs = (P("pair", None, "aux"), P("aux", "pair"))
    return jax.shard_map(body, mesh=mesh, in_specs=in_specs, out_specs=out_specs, check_vma=False)
```
